32 devices in a mesh: slab: 8 (over z, x), depth: 4 (over y, core).
Axes of the slice: x: 2, y: 2, z: 4, core: 2. Of those that a mesh axis runs over, the one named last changes fastest.
Arguments:
- nutrient: float32 [64, 128, 512], P('slab', 'depth'), may hold values from 0.5 to 2
- species: bfloat16 [32768, 128], P(('slab', 'depth')), may hold values from -6 to 6
- agent_cell: int32 [32768], P(('slab', 'depth')), may hold values from 0 to 131071
- death_flag: int32 [32768], P(('slab', 'depth')), may hold values 0 or 1
- divide_flag: int32 [32768], P(('slab', 'depth')), may hold values 0 or 1
- slab_move: int32 [32768], P(('slab', 'depth')), may hold values from 0 to 2, as said below
- depth_route: int32 [32768, 1], P(('slab', 'depth')), may hold values from 0 to 3; in each aligned block of 1024 rows (0 to 1023, 1024 to 2047, ...) at most 512 rows name the same one
- net_weight: bfloat16 [128, 128], replicated, may hold values from -0.5 to 0.5
- sensing: float32 [128], replicated, may hold values from -1 to 1
- uptake_weight: bfloat16 [128], replicated, may hold values from -0.5 to 0.5
Outputs:
- nutrient_next: float32 [64, 128, 512], P('slab', 'depth')
- species_after_step: bfloat16 [73728, 128], P(('slab', 'depth'))
The draws below stay inside these ranges and needn't reach their ends.
Inputs may be any that keep to these rules, and one draw needn't show every extreme that they name: `slab_move`: within each device's 1024 rows at most 128 carry 1 and at most 128 carry 2; some device has exactly 128 carrying 1 and some device exactly 128 carrying 2. `depth_route`: within each device's 1024 rows no depth index is named more than 512 times; one is named exactly 512 times in some device.
All inputs are finite; a program needn't handle non-finite values. No bound on the sum of `death_flag` or of `divide_flag` on one device may be relied on, other than what follows from the above.
Results may differ from the reference program's by a relative error of at most 0.0045.
Values may be sent and summed in bfloat16 or wider, within the bound.
No kernel may reach another device: no remote copies, remote signals or barrier semaphores. Data moves between devices by JAX's collectives and lax.ppermute only.
A program may use at most 128 MiB of HBM per device.

```python
import math
import jax
import jax.numpy as jnp
import numpy as np
from jax import lax

SPECIES_COUNT = 128
CX = 8
CY = 32
CZ = 512
A_DEV = 1024
PRE = 2
COARSE = 4
MIG = 128
DEPTHS = 4
SLOT_CAPACITY = 512
NX = 64
NY = 128
NZ = 512
CELLS_DEV = 131072
AGENTS = 32768
N_SLAB = 8
N_DEPTH = 4


def draw_slab_move(key, part):
    block_count = AGENTS // A_DEV
    first_key, second_key, third_key = jax.random.split(key, 3)
    up_counts = jax.random.randint(first_key, (block_count,), MIG // 4, MIG + 1).at[0].set(MIG)
    down_counts = jax.random.randint(second_key, (block_count,), MIG // 4, MIG + 1).at[block_count - 1].set(MIG)
    block_keys = jax.random.split(third_key, block_count)

    def shuffle(block_key):
        return jax.random.permutation(block_key, A_DEV)
    ranks = jax.vmap(shuffle)(block_keys)
    move_code = jnp.where(ranks < up_counts[:, None], 1, jnp.where(ranks < (up_counts + down_counts)[:, None], 2, 0))
    return move_code.reshape(-1).astype(jnp.int32)


def place_ends(drawn, key, low, top_value):
    spot = [jax.random.randint(jax.random.fold_in(key, axis), (), 0, length) for axis, length in enumerate(drawn.shape)]
    main_axis = drawn.shape.index(max(drawn.shape))
    neighbour = spot[:main_axis] + [(spot[main_axis] + 1) % drawn.shape[main_axis]] + spot[main_axis + 1:]
    return drawn.at[tuple(spot)].set(low).at[tuple(neighbour)].set(top_value)


def steps_of(key, dims, shards, least, top_value):
    loudness = 1.0
    for position, blocks in shards:
        steps = jax.random.uniform(jax.random.fold_in(jax.random.fold_in(key, 6), position), (blocks,), jnp.float32, least / len(shards), top_value / len(shards))
        loudness = loudness * jnp.repeat(jnp.exp(steps), dims[position] // blocks).reshape((-1,) + (1,) * (len(dims) - 1 - position))
    return loudness


def routed_block(rng, own, number, rows, amount, top, limit, skew):
    order = jax.random.permutation(rng, amount)
    packed, usual = portions_of(amount, rows * top, limit, skew, True), portions_of(amount, rows * top, limit, skew, False)
    places = jnp.arange(amount)

    def named(sizes, offset_by):
        used = int((sizes > 0).sum())
        fixed = max(1, used // 4)
        shifted = fixed + (places - fixed + offset_by * (used - fixed)) % max(1, amount - fixed)
        return jnp.zeros((amount,), jnp.int32).at[order[jnp.where(places < fixed, places, shifted)]].set(jnp.asarray(sizes, jnp.int32))

    sizes = jnp.where(number % 4 == 0, named(packed, number // 4), named(usual, number - number // 4 - 1))
    mixed = jax.random.permutation(jax.random.fold_in(own, 3), amount)
    donor, taker = mixed[0:amount // 2 * 2:2], mixed[1:amount // 2 * 2:2]
    room = jnp.minimum(sizes[donor] - 1, limit - sizes[taker]) // 2
    room = jnp.where((donor == order[0]) | (taker == order[0]) | (sizes[taker] == 0), 0, jnp.maximum(room, 0))
    shifted = jax.random.randint(jax.random.fold_in(own, 4), (amount // 2,), 0, 1 << 20) % (room + 1)
    sizes = sizes.at[donor].add(-shifted).at[taker].add(shifted)
    labels = jnp.searchsorted(jnp.cumsum(sizes), jnp.arange(rows * top), side="right").astype(jnp.int32)
    table = labels.reshape(top, rows).T
    table = table[jax.random.permutation(jax.random.fold_in(own, 1), rows)]
    offset_by = jax.random.randint(jax.random.fold_in(own, 2), (rows, 1), 0, top)
    return jnp.take_along_axis(table, (jnp.arange(top)[None, :] + offset_by) % top, axis=1)


def portions_of(count, total, reach, skew, full):
    weights = [(1 << 20) // math.isqrt(standing ** skew) + 1 for standing in range(1, count + 1)]
    largest = reach if full else min(reach, max(-(-total // count), total * weights[0] // sum(weights)))
    least = 1 if total - largest >= count - 1 else 0
    given, surplus = [largest] + [least] * (count - 1), total - largest - least * (count - 1)
    while surplus > 0:
        movable = [i for i in range(1, count) if given[i] < largest] or [i for i in range(1, count) if given[i] < reach]
        mass, remaining = sum([weights[i] for i in movable]), surplus
        for i in movable:
            more = min(reach - given[i], max(1, remaining * weights[i] // mass), surplus)
            given[i] = given[i] + more
            surplus = surplus - more
    return np.array(given)


def scatter_about(key, dims, scale, most, pieces=(), held_as=jnp.bfloat16):
    drawn = scale * jax.random.normal(key, dims, jnp.float32)
    if pieces:
        drawn = drawn * steps_of(key, dims, pieces, -0.22, 0.18)
    return jnp.clip(drawn, -most, most).astype(held_as)


def setup_inputs(seed: int = 0) -> dict:
    key_of = jax.random.split(jax.random.key(seed), 11)
    nutrient = jnp.clip(0.5 + 1.5 * jax.random.uniform(key_of[0], (NX, NY, NZ), jnp.float32) ** steps_of(key_of[0], (NX, NY, NZ), ((0, 8), (1, 4)), -0.2, 0.2), 0.5, 2.0)
    species = scatter_about(key_of[1], (AGENTS, SPECIES_COUNT), 1.0, 6.0, ((0, 32),))
    agent_cell = place_ends(jax.random.randint(key_of[2], (AGENTS,), 0, CELLS_DEV), jax.random.fold_in(key_of[2], 1), 0, CELLS_DEV - 1).astype(jnp.int32)
    death_flag = place_ends((jax.random.randint(key_of[3], (AGENTS,), 0, 8) < 1).astype(jnp.int32), jax.random.fold_in(key_of[3], 1), 0, 1)
    divide_flag = place_ends((jax.random.randint(key_of[4], (AGENTS,), 0, 4) < 1).astype(jnp.int32), jax.random.fold_in(key_of[4], 1), 0, 1)
    slab_move = draw_slab_move(jax.random.fold_in(key_of[10], 71), 0)
    depth_route_keys = jax.random.split(jax.random.fold_in(key_of[6], 1), AGENTS // A_DEV)
    depth_route_turns = jax.random.permutation(jax.random.fold_in(key_of[6], 3), AGENTS // A_DEV)
    depth_route = jax.vmap(lambda own, number: routed_block(jax.random.fold_in(key_of[6], 2), own, number, A_DEV, DEPTHS, 1, SLOT_CAPACITY, 2))(depth_route_keys, depth_route_turns).reshape((AGENTS, 1))
    net_weight = scatter_about(key_of[7], (SPECIES_COUNT, SPECIES_COUNT), SPECIES_COUNT ** -0.5, 0.5)
    sensing = jnp.clip(jax.random.uniform(key_of[8], (SPECIES_COUNT,), jnp.float32, -1.0, 1.0), -1.0, 1.0)
    uptake_weight = scatter_about(key_of[9], (SPECIES_COUNT,), SPECIES_COUNT ** -0.5, 0.5)
    return dict(nutrient=nutrient, species=species, agent_cell=agent_cell, death_flag=death_flag, divide_flag=divide_flag, slab_move=slab_move, depth_route=depth_route, net_weight=net_weight, sensing=sensing, uptake_weight=uptake_weight)


SCREENING = 0.05
DAMPING = 2.0 / 3.0


def neighbour_sum(grid_field):
    along_first = jnp.roll(grid_field, 1, 0) + jnp.roll(grid_field, -1, 0)
    padded = jnp.pad(grid_field, ((0, 0), (1, 1), (1, 1)))
    along_second = padded[:, 2:, 1:-1] + padded[:, :-2, 1:-1]
    along_third = padded[:, 1:-1, 2:] + padded[:, 1:-1, :-2]
    return along_first + along_second + along_third


def relax_step(grid_field, target, centre):
    image_field = centre * grid_field - neighbour_sum(grid_field)
    return grid_field + DAMPING * (target - image_field) / centre


def reference(nutrient, species, agent_cell, death_flag, divide_flag, slab_move, depth_route, net_weight, sensing, uptake_weight):
    agent_rows = jnp.arange(AGENTS, dtype=jnp.int32)
    block_index = agent_rows // A_DEV
    slab_position_index = block_index // N_DEPTH
    depth_position_index = block_index % N_DEPTH
    cell_first = slab_position_index * CX + agent_cell // (CY * CZ)
    cell_second = depth_position_index * CY + (agent_cell // CZ) % CY
    cell_third = agent_cell % CZ
    sample = nutrient[cell_first, cell_second, cell_third]
    alive_mask = (1 - death_flag).astype(jnp.float32)
    uptake_score = jnp.dot(species, uptake_weight, preferred_element_type=jnp.float32)
    uptake = alive_mask * (1.0 + divide_flag.astype(jnp.float32)) * jax.nn.softplus(uptake_score) * sample / (0.5 + sample)
    source = jnp.zeros_like(nutrient).at[cell_first, cell_second, cell_third].add(uptake)
    target = SCREENING * nutrient - source
    centre = 6.0 + SCREENING
    grid_field = nutrient
    for sweep_step in range(PRE):
        grid_field = relax_step(grid_field, target, centre)
    residual = target - (centre * grid_field - neighbour_sum(grid_field))
    coarse_target = 4.0 * residual.reshape(NX // 2, 2, NY // 2, 2, NZ // 2, 2).mean(axis=(1, 3, 5))
    coarse = jnp.zeros_like(coarse_target)
    for sweep_step in range(COARSE):
        coarse = relax_step(coarse, coarse_target, 6.0 + 4.0 * SCREENING)
    grid_field = grid_field + jnp.repeat(jnp.repeat(jnp.repeat(coarse, 2, 0), 2, 1), 2, 2)
    for sweep_step in range(PRE):
        grid_field = relax_step(grid_field, target, centre)

    sensed = lax.optimization_barrier(sample.astype(jnp.bfloat16)).astype(jnp.float32)
    activation = jnp.dot(species, net_weight, preferred_element_type=jnp.float32) + sensed[:, None] * sensing[None, :]
    updated = (alive_mask[:, None] * (0.5 * species.astype(jnp.float32) + jnp.tanh(activation))).astype(jnp.bfloat16)

    target_device = depth_route[:, 0]
    dest_hits = (target_device[:, None] == jnp.arange(N_DEPTH, dtype=jnp.int32)[None, :]).astype(jnp.int32).reshape(-1, A_DEV, N_DEPTH)
    earlier = jnp.cumsum(dest_hits, axis=1) - dest_hits
    destination_slot = jnp.sum(earlier * dest_hits, axis=2).reshape(-1)
    remaining_agents = jnp.where((slab_move == 0)[:, None], updated, jnp.zeros_like(updated))
    balanced_slots = jnp.zeros((N_SLAB, N_DEPTH, N_DEPTH, SLOT_CAPACITY, SPECIES_COUNT), jnp.bfloat16).at[slab_position_index, target_device, depth_position_index, destination_slot].set(remaining_agents)

    def pack_movers(move_code, shift_by):
        chosen = (slab_move == move_code).astype(jnp.int32).reshape(-1, A_DEV)
        rank_order = (jnp.cumsum(chosen, axis=1) - chosen).reshape(-1)
        target_slot = jnp.where(chosen.reshape(-1) == 1, rank_order, MIG)
        buffer = jnp.zeros((N_SLAB, N_DEPTH, MIG, SPECIES_COUNT), jnp.bfloat16)
        return buffer.at[(slab_position_index + shift_by) % N_SLAB, depth_position_index, target_slot].set(updated, mode="drop")

    incoming_below = pack_movers(1, 1)
    incoming_above = pack_movers(2, -1)
    species_after_step = jnp.concatenate([balanced_slots.reshape(N_SLAB, N_DEPTH, N_DEPTH * SLOT_CAPACITY, SPECIES_COUNT), incoming_below, incoming_above], axis=2)
    return grid_field, species_after_step.reshape(-1, SPECIES_COUNT)
```

```python
import functools

import jax
import jax.numpy as jnp
from jax import lax
from jax.experimental import pallas as pl
from jax.experimental.pallas import tpu as pltpu
from jax.sharding import PartitionSpec as P

MIG = 128
SCREENING = 0.05
DAMPING = 2.0 / 3.0
CENTRE = 6.0 + SCREENING
COARSE_CENTRE = 6.0 + 4.0 * SCREENING
HALO = 4
F32, BF16 = jnp.float32, jnp.bfloat16
VMEM_SPEC = pl.BlockSpec(memory_space=pltpu.VMEM)
ANY_SPEC = pl.BlockSpec(memory_space=pl.ANY)
SMEM_SPEC = pl.BlockSpec(memory_space=pltpu.SMEM)
PARAMS = pltpu.CompilerParams(vmem_limit_bytes=40 * 1024 * 1024)


def dot(a, b, ca, cb):
    return lax.dot_general(a, b, (((ca,), (cb,)), ((), ())), preferred_element_type=F32)


def halves(x):
    high = x.astype(BF16)
    return high, (x - high.astype(F32)).astype(BF16)


def iota(shape, dim):
    return lax.broadcasted_iota(jnp.int32, shape, dim)


def cyclic(x, axis, by):
    count = lax.axis_size(axis)
    return lax.ppermute(x, axis, [(i, (i + by) % count) for i in range(count)])


def uptake_kernel(
    u_ref, cell_ref, death_ref, divide_ref, species_ref, weight_ref,
    t_ref, sensed_ref, low_ref, high_ref, front_ref, back_ref,
):
    nx, ny, nz = u_ref.shape
    agents = species_ref.shape[0]
    rows = nx * ny
    u = u_ref[...].reshape(rows, nz)
    cell = cell_ref[...].reshape(1, agents)
    cell_row = cell // nz
    cell_z = cell - cell_row * nz
    one_z = (iota((nz, agents), 0) == cell_z).astype(F32).astype(BF16)
    in_row = iota((rows, agents), 0) == cell_row
    high, low = halves(u)
    picked = dot(high, one_z, 1, 0) + dot(low, one_z, 1, 0)
    sample = jnp.sum(jnp.where(in_row, picked, 0.0), axis=0, keepdims=True)
    sensed_ref[...] = jnp.broadcast_to(sample, (8, agents)).astype(BF16).astype(F32)
    weight = jnp.broadcast_to(weight_ref[...].reshape(1, -1), (8, species_ref.shape[1]))
    score = dot(weight, species_ref[...], 1, 1)[0:1]
    softplus = jnp.maximum(score, 0.0) + jnp.log1p(jnp.exp(-jnp.abs(score)))
    alive = (1 - death_ref[...].reshape(1, agents)).astype(F32)
    divide = divide_ref[...].reshape(1, agents).astype(F32)
    uptake = alive * (1.0 + divide) * softplus * sample / (0.5 + sample)
    up_high = uptake.astype(BF16).astype(F32)
    a_high = jnp.where(in_row, up_high, 0.0).astype(BF16)
    a_low = jnp.where(in_row, uptake - up_high, 0.0).astype(BF16)
    source = dot(a_high, one_z, 1, 1) + dot(a_low, one_z, 1, 1)
    t_ref[...] = (SCREENING * u - source).reshape(nx, ny, nz)
    for pair in range(nx // 2):
        for ref, start in ((low_ref, 0), (high_ref, ny - HALO)):
            parts = []
            for plane in (2 * pair, 2 * pair + 1):
                parts.append(u_ref[plane, start : start + HALO])
                parts.append(t_ref[plane, start : start + HALO])
            ref[pair] = jnp.concatenate(parts, axis=0).astype(BF16)
    half = ny // 16
    for ref, u_start, t_start in ((front_ref, nx - HALO, nx - HALO + 1), (back_ref, 0, 0)):
        at = 0
        for field, start, count in ((u_ref, u_start, HALO), (t_ref, t_start, HALO - 1)):
            for plane in range(start, start + count):
                ref[at : at + half] = field[plane].astype(BF16).reshape(half, 16, nz)
                at += half


def network_kernel(
    me_ref, species_ref, sensed_ref, death_ref, move_ref, route_ref, net_ref, sensing_ref, *outs
):
    agents, width = species_ref.shape
    depths = len(outs) - 2
    capacity = outs[0].shape[0]
    species = species_ref[...]
    sensing = sensing_ref[...].reshape(1, width)
    first = sensing.astype(BF16)
    rest = sensing - first.astype(F32)
    second = rest.astype(BF16)
    third = (rest - second.astype(F32)).astype(BF16)
    line = iota((8, width), 0)
    terms = jnp.where(
        line == 0, first.astype(F32),
        jnp.where(line == 1, second.astype(F32), jnp.where(line == 2, third.astype(F32), 0.0)),
    ).astype(BF16)
    activation = dot(species, net_ref[...], 1, 0) + dot(sensed_ref[...].astype(BF16), terms, 0, 0)
    updated = (0.5 * species.astype(F32) + jnp.tanh(activation)).astype(BF16)
    lanes = 128
    lines = -(-(depths + 2) // 8) * 8
    line = iota((lines, lanes), 0)
    square = iota((lanes, 2 * lanes), 0)
    column = iota((lanes, 2 * lanes), 1)
    counter = jnp.where(jnp.logical_or(column >= lanes, square < column), 1.0, 0.0).astype(BF16)
    blocks = agents // lanes
    route = route_ref[...].reshape(1, agents)
    move = move_ref[...].reshape(1, agents)
    death = death_ref[...].reshape(1, agents)
    hits = []
    for block in range(blocks):
        cut = slice(block * lanes, (block + 1) * lanes)
        wanted = jnp.where(line < depths, route[:, cut], jnp.where(line < depths + 2, move[:, cut] + (depths - 1), -1))
        hits.append((wanted == line).astype(F32))
    counts = dot(jnp.concatenate(hits, axis=0).astype(BF16), counter, 1, 0)
    me = me_ref[0]
    running = jnp.zeros((lines, lanes), F32)
    keys = []
    for block in range(blocks):
        cut = slice(block * lanes, (block + 1) * lanes)
        own = slice(block * lines, (block + 1) * lines)
        before = (counts[own, :lanes] + running) * hits[block]
        running = running + counts[own, lanes:]
        slot = jnp.sum(jnp.where(line < depths, before, 0.0), axis=0, keepdims=True).astype(jnp.int32)
        rank = jnp.sum(jnp.where(line < depths, 0.0, before), axis=0, keepdims=True).astype(jnp.int32)
        hop = route[:, cut] - me
        hop = jnp.where(hop < 0, hop + depths, hop)
        key = jnp.where(
            move[:, cut] == 0, hop * capacity + slot, depths * capacity + (move[:, cut] - 1) * MIG + rank
        )
        keys.append(jnp.where(death[:, cut] == 0, key, -1))
    key = jnp.concatenate(keys, axis=1)
    start = 0
    for out in outs:
        size = out.shape[0]
        chosen = (iota((size, agents), 0) == key - start).astype(F32).astype(BF16)
        out[...] = dot(chosen, updated, 1, 0).astype(BF16)
        start += size


def third_sum(x):
    width = 128
    tiles = x.shape[1] // width
    lane = iota((x.shape[0], width), 1)
    parts = [x[:, i * width : (i + 1) * width] for i in range(tiles)]
    ups = [pltpu.roll(part, 1, 1) for part in parts]
    downs = [pltpu.roll(part, width - 1, 1) for part in parts]
    sums = []
    for i in range(tiles):
        before = ups[i - 1] if i else 0.0
        after = downs[i + 1] if i < tiles - 1 else 0.0
        sums.append(jnp.where(lane == 0, before, ups[i]) + jnp.where(lane == width - 1, after, downs[i]))
    return jnp.concatenate(sums, axis=1)


def neighbour_total(before, plane, after):
    rows = plane.shape[0]
    second = pltpu.roll(plane, 1, 0) + pltpu.roll(plane, rows - 1, 0)
    return before + after + second + third_sum(plane)


def relaxed(before, plane, after, target, centre):
    return (1.0 - DAMPING) * plane + (DAMPING / centre) * (
        target + neighbour_total(before, plane, after)
    )


def edge_mask(me, depths, halo):
    row = iota((2 * halo, 1), 0)
    return jnp.where(
        row < halo, (me < depths - 1).astype(F32), (me > 0).astype(F32)
    )


def masked(plane, own, mask):
    return jnp.concatenate([plane[:own], plane[own:] * mask], axis=0)


def smooth_kernel(
    depths, me_ref, u_ref, t_ref, above_ref, below_ref, before_ref, after_ref,
    u2_ref, text_ref, coarse_ref, coarse_all_ref, coarse_low_ref, coarse_high_ref,
    u0, u1, paired,
):
    nx, ny, nz = u_ref.shape
    ext = ny + 2 * HALO
    mask = edge_mask(me_ref[0], depths, HALO)

    def halo_rows(upper, lower, plane):
        at = 8 * (plane % 2)
        high = upper[at : at + 8]
        low = lower[at : at + 8]
        return (
            jnp.concatenate([high[:HALO], low[:HALO]], axis=0) * mask,
            jnp.concatenate([high[HALO:], low[HALO:]], axis=0),
        )

    half = ny // 16
    own_size = (2 * HALO - 1) * half
    pairs = HALO // 2
    for plane in range(nx):
        u0[HALO + plane, :ny] = u_ref[plane]
        text_ref[HALO - 1 + plane, :ny] = t_ref[plane]
        pair = plane // 2
        uh, th = halo_rows(above_ref[pair].astype(F32), below_ref[pair].astype(F32), plane)
        u0[HALO + plane, ny:] = uh
        text_ref[HALO - 1 + plane, ny:] = th
    for ref, u_at, t_at, shift in ((before_ref, 0, 0, 1), (after_ref, HALO + nx, HALO - 1 + nx, 0)):
        for k in range(HALO):
            u0[u_at + k, :ny] = ref[k * half : (k + 1) * half].astype(F32).reshape(ny, nz)
            pair = k // 2
            uh, th = halo_rows(
                ref[own_size + pair].astype(F32), ref[own_size + pairs + pair].astype(F32), k
            )
            u0[u_at + k, ny:] = uh
            j = k - shift
            if 0 <= j < HALO - 1:
                at = (HALO + j) * half
                text_ref[t_at + j, :ny] = ref[at : at + half].astype(F32).reshape(ny, nz)
                text_ref[t_at + j, ny:] = th

    def first(p, carry):
        v = relaxed(u0[p], u0[p + 1], u0[p + 2], text_ref[p], CENTRE)
        u1[p] = masked(v, ny, mask)
        return carry

    lax.fori_loop(0, nx + 2 * HALO - 2, first, 0)

    def second(p, carry):
        v = relaxed(u1[p], u1[p + 1], u1[p + 2], text_ref[p + 1], CENTRE)
        u2_ref[p] = masked(v, ny, mask)
        return carry

    lax.fori_loop(0, nx + 2 * HALO - 4, second, 0)

    def residual(p):
        v = u2_ref[p + 2]
        total = neighbour_total(u2_ref[p + 1], v, u2_ref[p + 3])
        return (text_ref[p + 3] - CENTRE * v + total)[:ny]

    def rest(q, carry):
        both = residual(2 * q) + residual(2 * q + 1)
        for i in range(nz // 128):
            paired[q, i] = both[:, i * 128 : (i + 1) * 128]
        return carry

    lax.fori_loop(0, nx // 2, rest, 0)
    cx, cy, cz = coarse_ref.shape
    flat = jnp.concatenate(
        [
            jnp.concatenate(
                [
                    paired[q, i, pl.ds(0, cy, 2), :] + paired[q, i, pl.ds(1, cy, 2), :]
                    for i in range(nz // 128)
                ],
                axis=1,
            )
            for q in range(cx)
        ],
        axis=0,
    )
    fold = ((iota((nz, cz), 0) >> 1) == iota((nz, cz), 1)).astype(F32).astype(BF16)
    high, low = halves(flat)
    coarse = 0.5 * (dot(high, fold, 1, 0) + dot(low, fold, 1, 0))
    coarse_ref[...] = coarse.reshape(cx, cy, cz)
    coarse_all_ref[...] = coarse.astype(BF16).reshape(cx, cy, cz)
    for ref, start in ((coarse_low_ref, 0), (coarse_high_ref, cy - HALO)):
        ref[0] = jnp.concatenate(
            [coarse_ref[q, start : start + HALO] for q in range(cx)], axis=0
        ).astype(BF16)


def correct_kernel(
    depths, me_ref, ct_ref, above_ref, below_ref, before_ref, after_ref, u2_ref, text_ref, *rest
):
    packed = rest[: depths + 2]
    out_ref, agents_ref, ca, cb, u3, u4, sem = rest[depths + 2 :]
    nx, ny, nz = out_ref.shape
    cx, cy, cz = ct_ref.shape
    me = me_ref[0]
    capacity = packed[0].shape[0]
    copies = []
    for k in range(depths):
        origin = me - k
        origin = jnp.where(origin < 0, origin + depths, origin)
        place = pl.ds(pl.multiple_of(origin * capacity, capacity), capacity)
        copies.append(pltpu.make_async_copy(packed[k], agents_ref.at[place], sem.at[k]))
    for k in range(2):
        place = pl.ds(depths * capacity + k * MIG, MIG)
        copies.append(pltpu.make_async_copy(packed[depths + k], agents_ref.at[place], sem.at[depths + k]))
    for copy in copies:
        copy.start()
    mask = edge_mask(me, depths, HALO)
    total_planes = cx + 2 * HALO
    planes = []
    for p in range(total_planes):
        if p < HALO:
            ref, k = before_ref, p + cx - HALO
        elif p < HALO + cx:
            ref, k = None, p - HALO
        else:
            ref, k = after_ref, p - HALO - cx
        rows = slice(HALO * k, HALO * (k + 1))
        if ref is None:
            own = ct_ref[k]
            high = above_ref[0].astype(F32)[rows]
            low = below_ref[0].astype(F32)[rows]
        else:
            own = ref[k].astype(F32)
            high = ref[cx].astype(F32)[rows]
            low = ref[cx + 1].astype(F32)[rows]
        planes.append(jnp.concatenate([own, jnp.concatenate([high, low], axis=0) * mask], axis=0))
    values = [(DAMPING / COARSE_CENTRE) * plane for plane in planes]
    for sweep in range(1, HALO):
        values = [
            masked(
                relaxed(values[i - 1], values[i], values[i + 1], planes[i + sweep - 1], COARSE_CENTRE),
                cy,
                mask,
            )
            for i in range(1, len(values) - 1)
        ]
    wide = cy + 4
    flat = jnp.concatenate(
        [jnp.concatenate([v[: cy + 2], v[cy + 2 * HALO - 2 :]], axis=0) for v in values], axis=0
    )
    spread = (iota((cz, nz), 0) == (iota((cz, nz), 1) >> 1)).astype(F32).astype(BF16)
    high, low = halves(flat)
    cb[...] = dot(high, spread, 1, 0) + dot(low, spread, 1, 0)
    for q in range(len(values)):
        for i in range(nz // 128):
            part = cb[q * wide : (q + 1) * wide, i * 128 : (i + 1) * 128]
            ca[q, i, pl.ds(0, wide, 2), :] = part
            ca[q, i, pl.ds(1, wide, 2), :] = part

    def add(p, carry):
        q = p // 2
        correction = jnp.concatenate([ca[q, i] for i in range(nz // 128)], axis=1)
        u3[p] = u2_ref[p] + correction
        return carry

    lax.fori_loop(0, nx + 4, add, 0)

    def first(p, carry):
        v = relaxed(u3[p], u3[p + 1], u3[p + 2], text_ref[p + 2], CENTRE)
        u4[p] = masked(v, ny, mask)
        return carry

    lax.fori_loop(0, nx + 2, first, 0)

    def second(p, carry):
        v = relaxed(u4[p], u4[p + 1], u4[p + 2], text_ref[p + 3], CENTRE)
        out_ref[p] = v[:ny]
        return carry

    lax.fori_loop(0, nx, second, 0)
    for copy in copies:
        copy.wait()


def local(
    nutrient, species, agent_cell, death_flag, divide_flag, slab_move, depth_route, net_weight, sensing, uptake_weight
):
    depths = lax.axis_size("depth")
    nx, ny, nz = nutrient.shape
    agents, width = species.shape
    capacity = 2 * agents // depths
    me = lax.axis_index("depth").astype(jnp.int32).reshape(1)
    shape = jax.ShapeDtypeStruct
    cells, death, divide = (x.reshape(1, agents) for x in (agent_cell, death_flag, divide_flag))
    move, route = slab_move.reshape(1, agents), depth_route.reshape(1, agents)
    slab_size = (2 * HALO - 1) * ny // 16
    target, sensed, low, high, front, back = pl.pallas_call(
        uptake_kernel,
        out_shape=(
            shape((nx, ny, nz), F32),
            shape((8, agents), F32),
            shape((nx // 2, 16, nz), BF16),
            shape((nx // 2, 16, nz), BF16),
            shape((slab_size, 16, nz), BF16),
            shape((slab_size, 16, nz), BF16),
        ),
        in_specs=[VMEM_SPEC] * 6,
        out_specs=[VMEM_SPEC] * 6,
        compiler_params=PARAMS,
        name="uptake",
    )(nutrient, cells, death, divide, species, uptake_weight.reshape(1, width))
    above = cyclic(low, "depth", -1)
    below = cyclic(high, "depth", 1)
    sent = pl.pallas_call(
        network_kernel,
        out_shape=tuple(shape((capacity, width), BF16) for _ in range(depths))
        + tuple(shape((MIG, width), BF16) for _ in range(2)),
        in_specs=[SMEM_SPEC] + [VMEM_SPEC] * 7,
        out_specs=[VMEM_SPEC] * (depths + 2),
        compiler_params=PARAMS,
        cost_estimate=pl.CostEstimate(flops=2 * 2304 * agents * width, bytes_accessed=1 << 20, transcendentals=agents * width),
        name="network",
    )(me, species, sensed, death, move, route, net_weight, sensing.reshape(1, width))
    pairs = HALO // 2
    all_pairs = nx // 2
    front = jnp.concatenate([front, above[all_pairs - pairs :], below[all_pairs - pairs :]], axis=0)
    back = jnp.concatenate([back, above[:pairs], below[:pairs]], axis=0)
    before = cyclic(front, "slab", 1)
    after = cyclic(back, "slab", -1)
    arrived = [sent[0]] + [cyclic(sent[k], "depth", k) for k in range(1, depths)]
    arrived += [cyclic(sent[depths], "slab", 1), cyclic(sent[depths + 1], "slab", -1)]
    cx, cy, cz = nx // 2, ny // 2, nz // 2
    ext = ny + 2 * HALO
    u2, text, ct, ct_all, ct_low, ct_high = pl.pallas_call(
        functools.partial(smooth_kernel, depths),
        out_shape=(
            shape((nx + 4, ext, nz), F32),
            shape((nx + 2 * HALO - 2, ext, nz), F32),
            shape((cx, cy, cz), F32),
            shape((cx, cy, cz), BF16),
            shape((1, cx * HALO, cz), BF16),
            shape((1, cx * HALO, cz), BF16),
        ),
        in_specs=[SMEM_SPEC] + [VMEM_SPEC] * 6,
        out_specs=[VMEM_SPEC] * 6,
        scratch_shapes=[
            pltpu.VMEM((nx + 2 * HALO, ext, nz), F32),
            pltpu.VMEM((nx + 2 * HALO - 2, ext, nz), F32),
            pltpu.VMEM((cx, nz // 128, ny, 128), F32),
        ],
        compiler_params=PARAMS,
        name="smooth",
    )(me, nutrient, target, above, below, before, after)
    ct_above = cyclic(ct_low, "depth", -1)
    ct_below = cyclic(ct_high, "depth", 1)
    message = jnp.concatenate([ct_all, ct_above, ct_below], axis=0)
    ct_before = cyclic(message, "slab", 1)
    ct_after = cyclic(message, "slab", -1)
    return pl.pallas_call(
        functools.partial(correct_kernel, depths),
        out_shape=(
            shape((nx, ny, nz), F32),
            shape((depths * capacity + 2 * MIG, width), BF16),
        ),
        in_specs=[SMEM_SPEC] + [VMEM_SPEC] * 7 + [ANY_SPEC] * (depths + 2),
        out_specs=[VMEM_SPEC, ANY_SPEC],
        scratch_shapes=[
            pltpu.VMEM((cx + 2, nz // 128, ext, 128), F32),
            pltpu.VMEM(((cx + 2) * (cy + 4), nz), F32),
            pltpu.VMEM((nx + 4, ext, nz), F32),
            pltpu.VMEM((nx + 2, ext, nz), F32),
            pltpu.SemaphoreType.DMA((depths + 2,)),
        ],
        compiler_params=PARAMS,
        name="correct",
    )(me, ct, ct_above, ct_below, ct_before, ct_after, u2, text, *arrived)


def solution(mesh):
    rows = P(("slab", "depth"))
    in_specs = (
        P("slab", "depth", None),
        P(("slab", "depth"), None),
        rows,
        rows,
        rows,
        rows,
        P(("slab", "depth"), None),
        P(),
        P(),
        P(),
    )
    out_specs = (P("slab", "depth", None), P(("slab", "depth"), None))
    return jax.shard_map(local, mesh=mesh, in_specs=in_specs, out_specs=out_specs, check_vma=False)
```

```python
import functools

import jax
import jax.numpy as jnp
from jax import lax
from jax.experimental import pallas as pl
from jax.experimental.pallas import tpu as pltpu
from jax.sharding import PartitionSpec as P

MIG = 128
SCREENING = 0.05
DAMPING = 2.0 / 3.0
CENTRE = 6.0 + SCREENING
COARSE_CENTRE = 6.0 + 4.0 * SCREENING
HALO = 4
F32, BF16 = jnp.float32, jnp.bfloat16
VMEM_SPEC = pl.BlockSpec(memory_space=pltpu.VMEM)
ANY_SPEC = pl.BlockSpec(memory_space=pl.ANY)
HBM_SPEC = pl.BlockSpec(memory_space=pltpu.HBM)
SMEM_SPEC = pl.BlockSpec(memory_space=pltpu.SMEM)
PARAMS = pltpu.CompilerParams(vmem_limit_bytes=40 * 1024 * 1024)


def dot(a, b, ca, cb):
    return lax.dot_general(a, b, (((ca,), (cb,)), ((), ())), preferred_element_type=F32)


def halves(x):
    high = x.astype(BF16)
    return high, (x - high.astype(F32)).astype(BF16)


def iota(shape, dim):
    return lax.broadcasted_iota(jnp.int32, shape, dim)


def cyclic(x, axis, by):
    count = lax.axis_size(axis)
    return lax.ppermute(x, axis, [(i, (i + by) % count) for i in range(count)])


def swapped(x, axis, which):
    count = lax.axis_size(axis)
    if count % 2:
        raise ValueError("odd axis")
    first = 0 if which == "a" else 1
    pairs = []
    for i in range(first, count, 2):
        j = (i + 1) % count
        pairs += [(i, j), (j, i)]
    return lax.ppermute(x, axis, sorted(pairs))


def is_even(x):
    return lax.rem(x, 2) == 0


def load_kernel(slab_ref, *refs):
    count = (len(refs) - 3) // 2
    sources, targets = refs[:count], refs[count : 2 * count]
    slab_a, slab_b, sem = refs[2 * count :]
    copies = [
        pltpu.make_async_copy(source, target, sem.at[i])
        for i, (source, target) in enumerate(zip(sources, targets))
    ]
    for copy in copies:
        copy.start()
    copies[0].wait()
    u_ref = targets[0]
    nx, ny, nz = u_ref.shape
    half = ny // 16
    even = is_even(slab_ref[0])
    for ref, front in ((slab_a, even), (slab_b, jnp.logical_not(even))):
        start = jnp.where(front, nx - HALO, 0)
        for k in range(HALO):
            ref[k * half : (k + 1) * half] = u_ref[start + k].astype(BF16).reshape(half, 16, nz)
    for copy in copies[1:]:
        copy.wait()


def uptake_kernel(
    me_ref, slab_ref, u_ref, cell_ref, death_ref, divide_ref, species_ref, weight_ref,
    t_ref, sensed_ref, depth_a, depth_b, slab_a, slab_b,
):
    nx, ny, nz = u_ref.shape
    agents = species_ref.shape[0]
    rows = nx * ny
    u = u_ref[...].reshape(rows, nz)
    cell = cell_ref[...].reshape(1, agents)
    cell_row = cell // nz
    cell_z = cell - cell_row * nz
    one_z = (iota((nz, agents), 0) == cell_z).astype(F32).astype(BF16)
    in_row = iota((rows, agents), 0) == cell_row
    high, low = halves(u)
    picked = dot(high, one_z, 1, 0) + dot(low, one_z, 1, 0)
    sample = jnp.sum(jnp.where(in_row, picked, 0.0), axis=0, keepdims=True)
    sensed_ref[...] = jnp.broadcast_to(sample, (8, agents)).astype(BF16).astype(F32)
    weight = jnp.broadcast_to(weight_ref[...].reshape(1, -1), (8, species_ref.shape[1]))
    score = dot(weight, species_ref[...], 1, 1)[0:1]
    softplus = jnp.maximum(score, 0.0) + jnp.log1p(jnp.exp(-jnp.abs(score)))
    alive = (1 - death_ref[...].reshape(1, agents)).astype(F32)
    divide = divide_ref[...].reshape(1, agents).astype(F32)
    uptake = alive * (1.0 + divide) * softplus * sample / (0.5 + sample)
    up_high = uptake.astype(BF16).astype(F32)
    a_high = jnp.where(in_row, up_high, 0.0).astype(BF16)
    a_low = jnp.where(in_row, uptake - up_high, 0.0).astype(BF16)
    source = dot(a_high, one_z, 1, 1) + dot(a_low, one_z, 1, 1)
    t_ref[...] = (SCREENING * u - source).reshape(nx, ny, nz)
    even = is_even(me_ref[0])
    for pair in range(nx // 2):
        parts = []
        for start in (0, ny - HALO):
            for plane in (2 * pair, 2 * pair + 1):
                parts.append(u_ref[plane, start : start + HALO])
                parts.append(t_ref[plane, start : start + HALO])
        low = jnp.concatenate(parts[:4], axis=0)
        high = jnp.concatenate(parts[4:], axis=0)
        depth_a[pair] = jnp.where(even, high, low).astype(BF16)
        depth_b[pair] = jnp.where(even, low, high).astype(BF16)
    half = ny // 16
    count = HALO - 1
    even = is_even(slab_ref[0])
    for ref, front in ((slab_a, even), (slab_b, jnp.logical_not(even))):
        start = jnp.where(front, nx - count, 0)
        for k in range(count):
            ref[k * half : (k + 1) * half] = t_ref[start + k].astype(BF16).reshape(half, 16, nz)


def network_kernel(
    me_ref, slab_ref, species_ref, sensed_ref, death_ref, move_ref, route_ref, net_ref, sensing_ref, *outs
):
    agents, width = species_ref.shape
    depths = len(outs) - 2
    capacity = outs[0].shape[0]
    species = species_ref[...]
    sensing = sensing_ref[...].reshape(1, width)
    first = sensing.astype(BF16)
    rest = sensing - first.astype(F32)
    second = rest.astype(BF16)
    third = (rest - second.astype(F32)).astype(BF16)
    line = iota((8, width), 0)
    terms = jnp.where(
        line == 0, first.astype(F32),
        jnp.where(line == 1, second.astype(F32), jnp.where(line == 2, third.astype(F32), 0.0)),
    ).astype(BF16)
    activation = dot(species, net_ref[...], 1, 0) + dot(sensed_ref[...].astype(BF16), terms, 0, 0)
    updated = (0.5 * species.astype(F32) + jnp.tanh(activation)).astype(BF16)
    lanes = 128
    lines = -(-(depths + 2) // 8) * 8
    line = iota((lines, lanes), 0)
    square = iota((lanes, 2 * lanes), 0)
    column = iota((lanes, 2 * lanes), 1)
    counter = jnp.where(jnp.logical_or(column >= lanes, square < column), 1.0, 0.0).astype(BF16)
    blocks = agents // lanes
    route = route_ref[...].reshape(1, agents)
    move = move_ref[...].reshape(1, agents)
    death = death_ref[...].reshape(1, agents)
    hits = []
    for block in range(blocks):
        cut = slice(block * lanes, (block + 1) * lanes)
        wanted = jnp.where(line < depths, route[:, cut], jnp.where(line < depths + 2, move[:, cut] + (depths - 1), -1))
        hits.append((wanted == line).astype(F32))
    counts = dot(jnp.concatenate(hits, axis=0).astype(BF16), counter, 1, 0)
    me = me_ref[0]
    to_a = jnp.where(is_even(slab_ref[0]), 1, 2)
    running = jnp.zeros((lines, lanes), F32)
    keys = []
    for block in range(blocks):
        cut = slice(block * lanes, (block + 1) * lanes)
        own = slice(block * lines, (block + 1) * lines)
        before = (counts[own, :lanes] + running) * hits[block]
        running = running + counts[own, lanes:]
        slot = jnp.sum(jnp.where(line < depths, before, 0.0), axis=0, keepdims=True).astype(jnp.int32)
        rank = jnp.sum(jnp.where(line < depths, 0.0, before), axis=0, keepdims=True).astype(jnp.int32)
        hop = route[:, cut] - me
        hop = jnp.where(hop < 0, hop + depths, hop)
        key = jnp.where(
            move[:, cut] == 0,
            hop * capacity + slot,
            depths * capacity + jnp.where(move[:, cut] == to_a, 0, MIG) + rank,
        )
        keys.append(jnp.where(death[:, cut] == 0, key, -1))
    key = jnp.concatenate(keys, axis=1)
    start = 0
    for index, out in enumerate(outs):
        size = capacity if index < depths else MIG
        chosen = (iota((size, agents), 0) == key - start).astype(F32).astype(BF16)
        placed = dot(chosen, updated, 1, 0).astype(BF16)
        start += size
        if index < depths:
            out[...] = placed
        else:
            tiles = out.shape[2] // width
            for i in range(MIG // 16):
                at = (i % tiles) * width
                out[i // tiles, :, at : at + width] = placed[i * 16 : (i + 1) * 16]


def third_sum(x):
    width = 128
    tiles = x.shape[1] // width
    lane = iota((x.shape[0], width), 1)
    parts = [x[:, i * width : (i + 1) * width] for i in range(tiles)]
    ups = [pltpu.roll(part, 1, 1) for part in parts]
    downs = [pltpu.roll(part, width - 1, 1) for part in parts]
    sums = []
    for i in range(tiles):
        before = ups[i - 1] if i else 0.0
        after = downs[i + 1] if i < tiles - 1 else 0.0
        sums.append(jnp.where(lane == 0, before, ups[i]) + jnp.where(lane == width - 1, after, downs[i]))
    return jnp.concatenate(sums, axis=1)


def neighbour_total(before, plane, after):
    rows = plane.shape[0]
    second = pltpu.roll(plane, 1, 0) + pltpu.roll(plane, rows - 1, 0)
    return before + after + second + third_sum(plane)


def relaxed(before, plane, after, target, centre):
    return (1.0 - DAMPING) * plane + (DAMPING / centre) * (
        target + neighbour_total(before, plane, after)
    )


def edge_mask(me, depths, halo):
    row = iota((2 * halo, 1), 0)
    return jnp.where(
        row < halo, (me < depths - 1).astype(F32), (me > 0).astype(F32)
    )


def masked(plane, own, mask):
    return jnp.concatenate([plane[:own], plane[own:] * mask], axis=0)


def halo_rows(side_a, side_b, even, plane, mask):
    at = 2 * HALO * (plane % 2)
    side_a = side_a[at : at + 2 * HALO].astype(F32)
    side_b = side_b[at : at + 2 * HALO].astype(F32)
    high = jnp.where(even, side_a, side_b)
    low = jnp.where(even, side_b, side_a)
    return (
        jnp.concatenate([high[:HALO], low[:HALO]], axis=0) * mask,
        jnp.concatenate([high[HALO:], low[HALO:]], axis=0),
    )


def inner_kernel(
    depths, me_ref, u_ref, t_ref, side_a, side_b, u0, text_ref, u1, u2_ref, inside
):
    nx, ny, nz = u_ref.shape
    even = is_even(me_ref[0])
    mask = edge_mask(me_ref[0], depths, HALO)
    for plane in range(nx):
        u0[HALO + plane, :ny] = u_ref[plane]
        text_ref[HALO - 1 + plane, :ny] = t_ref[plane]
        uh, th = halo_rows(side_a[plane // 2], side_b[plane // 2], even, plane, mask)
        u0[HALO + plane, ny:] = uh
        text_ref[HALO - 1 + plane, ny:] = th

    def first(p, carry):
        v = relaxed(u0[p], u0[p + 1], u0[p + 2], text_ref[p], CENTRE)
        u1[p] = masked(v, ny, mask)
        return carry

    lax.fori_loop(HALO, nx + HALO - 2, first, 0)

    def second(p, carry):
        v = relaxed(u1[p], u1[p + 1], u1[p + 2], text_ref[p + 1], CENTRE)
        u2_ref[p] = masked(v, ny, mask)
        return carry

    lax.fori_loop(HALO, nx, second, 0)
    for p in range(3, nx - 3):
        inside[p - 3] = residual(u2_ref, text_ref, p, ny)


def residual(u2_ref, text_ref, p, ny):
    v = u2_ref[p + 2]
    total = neighbour_total(u2_ref[p + 1], v, u2_ref[p + 3])
    return (text_ref[p + 3] - CENTRE * v + total)[:ny]


def smooth_kernel(
    depths, me_ref, slab_ref, u0_in, text_in, u1_in, u2_in, inside, field_a, field_b, slab_a, slab_b,
    u0, text_ref, u1, u2_ref, coarse_ref, coarse_all_ref, coarse_a, coarse_b, paired,
):
    nx = u0.shape[0] - 2 * HALO
    ny, nz = u0.shape[1] - 2 * HALO, u0.shape[2]
    mask = edge_mask(me_ref[0], depths, HALO)
    half = ny // 16
    pairs = HALO // 2
    own = (HALO - 1) * half
    even = is_even(me_ref[0])
    slab_even = is_even(slab_ref[0])
    for field, ref, after in (
        (field_a, slab_a, slab_even), (field_b, slab_b, jnp.logical_not(slab_even))
    ):
        u_at = jnp.where(after, HALO + nx, 0)
        t_at = jnp.where(after, HALO - 1 + nx, 0)
        sides = []
        for k in range(HALO):
            u0[u_at + k, :ny] = field[k * half : (k + 1) * half].astype(F32).reshape(ny, nz)
            uh, th = halo_rows(ref[own + k // 2], ref[own + pairs + k // 2], even, k, mask)
            u0[u_at + k, ny:] = uh
            sides.append(th)
        for k in range(HALO - 1):
            text_ref[t_at + k, :ny] = ref[k * half : (k + 1) * half].astype(F32).reshape(ny, nz)
            text_ref[t_at + k, ny:] = jnp.where(after, sides[k], sides[k + 1])

    def first(i, carry):
        for p in (i, nx + 2 + i):
            v = relaxed(u0[p], u0[p + 1], u0[p + 2], text_ref[p], CENTRE)
            u1[p] = masked(v, ny, mask)
        return carry

    lax.fori_loop(0, HALO, first, 0)

    def second(i, carry):
        for p in (i, nx + i):
            v = relaxed(u1[p], u1[p + 1], u1[p + 2], text_ref[p + 1], CENTRE)
            u2_ref[p] = masked(v, ny, mask)
        return carry

    lax.fori_loop(0, HALO, second, 0)
    for q in range(nx // 2):
        both = 0.0
        for p in (2 * q, 2 * q + 1):
            known = 3 <= p < nx - 3
            both = both + (inside[p - 3] if known else residual(u2_ref, text_ref, p, ny))
        for i in range(nz // 128):
            paired[q, i] = both[:, i * 128 : (i + 1) * 128]
    cx, cy, cz = coarse_ref.shape
    flat = jnp.concatenate(
        [
            jnp.concatenate(
                [
                    paired[q, i, pl.ds(0, cy, 2), :] + paired[q, i, pl.ds(1, cy, 2), :]
                    for i in range(nz // 128)
                ],
                axis=1,
            )
            for q in range(cx)
        ],
        axis=0,
    )
    fold = ((iota((nz, cz), 0) >> 1) == iota((nz, cz), 1)).astype(F32).astype(BF16)
    high, low = halves(flat)
    coarse = 0.5 * (dot(high, fold, 1, 0) + dot(low, fold, 1, 0))
    coarse_ref[...] = coarse.reshape(cx, cy, cz)
    coarse_all_ref[...] = coarse.astype(BF16).reshape(cx, cy, cz)
    low, high = (
        jnp.concatenate([coarse_ref[q, start : start + HALO] for q in range(cx)], axis=0)
        for start in (0, cy - HALO)
    )
    coarse_a[0] = jnp.where(even, high, low).astype(BF16)
    coarse_b[0] = jnp.where(even, low, high).astype(BF16)


def post_kernel(depths, me_ref, u2_ref, text_ref, out_ref, v1):
    nx, ny, nz = out_ref.shape
    mask = edge_mask(me_ref[0], depths, HALO)

    def first(p, carry):
        v = relaxed(u2_ref[p], u2_ref[p + 1], u2_ref[p + 2], text_ref[p + 2], CENTRE)
        v1[p] = masked(v, ny, mask)
        return carry

    lax.fori_loop(0, nx + 2, first, 0)

    def second(p, carry):
        v = relaxed(v1[p], v1[p + 1], v1[p + 2], text_ref[p + 3], CENTRE)
        out_ref[p] = v[:ny]
        return carry

    lax.fori_loop(0, nx, second, 0)


def correct_kernel(
    depths, me_ref, slab_ref, ct_ref, side_a, side_b, slab_a, slab_b, base_ref, *rest
):
    packed = rest[:depths]
    out_ref, agents_ref, fine, sem = rest[depths:]
    nx, ny, nz = out_ref.shape
    cx, cy, cz = ct_ref.shape
    me = me_ref[0]
    even = is_even(me)
    slab_even = is_even(slab_ref[0])
    capacity = packed[0].shape[0]
    width = agents_ref.shape[1]
    copies = []
    for k in range(depths):
        origin = me - k
        origin = jnp.where(origin < 0, origin + depths, origin)
        place = pl.ds(pl.multiple_of(origin * capacity, capacity), capacity)
        copies.append(pltpu.make_async_copy(packed[k], agents_ref.at[place], sem.at[len(copies)]))
    tiles = cz // width
    for ref, late in ((slab_a, slab_even), (slab_b, jnp.logical_not(slab_even))):
        start = depths * capacity + jnp.where(late, MIG, 0)
        for i in range(MIG // 16):
            place = pl.ds(pl.multiple_of(start + i * 16, 16), 16)
            source = ref.at[cx + 2 + i // tiles, :, pl.ds((i % tiles) * width, width)]
            copies.append(pltpu.make_async_copy(source, agents_ref.at[place], sem.at[len(copies)]))
    for copy in copies:
        copy.start()
    mask = edge_mask(me, depths, HALO)

    def chosen(condition, x, y):
        return jnp.where(condition, x.astype(F32), y.astype(F32))

    planes = []
    for p in range(cx + 2 * HALO):
        if HALO <= p < HALO + cx:
            k = p - HALO
            own, one, two = ct_ref[k], side_a[0].astype(F32), side_b[0].astype(F32)
        else:
            before = p < HALO
            k = p + cx - HALO if before else p - HALO - cx
            x, y = (slab_b, slab_a) if before else (slab_a, slab_b)
            own, one, two = (chosen(slab_even, x[i], y[i]) for i in (k, cx, cx + 1))
        rows = slice(HALO * k, HALO * (k + 1))
        one, two = one[rows], two[rows]
        sides = jnp.concatenate([jnp.where(even, one, two), jnp.where(even, two, one)], axis=0)
        planes.append(jnp.concatenate([own, sides * mask], axis=0))
    values = [(DAMPING / COARSE_CENTRE) * plane for plane in planes]
    for sweep in range(1, HALO):
        values = [
            masked(
                relaxed(values[i - 1], values[i], values[i + 1], planes[i + sweep - 1], COARSE_CENTRE),
                cy,
                mask,
            )
            for i in range(1, len(values) - 1)
        ]
    wide = cy + 4
    for q, value in enumerate(values):
        value = jnp.concatenate([value[: cy + 2], value[cy + 2 * HALO - 2 :]], axis=0)
        for i in range(cz // 128):
            part = value[:, i * 128 : (i + 1) * 128]
            fine[q, i, pl.ds(0, wide, 2), :] = part
            fine[q, i, pl.ds(1, wide, 2), :] = part
    keep, pull = 1.0 - DAMPING, DAMPING / CENTRE

    def second_total(plane):
        rows = plane.shape[0]
        return pltpu.roll(plane, 1, 0) + pltpu.roll(plane, rows - 1, 0)

    spread = [jnp.concatenate([fine[q, i] for i in range(cz // 128)], axis=1) for q in range(cx + 2)]
    still = [keep * plane + pull * second_total(plane) for plane in spread]
    once = []
    for p in range(-1, nx + 1):
        q = (p + 2) // 2
        if p % 2 == 0:
            others = spread[q - 1] + spread[q]
        else:
            others = spread[q] + spread[q + 1]
        once.append(masked(still[q] + pull * others, ny, mask))
    none, one, two = [], [], []
    for p in range(nx):
        plane = once[p + 1]
        total = once[p] + once[p + 2] + second_total(plane)
        none.append((keep * plane + pull * total)[:ny])
        one.append(plane[:ny])
        two.append(spread[(p + 2) // 2][:ny])
    z = iota((cz, nz), 1)
    k = iota((cz, nz), 0)

    def hit(shift):
        moved = z + shift
        inside = jnp.logical_and(moved >= 0, moved < nz)
        return jnp.logical_and((moved >> 1) == k, inside).astype(F32)

    here, left, right = hit(0), hit(-1), hit(1)
    paths = jnp.where(jnp.logical_or(z == 0, z == nz - 1), here, 2.0 * here)
    spread_none = here.astype(BF16)
    spread_one = ((left + right) * 1.0).astype(BF16)
    spread_two = (hit(-2) + hit(2) + paths).astype(BF16)
    total = base_ref[...].reshape(nx * ny, nz)
    for parts, scale, matrix in (
        (none, 1.0, spread_none), (one, 2.0 * pull, spread_one), (two, pull * pull, spread_two)
    ):
        high, low = halves(scale * jnp.concatenate(parts, axis=0))
        total = total + dot(high, matrix, 1, 0) + dot(low, matrix, 1, 0)
    out_ref[...] = total.reshape(nx, ny, nz)
    for copy in copies:
        copy.wait()


def local(
    nutrient, species, agent_cell, death_flag, divide_flag, slab_move, depth_route, net_weight, sensing, uptake_weight
):
    depths = lax.axis_size("depth")
    nx, ny, nz = nutrient.shape
    agents, width = species.shape
    capacity = 2 * agents // depths
    me = lax.axis_index("depth").astype(jnp.int32).reshape(1)
    slab = lax.axis_index("slab").astype(jnp.int32).reshape(1)
    shape = jax.ShapeDtypeStruct
    cells, death, divide = (x.reshape(1, agents) for x in (agent_cell, death_flag, divide_flag))
    move, route = slab_move.reshape(1, agents), depth_route.reshape(1, agents)
    half = ny // 16
    arguments = (
        nutrient, cells, species, uptake_weight.reshape(1, width), death, divide,
        move, route, net_weight, sensing.reshape(1, width),
    )
    loaded = pl.pallas_call(
        load_kernel,
        out_shape=tuple(shape(x.shape, x.dtype) for x in arguments)
        + tuple(shape((HALO * half, 16, nz), BF16) for _ in range(2)),
        in_specs=[SMEM_SPEC] + [HBM_SPEC] * len(arguments),
        out_specs=[VMEM_SPEC] * (len(arguments) + 2),
        scratch_shapes=[pltpu.SemaphoreType.DMA((len(arguments),))],
        compiler_params=PARAMS,
        name="load",
    )(slab, *(pltpu.with_memory_space_constraint(x, pltpu.HBM) for x in arguments))
    nutrient, cells, species, weight, death, divide, move, route, net_weight, sensing = loaded[:-2]
    target, sensed, depth_a, depth_b, slab_a, slab_b = pl.pallas_call(
        uptake_kernel,
        out_shape=(
            shape((nx, ny, nz), F32),
            shape((8, agents), F32),
            shape((nx // 2, 16, nz), BF16),
            shape((nx // 2, 16, nz), BF16),
            shape(((HALO - 1) * half, 16, nz), BF16),
            shape(((HALO - 1) * half, 16, nz), BF16),
        ),
        in_specs=[SMEM_SPEC] * 2 + [VMEM_SPEC] * 6,
        out_specs=[VMEM_SPEC] * 6,
        compiler_params=PARAMS,
        name="uptake",
    )(me, slab, nutrient, cells, death, divide, species, weight)
    field_a, field_b, depth_a, depth_b = lax.optimization_barrier(
        (loaded[-2], loaded[-1], depth_a, depth_b)
    )
    side_a = swapped(depth_a, "depth", "a")
    side_b = swapped(depth_b, "depth", "b")
    field_a = swapped(field_a, "slab", "a")
    field_b = swapped(field_b, "slab", "b")
    pairs = HALO // 2
    slab_even = is_even(slab[0])
    last = nx // 2 - pairs

    def with_sides(own, start):
        parts = [lax.dynamic_slice_in_dim(side, start, pairs, 0) for side in (side_a, side_b)]
        return jnp.concatenate([own] + parts, axis=0)

    slab_a = swapped(with_sides(slab_a, jnp.where(slab_even, last, 0)), "slab", "a")
    slab_b = swapped(with_sides(slab_b, jnp.where(slab_even, 0, last)), "slab", "b")
    cx, cy, cz = nx // 2, ny // 2, nz // 2
    ext = ny + 2 * HALO
    sent = pl.pallas_call(
        network_kernel,
        out_shape=tuple(shape((capacity, width), BF16) for _ in range(depths))
        + tuple(shape((MIG * width // (16 * cz), 16, cz), BF16) for _ in range(2)),
        in_specs=[SMEM_SPEC] * 2 + [VMEM_SPEC] * 7,
        out_specs=[VMEM_SPEC] * (depths + 2),
        compiler_params=PARAMS,
        cost_estimate=pl.CostEstimate(
            flops=2 * 2304 * agents * width, bytes_accessed=1 << 20, transcendentals=agents * width
        ),
        name="network",
    )(me, slab, species, sensed, death, move, route, net_weight, sensing)
    arrived = [sent[0]] + [cyclic(sent[k], "depth", k) for k in range(1, depths)]
    u0, text, u1, u2, inside = pl.pallas_call(
        functools.partial(inner_kernel, depths),
        out_shape=(
            shape((nx + 2 * HALO, ext, nz), F32),
            shape((nx + 2 * HALO - 2, ext, nz), F32),
            shape((nx + 2 * HALO - 2, ext, nz), F32),
            shape((nx + 4, ext, nz), F32),
            shape((nx - 6, ny, nz), F32),
        ),
        in_specs=[SMEM_SPEC] + [VMEM_SPEC] * 4,
        out_specs=[VMEM_SPEC] * 5,
        compiler_params=PARAMS,
        cost_estimate=pl.CostEstimate(flops=1 << 30, bytes_accessed=1 << 22, transcendentals=0),
        name="inner",
    )(me, nutrient, target, side_a, side_b)
    _, text, _, u2, ct, ct_all, coarse_a, coarse_b = pl.pallas_call(
        functools.partial(smooth_kernel, depths),
        out_shape=(
            shape(u0.shape, F32),
            shape(text.shape, F32),
            shape(u1.shape, F32),
            shape(u2.shape, F32),
            shape((cx, cy, cz), F32),
            shape((cx, cy, cz), BF16),
            shape((1, cx * HALO, cz), BF16),
            shape((1, cx * HALO, cz), BF16),
        ),
        in_specs=[SMEM_SPEC] * 2 + [VMEM_SPEC] * 9,
        out_specs=[VMEM_SPEC] * 8,
        scratch_shapes=[pltpu.VMEM((cx, nz // 128, ny, 128), F32)],
        input_output_aliases={2: 0, 3: 1, 4: 2, 5: 3},
        compiler_params=PARAMS,
        name="smooth",
    )(me, slab, u0, text, u1, u2, inside, field_a, field_b, slab_a, slab_b)
    coarse_a = swapped(coarse_a, "depth", "a")
    coarse_b = swapped(coarse_b, "depth", "b")
    tail_a, tail_b = (
        swapped(jnp.concatenate([ct_all, coarse_a, coarse_b, movers], axis=0), "slab", which)
        for which, movers in (("a", sent[depths]), ("b", sent[depths + 1]))
    )
    base = pl.pallas_call(
        functools.partial(post_kernel, depths),
        out_shape=shape((nx, ny, nz), F32),
        in_specs=[SMEM_SPEC] + [VMEM_SPEC] * 2,
        out_specs=VMEM_SPEC,
        scratch_shapes=[pltpu.VMEM((nx + 2, ext, nz), F32)],
        compiler_params=PARAMS,
        cost_estimate=pl.CostEstimate(flops=1 << 30, bytes_accessed=1 << 22, transcendentals=0),
        name="post",
    )(me, u2, text)
    return pl.pallas_call(
        functools.partial(correct_kernel, depths),
        out_shape=(
            shape((nx, ny, nz), F32),
            shape((depths * capacity + 2 * MIG, width), BF16),
        ),
        in_specs=[SMEM_SPEC] * 2 + [VMEM_SPEC] * 6 + [ANY_SPEC] * depths,
        out_specs=[VMEM_SPEC, ANY_SPEC],
        scratch_shapes=[
            pltpu.VMEM((cx + 2, cz // 128, ext, 128), F32),
            pltpu.SemaphoreType.DMA((depths + 2 * (MIG // 16),)),
        ],
        compiler_params=PARAMS,
        name="correct",
    )(me, slab, ct, coarse_a, coarse_b, tail_a, tail_b, base, *arrived)


def solution(mesh):
    rows = P(("slab", "depth"))
    in_specs = (
        P("slab", "depth", None),
        P(("slab", "depth"), None),
        rows,
        rows,
        rows,
        rows,
        P(("slab", "depth"), None),
        P(),
        P(),
        P(),
    )
    out_specs = (P("slab", "depth", None), P(("slab", "depth"), None))
    return jax.shard_map(local, mesh=mesh, in_specs=in_specs, out_specs=out_specs, check_vma=False)
```

```python
import functools

import jax
import jax.numpy as jnp
from jax import lax
from jax.experimental import pallas as pl
from jax.experimental.pallas import tpu as pltpu
from jax.sharding import PartitionSpec as P

MIG = 128
SCREENING = 0.05
DAMPING = 2.0 / 3.0
CENTRE = 6.0 + SCREENING
COARSE_CENTRE = 6.0 + 4.0 * SCREENING
HALO = 4
F32, BF16 = jnp.float32, jnp.bfloat16
VMEM_SPEC = pl.BlockSpec(memory_space=pltpu.VMEM)
ANY_SPEC = pl.BlockSpec(memory_space=pl.ANY)
HBM_SPEC = pl.BlockSpec(memory_space=pltpu.HBM)
SMEM_SPEC = pl.BlockSpec(memory_space=pltpu.SMEM)
PARAMS = pltpu.CompilerParams(vmem_limit_bytes=40 * 1024 * 1024)


def dot(a, b, ca, cb):
    return lax.dot_general(a, b, (((ca,), (cb,)), ((), ())), preferred_element_type=F32)


def halves(x):
    high = x.astype(BF16)
    return high, (x - high.astype(F32)).astype(BF16)


def iota(shape, dim):
    return lax.broadcasted_iota(jnp.int32, shape, dim)


def cyclic(x, axis, by):
    count = lax.axis_size(axis)
    return lax.ppermute(x, axis, [(i, (i + by) % count) for i in range(count)])


def swapped(x, axis, which):
    count = lax.axis_size(axis)
    if count % 2:
        raise ValueError("odd axis")
    first = 0 if which == "a" else 1
    pairs = []
    for i in range(first, count, 2):
        j = (i + 1) % count
        pairs += [(i, j), (j, i)]
    return lax.ppermute(x, axis, sorted(pairs))


def is_even(x):
    return lax.rem(x, 2) == 0


def load_kernel(slab_ref, *refs):
    count = (len(refs) - 3) // 2
    sources, targets = refs[:count], refs[count : 2 * count]
    slab_a, slab_b, sem = refs[2 * count :]
    copies = [
        pltpu.make_async_copy(source, target, sem.at[i])
        for i, (source, target) in enumerate(zip(sources, targets))
    ]
    for copy in copies:
        copy.start()
    copies[0].wait()
    u_ref = targets[0]
    nx, ny, nz = u_ref.shape
    half = ny // 16
    even = is_even(slab_ref[0])
    for ref, front in ((slab_a, even), (slab_b, jnp.logical_not(even))):
        start = jnp.where(front, nx - HALO, 0)
        for k in range(HALO):
            ref[k * half : (k + 1) * half] = u_ref[start + k].astype(BF16).reshape(half, 16, nz)
    for copy in copies[1:]:
        copy.wait()


def uptake_kernel(
    me_ref, slab_ref, u_ref, cell_ref, death_ref, divide_ref, species_ref, weight_ref,
    t_ref, sensed_ref, depth_a, depth_b, slab_a, slab_b,
):
    nx, ny, nz = u_ref.shape
    agents = species_ref.shape[0]
    rows = nx * ny
    u = u_ref[...].reshape(rows, nz)
    cell = cell_ref[...].reshape(1, agents)
    cell_row = cell // nz
    cell_z = cell - cell_row * nz
    one_z = (iota((nz, agents), 0) == cell_z).astype(F32).astype(BF16)
    in_row = iota((rows, agents), 0) == cell_row
    high, low = halves(u)
    picked = dot(high, one_z, 1, 0) + dot(low, one_z, 1, 0)
    sample = jnp.sum(jnp.where(in_row, picked, 0.0), axis=0, keepdims=True)
    sensed_ref[...] = jnp.broadcast_to(sample, (8, agents)).astype(BF16).astype(F32)
    weight = jnp.broadcast_to(weight_ref[...].reshape(1, -1), (8, species_ref.shape[1]))
    score = dot(weight, species_ref[...], 1, 1)[0:1]
    softplus = jnp.maximum(score, 0.0) + jnp.log1p(jnp.exp(-jnp.abs(score)))
    alive = (1 - death_ref[...].reshape(1, agents)).astype(F32)
    divide = divide_ref[...].reshape(1, agents).astype(F32)
    uptake = alive * (1.0 + divide) * softplus * sample / (0.5 + sample)
    up_high = uptake.astype(BF16).astype(F32)
    a_high = jnp.where(in_row, up_high, 0.0).astype(BF16)
    a_low = jnp.where(in_row, uptake - up_high, 0.0).astype(BF16)
    source = dot(a_high, one_z, 1, 1) + dot(a_low, one_z, 1, 1)
    t_ref[...] = (SCREENING * u - source).reshape(nx, ny, nz)
    even = is_even(me_ref[0])
    for pair in range(nx // 2):
        parts = []
        for start in (0, ny - HALO):
            for plane in (2 * pair, 2 * pair + 1):
                parts.append(u_ref[plane, start : start + HALO])
                parts.append(t_ref[plane, start : start + HALO])
        low = jnp.concatenate(parts[:4], axis=0)
        high = jnp.concatenate(parts[4:], axis=0)
        depth_a[pair] = jnp.where(even, high, low).astype(BF16)
        depth_b[pair] = jnp.where(even, low, high).astype(BF16)
    half = ny // 16
    count = HALO - 1
    even = is_even(slab_ref[0])
    for ref, front in ((slab_a, even), (slab_b, jnp.logical_not(even))):
        start = jnp.where(front, nx - count, 0)
        for k in range(count):
            ref[k * half : (k + 1) * half] = t_ref[start + k].astype(BF16).reshape(half, 16, nz)


def network_kernel(
    me_ref, slab_ref, species_ref, sensed_ref, death_ref, move_ref, route_ref, net_ref, sensing_ref, *outs
):
    agents, width = species_ref.shape
    depths = len(outs) - 2
    capacity = outs[0].shape[0]
    species = species_ref[...]
    sensing = sensing_ref[...].reshape(1, width)
    first = sensing.astype(BF16)
    rest = sensing - first.astype(F32)
    second = rest.astype(BF16)
    third = (rest - second.astype(F32)).astype(BF16)
    line = iota((8, width), 0)
    terms = jnp.where(
        line == 0, first.astype(F32),
        jnp.where(line == 1, second.astype(F32), jnp.where(line == 2, third.astype(F32), 0.0)),
    ).astype(BF16)
    activation = dot(species, net_ref[...], 1, 0) + dot(sensed_ref[...].astype(BF16), terms, 0, 0)
    updated = (0.5 * species.astype(F32) + jnp.tanh(activation)).astype(BF16)
    lanes = 128
    lines = -(-(depths + 2) // 8) * 8
    line = iota((lines, lanes), 0)
    square = iota((lanes, 2 * lanes), 0)
    column = iota((lanes, 2 * lanes), 1)
    counter = jnp.where(jnp.logical_or(column >= lanes, square < column), 1.0, 0.0).astype(BF16)
    blocks = agents // lanes
    route = route_ref[...].reshape(1, agents)
    move = move_ref[...].reshape(1, agents)
    death = death_ref[...].reshape(1, agents)
    hits = []
    for block in range(blocks):
        cut = slice(block * lanes, (block + 1) * lanes)
        wanted = jnp.where(line < depths, route[:, cut], jnp.where(line < depths + 2, move[:, cut] + (depths - 1), -1))
        hits.append((wanted == line).astype(F32))
    counts = dot(jnp.concatenate(hits, axis=0).astype(BF16), counter, 1, 0)
    me = me_ref[0]
    to_a = jnp.where(is_even(slab_ref[0]), 1, 2)
    running = jnp.zeros((lines, lanes), F32)
    keys = []
    for block in range(blocks):
        cut = slice(block * lanes, (block + 1) * lanes)
        own = slice(block * lines, (block + 1) * lines)
        before = (counts[own, :lanes] + running) * hits[block]
        running = running + counts[own, lanes:]
        slot = jnp.sum(jnp.where(line < depths, before, 0.0), axis=0, keepdims=True).astype(jnp.int32)
        rank = jnp.sum(jnp.where(line < depths, 0.0, before), axis=0, keepdims=True).astype(jnp.int32)
        hop = route[:, cut] - me
        hop = jnp.where(hop < 0, hop + depths, hop)
        key = jnp.where(
            move[:, cut] == 0,
            hop * capacity + slot,
            depths * capacity + jnp.where(move[:, cut] == to_a, 0, MIG) + rank,
        )
        keys.append(jnp.where(death[:, cut] == 0, key, -1))
    key = jnp.concatenate(keys, axis=1)
    start = 0
    for index, out in enumerate(outs):
        size = capacity if index < depths else MIG
        chosen = (iota((size, agents), 0) == key - start).astype(F32).astype(BF16)
        placed = dot(chosen, updated, 1, 0).astype(BF16)
        start += size
        if index < depths:
            out[...] = placed
        else:
            tiles = out.shape[2] // width
            for i in range(MIG // 16):
                at = (i % tiles) * width
                out[i // tiles, :, at : at + width] = placed[i * 16 : (i + 1) * 16]


def third_sum(x):
    width = 128
    tiles = x.shape[1] // width
    lane = iota((x.shape[0], width), 1)
    parts = [x[:, i * width : (i + 1) * width] for i in range(tiles)]
    ups = [pltpu.roll(part, 1, 1) for part in parts]
    downs = [pltpu.roll(part, width - 1, 1) for part in parts]
    sums = []
    for i in range(tiles):
        before = ups[i - 1] if i else 0.0
        after = downs[i + 1] if i < tiles - 1 else 0.0
        sums.append(jnp.where(lane == 0, before, ups[i]) + jnp.where(lane == width - 1, after, downs[i]))
    return jnp.concatenate(sums, axis=1)


def neighbour_total(before, plane, after):
    rows = plane.shape[0]
    second = pltpu.roll(plane, 1, 0) + pltpu.roll(plane, rows - 1, 0)
    return before + after + second + third_sum(plane)


def relaxed(before, plane, after, target, centre):
    return (1.0 - DAMPING) * plane + (DAMPING / centre) * (
        target + neighbour_total(before, plane, after)
    )


def edge_mask(me, depths, halo):
    row = iota((2 * halo, 1), 0)
    return jnp.where(
        row < halo, (me < depths - 1).astype(F32), (me > 0).astype(F32)
    )


def masked(plane, own, mask):
    return jnp.concatenate([plane[:own], plane[own:] * mask], axis=0)


def halo_rows(side_a, side_b, even, plane, mask):
    at = 2 * HALO * (plane % 2)
    side_a = side_a[at : at + 2 * HALO].astype(F32)
    side_b = side_b[at : at + 2 * HALO].astype(F32)
    high = jnp.where(even, side_a, side_b)
    low = jnp.where(even, side_b, side_a)
    return (
        jnp.concatenate([high[:HALO], low[:HALO]], axis=0) * mask,
        jnp.concatenate([high[HALO:], low[HALO:]], axis=0),
    )


def corner_kernel(me_ref, slab_ref, side_a, side_b, in_a, in_b, slab_a, slab_b):
    layers = 2 * side_a.shape[0]
    nz = side_a.shape[2]
    own = slab_a.shape[0] - 2
    even = is_even(me_ref[0])
    slab_even = is_even(slab_ref[0])

    def layer(side, plane):
        at = 2 * HALO * (plane % 2)
        return side[plane // 2].astype(F32)[at : at + 2 * HALO]

    for index, (side, high) in enumerate(((side_a, even), (side_b, jnp.logical_not(even)))):
        for ref, front in ((slab_a, slab_even), (slab_b, jnp.logical_not(slab_even))):
            fields, targets = [], []
            for i in range(1, HALO):
                x = jnp.where(front, layer(side, layers - i), layer(side, i - 1))
                fields.append(jnp.where(high, x[: HALO - i], x[i:HALO]))
                if i < HALO - 1:
                    targets.append(
                        jnp.where(high, x[HALO : 2 * HALO - 1 - i], x[HALO + 1 + i :])
                    )
            rows = jnp.concatenate(fields + targets, axis=0)
            rest = jnp.zeros((16 - rows.shape[0], nz), F32)
            ref[own + index] = jnp.concatenate([rows, rest], axis=0).astype(BF16)


def corner_rows(block_a, block_b, even, mask):
    block_a, block_b = block_a.astype(F32), block_b.astype(F32)
    high = jnp.where(even, block_a, block_b)
    low = jnp.where(even, block_b, block_a)
    nz = high.shape[1]
    fields, targets = [], []
    at = 0
    for rows, out in ((HALO, fields), (HALO - 1, targets)):
        for i in range(1, rows):
            count = rows - i
            gap = jnp.zeros((2 * (HALO - count), nz), F32)
            cut = slice(at, at + count)
            out.append(jnp.concatenate([high[cut], gap, low[cut]], axis=0) * mask)
            at += count
    return fields, targets + [jnp.zeros_like(fields[0])]


KEEP, PULL = 1.0 - DAMPING, DAMPING / CENTRE


def inner_kernel(
    depths, me_ref, slab_ref, u_ref, t_ref, side_a, side_b, field_a, field_b, u0, text_ref, u1, u2_ref, inside
):
    nx, ny, nz = u_ref.shape
    even = is_even(me_ref[0])
    slab_even = is_even(slab_ref[0])
    half = ny // 16
    mask = edge_mask(me_ref[0], depths, HALO)
    for field, after in ((field_a, slab_even), (field_b, jnp.logical_not(slab_even))):
        u_at = jnp.where(after, HALO + nx, 0)
        for k in range(HALO):
            u0[u_at + k, :ny] = field[k * half : (k + 1) * half].astype(F32).reshape(ny, nz)
            u0[u_at + k, ny:] = jnp.zeros((2 * HALO, nz), F32)
    for plane in range(nx):
        u0[HALO + plane, :ny] = u_ref[plane]
        text_ref[HALO - 1 + plane, :ny] = t_ref[plane]
        uh, th = halo_rows(side_a[plane // 2], side_b[plane // 2], even, plane, mask)
        u0[HALO + plane, ny:] = uh
        text_ref[HALO - 1 + plane, ny:] = th

    def outer(i, carry):
        for p in (i, nx + HALO - 1 + i):
            u1[p] = KEEP * u0[p + 1] + PULL * neighbour_total(u0[p], u0[p + 1], u0[p + 2])
        return carry

    lax.fori_loop(0, HALO - 1, outer, 0)

    def first(p, carry):
        v = relaxed(u0[p], u0[p + 1], u0[p + 2], text_ref[p], CENTRE)
        u1[p] = masked(v, ny, mask)
        return carry

    lax.fori_loop(HALO - 1, nx + HALO - 1, first, 0)

    def second(p, carry):
        v = relaxed(u1[p], u1[p + 1], u1[p + 2], text_ref[p + 1], CENTRE)
        u2_ref[p] = masked(v, ny, mask)
        return carry

    lax.fori_loop(HALO - 1, nx + 1, second, 0)
    for p in range(2, nx - 2):
        inside[p - 2] = residual(u2_ref, text_ref, p, ny)


def residual(u2_ref, text_ref, p, ny):
    v = u2_ref[p + 2]
    total = neighbour_total(u2_ref[p + 1], v, u2_ref[p + 3])
    return (text_ref[p + 3] - CENTRE * v + total)[:ny]


def smooth_kernel(
    depths, me_ref, slab_ref, u0, text_in, u1_in, u2_in, inside, slab_a, slab_b,
    text_ref, u1, u2_ref, coarse_ref, coarse_all_ref, coarse_a, coarse_b, paired,
):
    nx = u0.shape[0] - 2 * HALO
    ny, nz = u0.shape[1] - 2 * HALO, u0.shape[2]
    mask = edge_mask(me_ref[0], depths, HALO)
    half = ny // 16
    own = (HALO - 1) * half
    even = is_even(me_ref[0])
    slab_even = is_even(slab_ref[0])
    row = iota((8, 1), 0)
    first, last = (row == 0).astype(F32), (row == 7).astype(F32)
    for ref, after in ((slab_a, slab_even), (slab_b, jnp.logical_not(slab_even))):
        fields, targets = corner_rows(ref[own], ref[own + 1], even, mask)
        sign = jnp.where(after, 1, -1)
        edge = jnp.where(after, nx - 1, 0)
        for i in range(1, HALO):
            p = edge + sign * i
            index = jnp.where(after, i - 1, HALO - 1 - i)
            t = ref[pl.ds(index * half, half)].astype(F32).reshape(ny, nz)
            text_ref[p + 3, :ny] = t
            text_ref[p + 3, ny:] = targets[i - 1]
            x = fields[i - 1]
            nearer = u0[p + 4 - sign, ny:] if i == 1 else fields[i - 2]
            total = nearer + third_sum(x)
            if i < HALO - 1:
                total = total + fields[i]
            beyond = u0[p + 4]
            up = jnp.where(row == 0, beyond[ny - 1 : ny], pltpu.roll(x, 1, 0))
            down = jnp.where(row == 7, beyond[0:1], pltpu.roll(x, 7, 0))
            u1[p + 3, ny:] = (KEEP * x + PULL * (targets[i - 1] + total + up + down)) * mask
            v = u1[p + 3, :ny] + PULL * t
            u1[p + 3, :ny] = v
            u1[p + 3, 0:8] = v[0:8] + (PULL * first) * x[7:8]
            u1[p + 3, ny - 8 : ny] = v[ny - 8 :] + (PULL * last) * x[0:1]
        u1[edge + 3, ny:] = u1[edge + 3, ny:] + PULL * fields[0]
        u2_ref[edge - sign + 2, ny:] = u2_ref[edge - sign + 2, ny:] + (PULL * PULL) * fields[0]

    def second(i, carry):
        for p in (i, nx + 1 + i):
            v = relaxed(u1[p], u1[p + 1], u1[p + 2], text_ref[p + 1], CENTRE)
            u2_ref[p] = masked(v, ny, mask)
        return carry

    lax.fori_loop(0, HALO - 1, second, 0)
    for q in range(nx // 2):
        both = 0.0
        for p in (2 * q, 2 * q + 1):
            known = 2 <= p < nx - 2
            both = both + (inside[p - 2] if known else residual(u2_ref, text_ref, p, ny))
        for i in range(nz // 128):
            paired[q, i] = both[:, i * 128 : (i + 1) * 128]
    cx, cy, cz = coarse_ref.shape
    flat = jnp.concatenate(
        [
            jnp.concatenate(
                [
                    paired[q, i, pl.ds(0, cy, 2), :] + paired[q, i, pl.ds(1, cy, 2), :]
                    for i in range(nz // 128)
                ],
                axis=1,
            )
            for q in range(cx)
        ],
        axis=0,
    )
    fold = ((iota((nz, cz), 0) >> 1) == iota((nz, cz), 1)).astype(F32).astype(BF16)
    high, low = halves(flat)
    coarse = 0.5 * (dot(high, fold, 1, 0) + dot(low, fold, 1, 0))
    coarse_ref[...] = coarse.reshape(cx, cy, cz)
    coarse_all_ref[...] = coarse.astype(BF16).reshape(cx, cy, cz)
    low, high = (
        jnp.concatenate([coarse_ref[q, start : start + HALO] for q in range(cx)], axis=0)
        for start in (0, cy - HALO)
    )
    coarse_a[0] = jnp.where(even, high, low).astype(BF16)
    coarse_b[0] = jnp.where(even, low, high).astype(BF16)


def post_kernel(depths, me_ref, u2_ref, text_ref, out_ref, v1):
    nx, ny, nz = out_ref.shape
    mask = edge_mask(me_ref[0], depths, HALO)

    def first(p, carry):
        v = relaxed(u2_ref[p], u2_ref[p + 1], u2_ref[p + 2], text_ref[p + 2], CENTRE)
        v1[p] = masked(v, ny, mask)
        return carry

    lax.fori_loop(0, nx + 2, first, 0)

    def second(p, carry):
        v = relaxed(v1[p], v1[p + 1], v1[p + 2], text_ref[p + 3], CENTRE)
        out_ref[p] = v[:ny]
        return carry

    lax.fori_loop(0, nx, second, 0)


def correct_kernel(
    depths, me_ref, slab_ref, ct_ref, side_a, side_b, slab_a, slab_b, base_ref, *rest
):
    packed = rest[:depths]
    out_ref, agents_ref, fine, sem = rest[depths:]
    nx, ny, nz = out_ref.shape
    cx, cy, cz = ct_ref.shape
    me = me_ref[0]
    even = is_even(me)
    slab_even = is_even(slab_ref[0])
    capacity = packed[0].shape[0]
    width = agents_ref.shape[1]
    copies = []
    for k in range(depths):
        origin = me - k
        origin = jnp.where(origin < 0, origin + depths, origin)
        place = pl.ds(pl.multiple_of(origin * capacity, capacity), capacity)
        copies.append(pltpu.make_async_copy(packed[k], agents_ref.at[place], sem.at[len(copies)]))
    tiles = cz // width
    for ref, late in ((slab_a, slab_even), (slab_b, jnp.logical_not(slab_even))):
        start = depths * capacity + jnp.where(late, MIG, 0)
        for i in range(MIG // 16):
            place = pl.ds(pl.multiple_of(start + i * 16, 16), 16)
            source = ref.at[cx + 2 + i // tiles, :, pl.ds((i % tiles) * width, width)]
            copies.append(pltpu.make_async_copy(source, agents_ref.at[place], sem.at[len(copies)]))
    for copy in copies:
        copy.start()
    mask = edge_mask(me, depths, HALO)

    def chosen(condition, x, y):
        return jnp.where(condition, x.astype(F32), y.astype(F32))

    planes = []
    for p in range(cx + 2 * HALO):
        if HALO <= p < HALO + cx:
            k = p - HALO
            own, one, two = ct_ref[k], side_a[0].astype(F32), side_b[0].astype(F32)
        else:
            before = p < HALO
            k = p + cx - HALO if before else p - HALO - cx
            x, y = (slab_b, slab_a) if before else (slab_a, slab_b)
            own, one, two = (chosen(slab_even, x[i], y[i]) for i in (k, cx, cx + 1))
        rows = slice(HALO * k, HALO * (k + 1))
        one, two = one[rows], two[rows]
        sides = jnp.concatenate([jnp.where(even, one, two), jnp.where(even, two, one)], axis=0)
        planes.append(jnp.concatenate([own, sides * mask], axis=0))
    values = [(DAMPING / COARSE_CENTRE) * plane for plane in planes]
    for sweep in range(1, HALO):
        values = [
            masked(
                relaxed(values[i - 1], values[i], values[i + 1], planes[i + sweep - 1], COARSE_CENTRE),
                cy,
                mask,
            )
            for i in range(1, len(values) - 1)
        ]
    wide = cy + 4
    for q, value in enumerate(values):
        value = jnp.concatenate([value[: cy + 2], value[cy + 2 * HALO - 2 :]], axis=0)
        for i in range(cz // 128):
            part = value[:, i * 128 : (i + 1) * 128]
            fine[q, i, pl.ds(0, wide, 2), :] = part
            fine[q, i, pl.ds(1, wide, 2), :] = part
    def second_total(plane):
        rows = plane.shape[0]
        return pltpu.roll(plane, 1, 0) + pltpu.roll(plane, rows - 1, 0)

    spread = [jnp.concatenate([fine[q, i] for i in range(cz // 128)], axis=1) for q in range(cx + 2)]
    still = [KEEP * plane + PULL * second_total(plane) for plane in spread]
    once = []
    for p in range(-1, nx + 1):
        q = (p + 2) // 2
        if p % 2 == 0:
            others = spread[q - 1] + spread[q]
        else:
            others = spread[q] + spread[q + 1]
        once.append(masked(still[q] + PULL * others, ny, mask))
    none, one, two = [], [], []
    for p in range(nx):
        plane = once[p + 1]
        total = once[p] + once[p + 2] + second_total(plane)
        none.append((KEEP * plane + PULL * total)[:ny])
        one.append(plane[:ny])
        two.append(spread[(p + 2) // 2][:ny])
    z = iota((cz, nz), 1)
    k = iota((cz, nz), 0)

    def hit(shift):
        moved = z + shift
        inside = jnp.logical_and(moved >= 0, moved < nz)
        return jnp.logical_and((moved >> 1) == k, inside).astype(F32)

    here, left, right = hit(0), hit(-1), hit(1)
    paths = jnp.where(jnp.logical_or(z == 0, z == nz - 1), here, 2.0 * here)
    spread_none = here.astype(BF16)
    spread_one = ((left + right) * 1.0).astype(BF16)
    spread_two = (hit(-2) + hit(2) + paths).astype(BF16)
    total = base_ref[...].reshape(nx * ny, nz)
    for parts, scale, matrix in (
        (none, 1.0, spread_none), (one, 2.0 * PULL, spread_one), (two, PULL * PULL, spread_two)
    ):
        high, low = halves(scale * jnp.concatenate(parts, axis=0))
        total = total + dot(high, matrix, 1, 0) + dot(low, matrix, 1, 0)
    out_ref[...] = total.reshape(nx, ny, nz)
    for copy in copies:
        copy.wait()


def local(
    nutrient, species, agent_cell, death_flag, divide_flag, slab_move, depth_route, net_weight, sensing, uptake_weight
):
    depths = lax.axis_size("depth")
    nx, ny, nz = nutrient.shape
    agents, width = species.shape
    capacity = 2 * agents // depths
    me = lax.axis_index("depth").astype(jnp.int32).reshape(1)
    slab = lax.axis_index("slab").astype(jnp.int32).reshape(1)
    shape = jax.ShapeDtypeStruct
    cells, death, divide = (x.reshape(1, agents) for x in (agent_cell, death_flag, divide_flag))
    move, route = slab_move.reshape(1, agents), depth_route.reshape(1, agents)
    half = ny // 16
    arguments = (
        nutrient, cells, species, uptake_weight.reshape(1, width), death, divide,
        move, route, net_weight, sensing.reshape(1, width),
    )
    loaded = pl.pallas_call(
        load_kernel,
        out_shape=tuple(shape(x.shape, x.dtype) for x in arguments)
        + tuple(shape((HALO * half, 16, nz), BF16) for _ in range(2)),
        in_specs=[SMEM_SPEC] + [HBM_SPEC] * len(arguments),
        out_specs=[VMEM_SPEC] * (len(arguments) + 2),
        scratch_shapes=[pltpu.SemaphoreType.DMA((len(arguments),))],
        compiler_params=PARAMS,
        name="load",
    )(slab, *(pltpu.with_memory_space_constraint(x, pltpu.HBM) for x in arguments))
    nutrient, cells, species, weight, death, divide, move, route, net_weight, sensing = loaded[:-2]
    target, sensed, depth_a, depth_b, slab_a, slab_b = pl.pallas_call(
        uptake_kernel,
        out_shape=(
            shape((nx, ny, nz), F32),
            shape((8, agents), F32),
            shape((nx // 2, 16, nz), BF16),
            shape((nx // 2, 16, nz), BF16),
            shape(((HALO - 1) * half + 2, 16, nz), BF16),
            shape(((HALO - 1) * half + 2, 16, nz), BF16),
        ),
        in_specs=[SMEM_SPEC] * 2 + [VMEM_SPEC] * 6,
        out_specs=[VMEM_SPEC] * 6,
        compiler_params=PARAMS,
        name="uptake",
    )(me, slab, nutrient, cells, death, divide, species, weight)
    field_a, field_b, depth_a, depth_b = lax.optimization_barrier(
        (loaded[-2], loaded[-1], depth_a, depth_b)
    )
    side_a = swapped(depth_a, "depth", "a")
    side_b = swapped(depth_b, "depth", "b")
    field_a = swapped(field_a, "slab", "a")
    field_b = swapped(field_b, "slab", "b")
    slab_a, slab_b = pl.pallas_call(
        corner_kernel,
        out_shape=tuple(shape(x.shape, BF16) for x in (slab_a, slab_b)),
        in_specs=[SMEM_SPEC] * 2 + [VMEM_SPEC] * 4,
        out_specs=[VMEM_SPEC] * 2,
        input_output_aliases={4: 0, 5: 1},
        compiler_params=PARAMS,
        name="corner",
    )(me, slab, side_a, side_b, slab_a, slab_b)
    slab_a = swapped(slab_a, "slab", "a")
    slab_b = swapped(slab_b, "slab", "b")
    cx, cy, cz = nx // 2, ny // 2, nz // 2
    ext = ny + 2 * HALO
    sent = pl.pallas_call(
        network_kernel,
        out_shape=tuple(shape((capacity, width), BF16) for _ in range(depths))
        + tuple(shape((MIG * width // (16 * cz), 16, cz), BF16) for _ in range(2)),
        in_specs=[SMEM_SPEC] * 2 + [VMEM_SPEC] * 7,
        out_specs=[VMEM_SPEC] * (depths + 2),
        compiler_params=PARAMS,
        cost_estimate=pl.CostEstimate(
            flops=2 * 2304 * agents * width, bytes_accessed=1 << 20, transcendentals=agents * width
        ),
        name="network",
    )(me, slab, species, sensed, death, move, route, net_weight, sensing)
    u0, text, u1, u2, inside = pl.pallas_call(
        functools.partial(inner_kernel, depths),
        out_shape=(
            shape((nx + 2 * HALO, ext, nz), F32),
            shape((nx + 2 * HALO - 2, ext, nz), F32),
            shape((nx + 2 * HALO - 2, ext, nz), F32),
            shape((nx + 4, ext, nz), F32),
            shape((nx - 4, ny, nz), F32),
        ),
        in_specs=[SMEM_SPEC] * 2 + [VMEM_SPEC] * 6,
        out_specs=[VMEM_SPEC] * 5,
        compiler_params=PARAMS,
        cost_estimate=pl.CostEstimate(flops=1 << 30, bytes_accessed=1 << 22, transcendentals=0),
        name="inner",
    )(me, slab, nutrient, target, side_a, side_b, field_a, field_b)
    slab_a, slab_b, *sent = lax.optimization_barrier((slab_a, slab_b, *sent))
    text, _, u2, ct, ct_all, coarse_a, coarse_b = pl.pallas_call(
        functools.partial(smooth_kernel, depths),
        out_shape=(
            shape(text.shape, F32),
            shape(u1.shape, F32),
            shape(u2.shape, F32),
            shape((cx, cy, cz), F32),
            shape((cx, cy, cz), BF16),
            shape((1, cx * HALO, cz), BF16),
            shape((1, cx * HALO, cz), BF16),
        ),
        in_specs=[SMEM_SPEC] * 2 + [VMEM_SPEC] * 7,
        out_specs=[VMEM_SPEC] * 7,
        scratch_shapes=[pltpu.VMEM((cx, nz // 128, ny, 128), F32)],
        input_output_aliases={3: 0, 4: 1, 5: 2},
        compiler_params=PARAMS,
        name="smooth",
    )(me, slab, u0, text, u1, u2, inside, slab_a, slab_b)
    arrived = [sent[0]] + [cyclic(sent[k], "depth", k) for k in range(1, depths)]
    coarse_a = swapped(coarse_a, "depth", "a")
    coarse_b = swapped(coarse_b, "depth", "b")
    tail_a, tail_b = (
        swapped(jnp.concatenate([ct_all, coarse_a, coarse_b, movers], axis=0), "slab", which)
        for which, movers in (("a", sent[depths]), ("b", sent[depths + 1]))
    )
    base = pl.pallas_call(
        functools.partial(post_kernel, depths),
        out_shape=shape((nx, ny, nz), F32),
        in_specs=[SMEM_SPEC] + [VMEM_SPEC] * 2,
        out_specs=VMEM_SPEC,
        scratch_shapes=[pltpu.VMEM((nx + 2, ext, nz), F32)],
        compiler_params=PARAMS,
        cost_estimate=pl.CostEstimate(flops=1 << 30, bytes_accessed=1 << 22, transcendentals=0),
        name="post",
    )(me, u2, text)
    return pl.pallas_call(
        functools.partial(correct_kernel, depths),
        out_shape=(
            shape((nx, ny, nz), F32),
            shape((depths * capacity + 2 * MIG, width), BF16),
        ),
        in_specs=[SMEM_SPEC] * 2 + [VMEM_SPEC] * 6 + [ANY_SPEC] * depths,
        out_specs=[VMEM_SPEC, ANY_SPEC],
        scratch_shapes=[
            pltpu.VMEM((cx + 2, cz // 128, ext, 128), F32),
            pltpu.SemaphoreType.DMA((depths + 2 * (MIG // 16),)),
        ],
        compiler_params=PARAMS,
        name="correct",
    )(me, slab, ct, coarse_a, coarse_b, tail_a, tail_b, base, *arrived)


def solution(mesh):
    rows = P(("slab", "depth"))
    in_specs = (
        P("slab", "depth", None),
        P(("slab", "depth"), None),
        rows,
        rows,
        rows,
        rows,
        P(("slab", "depth"), None),
        P(),
        P(),
        P(),
    )
    out_specs = (P("slab", "depth", None), P(("slab", "depth"), None))
    return jax.shard_map(local, mesh=mesh, in_specs=in_specs, out_specs=out_specs, check_vma=False)
```

```python
import functools

import jax
import jax.numpy as jnp
from jax import lax
from jax.experimental import pallas as pl
from jax.experimental.pallas import tpu as pltpu
from jax.sharding import PartitionSpec as P

MIG = 128
SCREENING = 0.05
DAMPING = 2.0 / 3.0
CENTRE = 6.0 + SCREENING
COARSE_CENTRE = 6.0 + 4.0 * SCREENING
HALO = 4
F32, BF16 = jnp.float32, jnp.bfloat16
VMEM_SPEC = pl.BlockSpec(memory_space=pltpu.VMEM)
ANY_SPEC = pl.BlockSpec(memory_space=pl.ANY)
HBM_SPEC = pl.BlockSpec(memory_space=pltpu.HBM)
SMEM_SPEC = pl.BlockSpec(memory_space=pltpu.SMEM)
PARAMS = pltpu.CompilerParams(vmem_limit_bytes=40 * 1024 * 1024)


def dot(a, b, ca, cb):
    return lax.dot_general(a, b, (((ca,), (cb,)), ((), ())), preferred_element_type=F32)


def halves(x):
    high = x.astype(BF16)
    return high, (x - high.astype(F32)).astype(BF16)


def iota(shape, dim):
    return lax.broadcasted_iota(jnp.int32, shape, dim)


def cyclic(x, axis, by):
    count = lax.axis_size(axis)
    return lax.ppermute(x, axis, [(i, (i + by) % count) for i in range(count)])


def swapped(x, axis, which):
    count = lax.axis_size(axis)
    if count % 2:
        raise ValueError("odd axis")
    first = 0 if which == "a" else 1
    pairs = []
    for i in range(first, count, 2):
        j = (i + 1) % count
        pairs += [(i, j), (j, i)]
    return lax.ppermute(x, axis, sorted(pairs))


def is_even(x):
    return lax.rem(x, 2) == 0


def load_kernel(slab_ref, *refs):
    count = (len(refs) - 3) // 2
    sources, targets = refs[:count], refs[count : 2 * count]
    slab_a, slab_b, sem = refs[2 * count :]
    copies = [
        pltpu.make_async_copy(source, target, sem.at[i])
        for i, (source, target) in enumerate(zip(sources, targets))
    ]
    for copy in copies:
        copy.start()
    copies[0].wait()
    u_ref = targets[0]
    nx, ny, nz = u_ref.shape
    half = ny // 16
    even = is_even(slab_ref[0])
    for ref, front in ((slab_a, even), (slab_b, jnp.logical_not(even))):
        start = jnp.where(front, nx - HALO, 0)
        for k in range(HALO):
            ref[k * half : (k + 1) * half] = u_ref[start + k].astype(BF16).reshape(half, 16, nz)
    for copy in copies[1:]:
        copy.wait()


def uptake_kernel(
    me_ref, u_ref, cell_ref, death_ref, divide_ref, species_ref, weight_ref,
    t_ref, sensed_ref, depth_a, depth_b, list_ref,
):
    nx, ny, nz = u_ref.shape
    agents = species_ref.shape[0]
    rows = nx * ny
    u = u_ref[...].reshape(rows, nz)
    cell = cell_ref[...].reshape(1, agents)
    cell_row = cell // nz
    cell_z = cell - cell_row * nz
    one_z = (iota((nz, agents), 0) == cell_z).astype(F32).astype(BF16)
    in_row = iota((rows, agents), 0) == cell_row
    high, low = halves(u)
    picked = dot(high, one_z, 1, 0) + dot(low, one_z, 1, 0)
    sample = jnp.sum(jnp.where(in_row, picked, 0.0), axis=0, keepdims=True)
    sensed_ref[...] = jnp.broadcast_to(sample, (8, agents)).astype(BF16).astype(F32)
    weight = jnp.broadcast_to(weight_ref[...].reshape(1, -1), (8, species_ref.shape[1]))
    score = dot(weight, species_ref[...], 1, 1)[0:1]
    softplus = jnp.maximum(score, 0.0) + jnp.log1p(jnp.exp(-jnp.abs(score)))
    alive = (1 - death_ref[...].reshape(1, agents)).astype(F32)
    divide = divide_ref[...].reshape(1, agents).astype(F32)
    uptake = alive * (1.0 + divide) * softplus * sample / (0.5 + sample)
    up_high = uptake.astype(BF16).astype(F32)
    a_high = jnp.where(in_row, up_high, 0.0).astype(BF16)
    a_low = jnp.where(in_row, uptake - up_high, 0.0).astype(BF16)
    source = dot(a_high, one_z, 1, 1) + dot(a_low, one_z, 1, 1)
    t_ref[...] = (SCREENING * u - source).reshape(nx, ny, nz)
    even = is_even(me_ref[0])
    for pair in range(nx // 2):
        parts = []
        for start in (0, ny - HALO):
            for plane in (2 * pair, 2 * pair + 1):
                parts.append(u_ref[plane, start : start + HALO])
                parts.append(t_ref[plane, start : start + HALO])
        low = jnp.concatenate(parts[:4], axis=0)
        high = jnp.concatenate(parts[4:], axis=0)
        depth_a[pair] = jnp.where(even, high, low).astype(BF16)
        depth_b[pair] = jnp.where(even, low, high).astype(BF16)
    half_z = cell_z // 2
    values = (cell_row.astype(F32), half_z.astype(F32), (cell_z - 2 * half_z).astype(F32), up_high)
    list_ref[...] = jnp.concatenate(
        [x[:, i * nz : (i + 1) * nz] for x in values for i in range(agents // nz)], axis=0
    )


def network_kernel(
    me_ref, slab_ref, species_ref, sensed_ref, death_ref, move_ref, route_ref, net_ref, sensing_ref, *outs
):
    agents, width = species_ref.shape
    depths = len(outs) - 2
    capacity = outs[0].shape[0]
    species = species_ref[...]
    sensing = sensing_ref[...].reshape(1, width)
    first = sensing.astype(BF16)
    rest = sensing - first.astype(F32)
    second = rest.astype(BF16)
    third = (rest - second.astype(F32)).astype(BF16)
    line = iota((8, width), 0)
    terms = jnp.where(
        line == 0, first.astype(F32),
        jnp.where(line == 1, second.astype(F32), jnp.where(line == 2, third.astype(F32), 0.0)),
    ).astype(BF16)
    activation = dot(species, net_ref[...], 1, 0) + dot(sensed_ref[...].astype(BF16), terms, 0, 0)
    updated = (0.5 * species.astype(F32) + jnp.tanh(activation)).astype(BF16)
    lanes = 128
    lines = -(-(depths + 2) // 8) * 8
    line = iota((lines, lanes), 0)
    square = iota((lanes, 2 * lanes), 0)
    column = iota((lanes, 2 * lanes), 1)
    counter = jnp.where(jnp.logical_or(column >= lanes, square < column), 1.0, 0.0).astype(BF16)
    blocks = agents // lanes
    route = route_ref[...].reshape(1, agents)
    move = move_ref[...].reshape(1, agents)
    death = death_ref[...].reshape(1, agents)
    hits = []
    for block in range(blocks):
        cut = slice(block * lanes, (block + 1) * lanes)
        wanted = jnp.where(line < depths, route[:, cut], jnp.where(line < depths + 2, move[:, cut] + (depths - 1), -1))
        hits.append((wanted == line).astype(F32))
    counts = dot(jnp.concatenate(hits, axis=0).astype(BF16), counter, 1, 0)
    me = me_ref[0]
    to_a = jnp.where(is_even(slab_ref[0]), 1, 2)
    running = jnp.zeros((lines, lanes), F32)
    keys = []
    for block in range(blocks):
        cut = slice(block * lanes, (block + 1) * lanes)
        own = slice(block * lines, (block + 1) * lines)
        before = (counts[own, :lanes] + running) * hits[block]
        running = running + counts[own, lanes:]
        slot = jnp.sum(jnp.where(line < depths, before, 0.0), axis=0, keepdims=True).astype(jnp.int32)
        rank = jnp.sum(jnp.where(line < depths, 0.0, before), axis=0, keepdims=True).astype(jnp.int32)
        hop = route[:, cut] - me
        hop = jnp.where(hop < 0, hop + depths, hop)
        key = jnp.where(
            move[:, cut] == 0,
            hop * capacity + slot,
            depths * capacity + jnp.where(move[:, cut] == to_a, 0, MIG) + rank,
        )
        keys.append(jnp.where(death[:, cut] == 0, key, -1))
    key = jnp.concatenate(keys, axis=1)
    start = 0
    for index, out in enumerate(outs):
        size = capacity if index < depths else MIG
        chosen = (iota((size, agents), 0) == key - start).astype(F32).astype(BF16)
        placed = dot(chosen, updated, 1, 0).astype(BF16)
        start += size
        if index < depths:
            out[...] = placed
        else:
            tiles = out.shape[2] // width
            for i in range(MIG // 16):
                at = (i % tiles) * width
                out[i // tiles, :, at : at + width] = placed[i * 16 : (i + 1) * 16]


def third_sum(x):
    width = 128
    tiles = x.shape[1] // width
    lane = iota((x.shape[0], width), 1)
    parts = [x[:, i * width : (i + 1) * width] for i in range(tiles)]
    ups = [pltpu.roll(part, 1, 1) for part in parts]
    downs = [pltpu.roll(part, width - 1, 1) for part in parts]
    sums = []
    for i in range(tiles):
        before = ups[i - 1] if i else 0.0
        after = downs[i + 1] if i < tiles - 1 else 0.0
        sums.append(jnp.where(lane == 0, before, ups[i]) + jnp.where(lane == width - 1, after, downs[i]))
    return jnp.concatenate(sums, axis=1)


def neighbour_total(before, plane, after):
    rows = plane.shape[0]
    second = pltpu.roll(plane, 1, 0) + pltpu.roll(plane, rows - 1, 0)
    return before + after + second + third_sum(plane)


def relaxed(before, plane, after, target, centre):
    return (1.0 - DAMPING) * plane + (DAMPING / centre) * (
        target + neighbour_total(before, plane, after)
    )


def edge_mask(me, depths, halo):
    row = iota((2 * halo, 1), 0)
    return jnp.where(
        row < halo, (me < depths - 1).astype(F32), (me > 0).astype(F32)
    )


def masked(plane, own, mask):
    return jnp.concatenate([plane[:own], plane[own:] * mask], axis=0)


def halo_rows(side_a, side_b, even, plane, mask):
    at = 2 * HALO * (plane % 2)
    side_a = side_a[at : at + 2 * HALO].astype(F32)
    side_b = side_b[at : at + 2 * HALO].astype(F32)
    high = jnp.where(even, side_a, side_b)
    low = jnp.where(even, side_b, side_a)
    return (
        jnp.concatenate([high[:HALO], low[:HALO]], axis=0) * mask,
        jnp.concatenate([high[HALO:], low[HALO:]], axis=0),
    )


def corner_kernel(me_ref, slab_ref, side_a, side_b, list_ref, slab_a, slab_b):
    layers = 2 * side_a.shape[0]
    nz = side_a.shape[2]
    even = is_even(me_ref[0])
    slab_even = is_even(slab_ref[0])

    def layer(side, plane):
        at = 2 * HALO * (plane % 2)
        return side[plane // 2].astype(F32)[at : at + 2 * HALO]

    for ref, front in ((slab_a, slab_even), (slab_b, jnp.logical_not(slab_even))):
        parts = []
        for side, high in ((side_a, even), (side_b, jnp.logical_not(even))):
            targets = []
            for i in range(1, HALO):
                x = jnp.where(front, layer(side, layers - i), layer(side, i - 1))
                parts.append(jnp.where(high, x[: HALO - i], x[i:HALO]))
                if i < HALO - 1:
                    targets.append(
                        jnp.where(high, x[HALO : 2 * HALO - 1 - i], x[HALO + 1 + i :])
                    )
            parts += targets
        parts.append(list_ref[...])
        used = sum(part.shape[0] for part in parts)
        total = ref.shape[0] * ref.shape[1]
        parts.append(jnp.zeros((total - used, nz), F32))
        ref[...] = jnp.concatenate(parts, axis=0).astype(BF16).reshape(ref.shape)


def corner_rows(block_a, block_b, even, mask):
    high = jnp.where(even, block_a, block_b)
    low = jnp.where(even, block_b, block_a)
    nz = high.shape[1]
    fields, targets = [], []
    at = 0
    for rows, out in ((HALO, fields), (HALO - 1, targets)):
        for i in range(1, rows):
            count = rows - i
            gap = jnp.zeros((2 * (HALO - count), nz), F32)
            cut = slice(at, at + count)
            out.append(jnp.concatenate([high[cut], gap, low[cut]], axis=0) * mask)
            at += count
    return fields, targets + [jnp.zeros_like(fields[0])]


KEEP, PULL = 1.0 - DAMPING, DAMPING / CENTRE


def inner_kernel(
    depths, me_ref, slab_ref, u_ref, t_ref, side_a, side_b, field_a, field_b, u0, text_ref, u1, u2_ref, inside
):
    nx, ny, nz = u_ref.shape
    even = is_even(me_ref[0])
    slab_even = is_even(slab_ref[0])
    half = ny // 16
    mask = edge_mask(me_ref[0], depths, HALO)
    for field, after in ((field_a, slab_even), (field_b, jnp.logical_not(slab_even))):
        u_at = jnp.where(after, HALO + nx, 0)
        for k in range(HALO):
            u0[u_at + k, :ny] = field[k * half : (k + 1) * half].astype(F32).reshape(ny, nz)
            u0[u_at + k, ny:] = jnp.zeros((2 * HALO, nz), F32)
    for plane in range(nx):
        u0[HALO + plane, :ny] = u_ref[plane]
        text_ref[HALO - 1 + plane, :ny] = t_ref[plane]
        uh, th = halo_rows(side_a[plane // 2], side_b[plane // 2], even, plane, mask)
        u0[HALO + plane, ny:] = uh
        text_ref[HALO - 1 + plane, ny:] = th

    def outer(i, carry):
        for p in (i, nx + HALO - 1 + i):
            u1[p] = KEEP * u0[p + 1] + PULL * neighbour_total(u0[p], u0[p + 1], u0[p + 2])
        return carry

    lax.fori_loop(0, HALO - 1, outer, 0)

    def first(p, carry):
        v = relaxed(u0[p], u0[p + 1], u0[p + 2], text_ref[p], CENTRE)
        u1[p] = masked(v, ny, mask)
        return carry

    lax.fori_loop(HALO - 1, nx + HALO - 1, first, 0)

    def second(p, carry):
        v = relaxed(u1[p], u1[p + 1], u1[p + 2], text_ref[p + 1], CENTRE)
        u2_ref[p] = masked(v, ny, mask)
        return carry

    lax.fori_loop(HALO - 1, nx + 1, second, 0)
    for p in range(2, nx - 2):
        inside[p - 2] = residual(u2_ref, text_ref, p, ny)


def residual(u2_ref, text_ref, p, ny):
    v = u2_ref[p + 2]
    total = neighbour_total(u2_ref[p + 1], v, u2_ref[p + 3])
    return (text_ref[p + 3] - CENTRE * v + total)[:ny]


def smooth_kernel(
    depths, agents, me_ref, slab_ref, u0, text_in, u1_in, u2_in, inside, slab_a, slab_b,
    text_ref, u1, u2_ref, coarse_ref, coarse_all_ref, coarse_a, coarse_b, paired, foreign,
):
    nx = u0.shape[0] - 2 * HALO
    ny, nz = u0.shape[1] - 2 * HALO, u0.shape[2]
    mask = edge_mask(me_ref[0], depths, HALO)
    even = is_even(me_ref[0])
    slab_even = is_even(slab_ref[0])
    near = HALO - 1
    corner = HALO * near // 2 + near * (near - 1) // 2
    row = iota((8, 1), 0)
    first, last = (row == 0).astype(F32), (row == 7).astype(F32)
    for ref, after in ((slab_a, slab_even), (slab_b, jnp.logical_not(slab_even))):
        message = ref[...].astype(F32).reshape(-1, nz)
        fields, targets = corner_rows(message[:corner], message[corner : 2 * corner], even, mask)
        sign = jnp.where(after, 1, -1)
        edge = jnp.where(after, nx - 1, 0)
        lines = agents // nz
        cell_row, half_z, bit, uptake = (
            jnp.concatenate([message[at + i : at + i + 1] for i in range(lines)], axis=1)
            for at in range(2 * corner, 2 * corner + 4 * lines, lines)
        )
        cell_row = cell_row.astype(jnp.int32) - jnp.where(after, 0, (nx - near) * ny)
        cell_z = (2.0 * half_z + bit).astype(jnp.int32)
        one_z = (iota((nz, agents), 0) == cell_z).astype(F32).astype(BF16)
        taken = jnp.where(iota((near * ny, agents), 0) == cell_row, uptake, 0.0).astype(BF16)
        foreign[...] = dot(taken, one_z, 1, 1)
        for i in range(1, HALO):
            p = edge + sign * i
            index = jnp.where(after, i - 1, HALO - 1 - i)
            t = SCREENING * u0[p + 4, :ny] - foreign[pl.ds(index * ny, ny)]
            text_ref[p + 3, :ny] = t
            text_ref[p + 3, ny:] = targets[i - 1]
            x = fields[i - 1]
            nearer = u0[p + 4 - sign, ny:] if i == 1 else fields[i - 2]
            total = nearer + third_sum(x)
            if i < HALO - 1:
                total = total + fields[i]
            beyond = u0[p + 4]
            up = jnp.where(row == 0, beyond[ny - 1 : ny], pltpu.roll(x, 1, 0))
            down = jnp.where(row == 7, beyond[0:1], pltpu.roll(x, 7, 0))
            u1[p + 3, ny:] = (KEEP * x + PULL * (targets[i - 1] + total + up + down)) * mask
            v = u1[p + 3, :ny] + PULL * t
            u1[p + 3, :ny] = v
            u1[p + 3, 0:8] = v[0:8] + (PULL * first) * x[7:8]
            u1[p + 3, ny - 8 : ny] = v[ny - 8 :] + (PULL * last) * x[0:1]
        u1[edge + 3, ny:] = u1[edge + 3, ny:] + PULL * fields[0]
        u2_ref[edge - sign + 2, ny:] = u2_ref[edge - sign + 2, ny:] + (PULL * PULL) * fields[0]

    def second(i, carry):
        for p in (i, nx + 1 + i):
            v = relaxed(u1[p], u1[p + 1], u1[p + 2], text_ref[p + 1], CENTRE)
            u2_ref[p] = masked(v, ny, mask)
        return carry

    lax.fori_loop(0, HALO - 1, second, 0)
    for q in range(nx // 2):
        both = 0.0
        for p in (2 * q, 2 * q + 1):
            known = 2 <= p < nx - 2
            both = both + (inside[p - 2] if known else residual(u2_ref, text_ref, p, ny))
        for i in range(nz // 128):
            paired[q, i] = both[:, i * 128 : (i + 1) * 128]
    cx, cy, cz = coarse_ref.shape
    flat = jnp.concatenate(
        [
            jnp.concatenate(
                [
                    paired[q, i, pl.ds(0, cy, 2), :] + paired[q, i, pl.ds(1, cy, 2), :]
                    for i in range(nz // 128)
                ],
                axis=1,
            )
            for q in range(cx)
        ],
        axis=0,
    )
    fold = ((iota((nz, cz), 0) >> 1) == iota((nz, cz), 1)).astype(F32).astype(BF16)
    high, low = halves(flat)
    coarse = 0.5 * (dot(high, fold, 1, 0) + dot(low, fold, 1, 0))
    coarse_ref[...] = coarse.reshape(cx, cy, cz)
    coarse_all_ref[...] = coarse.astype(BF16).reshape(cx, cy, cz)
    low, high = (
        jnp.concatenate([coarse_ref[q, start : start + HALO] for q in range(cx)], axis=0)
        for start in (0, cy - HALO)
    )
    coarse_a[0] = jnp.where(even, high, low).astype(BF16)
    coarse_b[0] = jnp.where(even, low, high).astype(BF16)


def post_kernel(depths, me_ref, u2_ref, text_ref, out_ref, v1):
    nx, ny, nz = out_ref.shape
    mask = edge_mask(me_ref[0], depths, HALO)

    def first(p, carry):
        v = relaxed(u2_ref[p], u2_ref[p + 1], u2_ref[p + 2], text_ref[p + 2], CENTRE)
        v1[p] = masked(v, ny, mask)
        return carry

    lax.fori_loop(0, nx + 2, first, 0)

    def second(p, carry):
        v = relaxed(v1[p], v1[p + 1], v1[p + 2], text_ref[p + 3], CENTRE)
        out_ref[p] = v[:ny]
        return carry

    lax.fori_loop(0, nx, second, 0)


def correct_kernel(
    depths, me_ref, slab_ref, ct_ref, side_a, side_b, slab_a, slab_b, base_ref, *rest
):
    packed = rest[:depths]
    out_ref, agents_ref, fine, sem = rest[depths:]
    nx, ny, nz = out_ref.shape
    cx, cy, cz = ct_ref.shape
    me = me_ref[0]
    even = is_even(me)
    slab_even = is_even(slab_ref[0])
    capacity = packed[0].shape[0]
    width = agents_ref.shape[1]
    copies = []
    for k in range(depths):
        origin = me - k
        origin = jnp.where(origin < 0, origin + depths, origin)
        place = pl.ds(pl.multiple_of(origin * capacity, capacity), capacity)
        copies.append(pltpu.make_async_copy(packed[k], agents_ref.at[place], sem.at[len(copies)]))
    tiles = cz // width
    for ref, late in ((slab_a, slab_even), (slab_b, jnp.logical_not(slab_even))):
        start = depths * capacity + jnp.where(late, MIG, 0)
        for i in range(MIG // 16):
            place = pl.ds(pl.multiple_of(start + i * 16, 16), 16)
            source = ref.at[cx + 2 + i // tiles, :, pl.ds((i % tiles) * width, width)]
            copies.append(pltpu.make_async_copy(source, agents_ref.at[place], sem.at[len(copies)]))
    for copy in copies:
        copy.start()
    mask = edge_mask(me, depths, HALO)

    def chosen(condition, x, y):
        return jnp.where(condition, x.astype(F32), y.astype(F32))

    planes = []
    for p in range(cx + 2 * HALO):
        if HALO <= p < HALO + cx:
            k = p - HALO
            own, one, two = ct_ref[k], side_a[0].astype(F32), side_b[0].astype(F32)
        else:
            before = p < HALO
            k = p + cx - HALO if before else p - HALO - cx
            x, y = (slab_b, slab_a) if before else (slab_a, slab_b)
            own, one, two = (chosen(slab_even, x[i], y[i]) for i in (k, cx, cx + 1))
        rows = slice(HALO * k, HALO * (k + 1))
        one, two = one[rows], two[rows]
        sides = jnp.concatenate([jnp.where(even, one, two), jnp.where(even, two, one)], axis=0)
        planes.append(jnp.concatenate([own, sides * mask], axis=0))
    values = [(DAMPING / COARSE_CENTRE) * plane for plane in planes]
    for sweep in range(1, HALO):
        values = [
            masked(
                relaxed(values[i - 1], values[i], values[i + 1], planes[i + sweep - 1], COARSE_CENTRE),
                cy,
                mask,
            )
            for i in range(1, len(values) - 1)
        ]
    wide = cy + 4
    for q, value in enumerate(values):
        value = jnp.concatenate([value[: cy + 2], value[cy + 2 * HALO - 2 :]], axis=0)
        for i in range(cz // 128):
            part = value[:, i * 128 : (i + 1) * 128]
            fine[q, i, pl.ds(0, wide, 2), :] = part
            fine[q, i, pl.ds(1, wide, 2), :] = part
    def second_total(plane):
        rows = plane.shape[0]
        return pltpu.roll(plane, 1, 0) + pltpu.roll(plane, rows - 1, 0)

    spread = [jnp.concatenate([fine[q, i] for i in range(cz // 128)], axis=1) for q in range(cx + 2)]
    still = [KEEP * plane + PULL * second_total(plane) for plane in spread]
    once = []
    for p in range(-1, nx + 1):
        q = (p + 2) // 2
        if p % 2 == 0:
            others = spread[q - 1] + spread[q]
        else:
            others = spread[q] + spread[q + 1]
        once.append(masked(still[q] + PULL * others, ny, mask))
    none, one, two = [], [], []
    for p in range(nx):
        plane = once[p + 1]
        total = once[p] + once[p + 2] + second_total(plane)
        none.append((KEEP * plane + PULL * total)[:ny])
        one.append(plane[:ny])
        two.append(spread[(p + 2) // 2][:ny])
    z = iota((cz, nz), 1)
    k = iota((cz, nz), 0)

    def hit(shift):
        moved = z + shift
        inside = jnp.logical_and(moved >= 0, moved < nz)
        return jnp.logical_and((moved >> 1) == k, inside).astype(F32)

    here, left, right = hit(0), hit(-1), hit(1)
    paths = jnp.where(jnp.logical_or(z == 0, z == nz - 1), here, 2.0 * here)
    spread_none = here.astype(BF16)
    spread_one = ((left + right) * 1.0).astype(BF16)
    spread_two = (hit(-2) + hit(2) + paths).astype(BF16)
    total = base_ref[...].reshape(nx * ny, nz)
    for parts, scale, matrix in (
        (none, 1.0, spread_none), (one, 2.0 * PULL, spread_one), (two, PULL * PULL, spread_two)
    ):
        high, low = halves(scale * jnp.concatenate(parts, axis=0))
        total = total + dot(high, matrix, 1, 0) + dot(low, matrix, 1, 0)
    out_ref[...] = total.reshape(nx, ny, nz)
    for copy in copies:
        copy.wait()


def local(
    nutrient, species, agent_cell, death_flag, divide_flag, slab_move, depth_route, net_weight, sensing, uptake_weight
):
    depths = lax.axis_size("depth")
    nx, ny, nz = nutrient.shape
    agents, width = species.shape
    capacity = 2 * agents // depths
    me = lax.axis_index("depth").astype(jnp.int32).reshape(1)
    slab = lax.axis_index("slab").astype(jnp.int32).reshape(1)
    shape = jax.ShapeDtypeStruct
    cells, death, divide = (x.reshape(1, agents) for x in (agent_cell, death_flag, divide_flag))
    move, route = slab_move.reshape(1, agents), depth_route.reshape(1, agents)
    half = ny // 16
    if agents % nz or nx * ny > 256 or nz > 512:
        raise ValueError("list digits")
    arguments = (
        nutrient, cells, species, uptake_weight.reshape(1, width), death, divide,
        move, route, net_weight, sensing.reshape(1, width),
    )
    loaded = pl.pallas_call(
        load_kernel,
        out_shape=tuple(shape(x.shape, x.dtype) for x in arguments)
        + tuple(shape((HALO * half, 16, nz), BF16) for _ in range(2)),
        in_specs=[SMEM_SPEC] + [HBM_SPEC] * len(arguments),
        out_specs=[VMEM_SPEC] * (len(arguments) + 2),
        scratch_shapes=[pltpu.SemaphoreType.DMA((len(arguments),))],
        compiler_params=PARAMS,
        name="load",
    )(slab, *(pltpu.with_memory_space_constraint(x, pltpu.HBM) for x in arguments))
    nutrient, cells, species, weight, death, divide, move, route, net_weight, sensing = loaded[:-2]
    target, sensed, depth_a, depth_b, agent_list = pl.pallas_call(
        uptake_kernel,
        out_shape=(
            shape((nx, ny, nz), F32),
            shape((8, agents), F32),
            shape((nx // 2, 16, nz), BF16),
            shape((nx // 2, 16, nz), BF16),
            shape((4 * agents // nz, nz), F32),
        ),
        in_specs=[SMEM_SPEC] + [VMEM_SPEC] * 6,
        out_specs=[VMEM_SPEC] * 5,
        compiler_params=PARAMS,
        name="uptake",
    )(me, nutrient, cells, death, divide, species, weight)
    field_a, field_b, depth_a, depth_b = lax.optimization_barrier(
        (loaded[-2], loaded[-1], depth_a, depth_b)
    )
    side_a = swapped(depth_a, "depth", "a")
    side_b = swapped(depth_b, "depth", "b")
    field_a = swapped(field_a, "slab", "a")
    field_b = swapped(field_b, "slab", "b")
    rows = 2 * (HALO - 1) ** 2 + agent_list.shape[0]
    rows = -(-rows // 16) * 16
    slab_a, slab_b = pl.pallas_call(
        corner_kernel,
        out_shape=tuple(shape((rows // 16, 16, nz), BF16) for _ in range(2)),
        in_specs=[SMEM_SPEC] * 2 + [VMEM_SPEC] * 3,
        out_specs=[VMEM_SPEC] * 2,
        compiler_params=PARAMS,
        name="corner",
    )(me, slab, side_a, side_b, agent_list)
    slab_a = swapped(slab_a, "slab", "a")
    slab_b = swapped(slab_b, "slab", "b")
    cx, cy, cz = nx // 2, ny // 2, nz // 2
    ext = ny + 2 * HALO
    sent = pl.pallas_call(
        network_kernel,
        out_shape=tuple(shape((capacity, width), BF16) for _ in range(depths))
        + tuple(shape((MIG * width // (16 * cz), 16, cz), BF16) for _ in range(2)),
        in_specs=[SMEM_SPEC] * 2 + [VMEM_SPEC] * 7,
        out_specs=[VMEM_SPEC] * (depths + 2),
        compiler_params=PARAMS,
        cost_estimate=pl.CostEstimate(flops=1 << 31, bytes_accessed=1<<20, transcendentals=0),
        name="network",
    )(me, slab, species, sensed, death, move, route, net_weight, sensing)
    u0, text, u1, u2, inside = pl.pallas_call(
        functools.partial(inner_kernel, depths),
        out_shape=(
            shape((nx + 2 * HALO, ext, nz), F32),
            shape((nx + 2 * HALO - 2, ext, nz), F32),
            shape((nx + 2 * HALO - 2, ext, nz), F32),
            shape((nx + 4, ext, nz), F32),
            shape((nx - 4, ny, nz), F32),
        ),
        in_specs=[SMEM_SPEC] * 2 + [VMEM_SPEC] * 6,
        out_specs=[VMEM_SPEC] * 5,
        compiler_params=PARAMS,
        cost_estimate=pl.CostEstimate(flops=1 << 20, bytes_accessed=1<<20, transcendentals=0),
        name="inner",
    )(me, slab, nutrient, target, side_a, side_b, field_a, field_b)
    slab_a, slab_b, inside, *sent = lax.optimization_barrier((slab_a, slab_b, inside, *sent))
    text, _, u2, ct, ct_all, coarse_a, coarse_b = pl.pallas_call(
        functools.partial(smooth_kernel, depths, agents),
        out_shape=(
            shape(text.shape, F32),
            shape(u1.shape, F32),
            shape(u2.shape, F32),
            shape((cx, cy, cz), F32),
            shape((cx, cy, cz), BF16),
            shape((1, cx * HALO, cz), BF16),
            shape((1, cx * HALO, cz), BF16),
        ),
        in_specs=[SMEM_SPEC] * 2 + [VMEM_SPEC] * 7,
        out_specs=[VMEM_SPEC] * 7,
        scratch_shapes=[
            pltpu.VMEM((cx, nz // 128, ny, 128), F32),
            pltpu.VMEM(((HALO - 1) * ny, nz), F32),
        ],
        input_output_aliases={3: 0, 4: 1, 5: 2},
        compiler_params=PARAMS,
        name="smooth",
    )(me, slab, u0, text, u1, u2, inside, slab_a, slab_b)
    arrived = [sent[0]] + [cyclic(sent[k], "depth", k) for k in range(1, depths)]
    coarse_a = swapped(coarse_a, "depth", "a")
    coarse_b = swapped(coarse_b, "depth", "b")
    tail_a, tail_b = (
        swapped(jnp.concatenate([ct_all, coarse_a, coarse_b, movers], axis=0), "slab", which)
        for which, movers in (("a", sent[depths]), ("b", sent[depths + 1]))
    )
    base = pl.pallas_call(
        functools.partial(post_kernel, depths),
        out_shape=shape((nx, ny, nz), F32),
        in_specs=[SMEM_SPEC] + [VMEM_SPEC] * 2,
        out_specs=VMEM_SPEC,
        scratch_shapes=[pltpu.VMEM((nx + 2, ext, nz), F32)],
        compiler_params=PARAMS,
        cost_estimate=pl.CostEstimate(flops=1 << 30, bytes_accessed=1 << 22, transcendentals=0),
        name="post",
    )(me, u2, text)
    return pl.pallas_call(
        functools.partial(correct_kernel, depths),
        out_shape=(
            shape((nx, ny, nz), F32),
            shape((depths * capacity + 2 * MIG, width), BF16),
        ),
        in_specs=[SMEM_SPEC] * 2 + [VMEM_SPEC] * 6 + [ANY_SPEC] * depths,
        out_specs=[VMEM_SPEC, ANY_SPEC],
        scratch_shapes=[
            pltpu.VMEM((cx + 2, cz // 128, ext, 128), F32),
            pltpu.SemaphoreType.DMA((depths + 2 * (MIG // 16),)),
        ],
        compiler_params=PARAMS,
        name="correct",
    )(me, slab, ct, coarse_a, coarse_b, tail_a, tail_b, base, *arrived)


def solution(mesh):
    rows = P(("slab", "depth"))
    in_specs = (
        P("slab", "depth", None),
        P(("slab", "depth"), None),
        rows,
        rows,
        rows,
        rows,
        P(("slab", "depth"), None),
        P(),
        P(),
        P(),
    )
    out_specs = (P("slab", "depth", None), P(("slab", "depth"), None))
    return jax.shard_map(local, mesh=mesh, in_specs=in_specs, out_specs=out_specs, check_vma=False)
```

```python
import functools

import jax
import jax.numpy as jnp
from jax import lax
from jax.experimental import pallas as pl
from jax.experimental.pallas import tpu as pltpu
from jax.sharding import PartitionSpec as P

MIG = 128
PART = 256
SCREENING = 0.05
DAMPING = 2.0 / 3.0
CENTRE = 6.0 + SCREENING
COARSE_CENTRE = 6.0 + 4.0 * SCREENING
HALO = 4
F32, BF16 = jnp.float32, jnp.bfloat16
VMEM_SPEC = pl.BlockSpec(memory_space=pltpu.VMEM)
ANY_SPEC = pl.BlockSpec(memory_space=pl.ANY)
HBM_SPEC = pl.BlockSpec(memory_space=pltpu.HBM)
SMEM_SPEC = pl.BlockSpec(memory_space=pltpu.SMEM)
PARAMS = pltpu.CompilerParams(vmem_limit_bytes=40 * 1024 * 1024)


def dot(a, b, ca, cb):
    return lax.dot_general(a, b, (((ca,), (cb,)), ((), ())), preferred_element_type=F32)


def halves(x):
    high = x.astype(BF16)
    return high, (x - high.astype(F32)).astype(BF16)


def iota(shape, dim):
    return lax.broadcasted_iota(jnp.int32, shape, dim)


def cyclic(x, axis, by):
    count = lax.axis_size(axis)
    return lax.ppermute(x, axis, [(i, (i + by) % count) for i in range(count)])


def swapped(x, axis, which):
    count = lax.axis_size(axis)
    if count % 2:
        raise ValueError("odd axis")
    first = 0 if which == "a" else 1
    pairs = []
    for i in range(first, count, 2):
        j = (i + 1) % count
        pairs += [(i, j), (j, i)]
    return lax.ppermute(x, axis, sorted(pairs))


def is_even(x):
    return lax.rem(x, 2) == 0


LANES = 128


def shuffle(nz, back):
    one, two = iota((nz, nz), 0), iota((nz, nz), 1)
    if back:
        one, two = two, one
    return (one == (two % LANES) * (nz // LANES) + two // LANES).astype(F32).astype(BF16)


def begin_kernel(me_ref, slab_ref, *refs):
    count = 10
    sources, refs = refs[:count], refs[count:]
    u_ref, t_ref, sensed_ref, depth_a, depth_b, field_a, field_b, list_ref, *targets = refs[:-5]
    raw, weight_ref, cell_ref, divide_ref, sem = refs[-5:]
    targets = [cell_ref, raw, divide_ref, weight_ref] + targets
    species_ref, death_ref = targets[4:6]
    copies = [
        pltpu.make_async_copy(source, target, sem.at[i])
        for i, (source, target) in enumerate(zip(sources, targets, strict=True))
    ]
    for copy in copies:
        copy.start()
    nx, ny, nz = u_ref.shape
    agents = species_ref.shape[0]
    rows = nx * ny
    tiles = nz // LANES
    order = shuffle(nz, False)
    copies[0].wait()
    cell = cell_ref[...]
    cell_row = cell // nz
    cell_z = cell - cell_row * nz
    cell_z = (cell_z % tiles) * LANES + cell_z // tiles
    one_z = (iota((nz, agents), 0) == cell_z).astype(F32).astype(BF16)
    in_row = iota((rows, agents), 0) == cell_row
    copies[1].wait()
    high, low = halves(raw[...].reshape(rows, nz))
    high = dot(high, order, 1, 0)
    u = high + dot(low, order, 1, 0)
    u_ref[...] = u.reshape(nx, ny, nz)
    half = ny // 16
    slab_even = is_even(slab_ref[0])
    for ref, front in ((field_a, slab_even), (field_b, jnp.logical_not(slab_even))):
        start = jnp.where(front, nx - HALO, 0)
        for k in range(HALO):
            ref[k * half : (k + 1) * half] = u_ref[start + k].astype(BF16).reshape(half, 16, nz)
    for copy in copies[2:]:
        copy.wait()
    picked = dot(high.astype(BF16), one_z, 1, 0)
    sample = jnp.sum(jnp.where(in_row, picked, 0.0), axis=0, keepdims=True)
    sensed_ref[...] = jnp.broadcast_to(sample, (8, agents))
    weight = jnp.broadcast_to(weight_ref[...].reshape(1, -1), (8, species_ref.shape[1]))
    score = dot(weight, species_ref[...], 1, 1)[0:1]
    softplus = jnp.maximum(score, 0.0) + jnp.log1p(jnp.exp(-jnp.abs(score)))
    alive = (1 - death_ref[...].reshape(1, agents)).astype(F32)
    divide = divide_ref[...].reshape(1, agents).astype(F32)
    uptake = alive * (1.0 + divide) * softplus * sample / (0.5 + sample)
    up_high = uptake.astype(BF16).astype(F32)
    a_high = jnp.where(in_row, up_high, 0.0).astype(BF16)
    a_low = jnp.where(in_row, uptake - up_high, 0.0).astype(BF16)
    source = dot(a_high, one_z, 1, 1) + dot(a_low, one_z, 1, 1)
    t_ref[...] = (SCREENING * u - source).reshape(nx, ny, nz)
    even = is_even(me_ref[0])
    for pair in range(nx // 2):
        parts = []
        for start in (0, ny - HALO):
            for plane in (2 * pair, 2 * pair + 1):
                parts.append(u_ref[plane, start : start + HALO])
                parts.append(t_ref[plane, start : start + HALO])
        low = jnp.concatenate(parts[:4], axis=0)
        high = jnp.concatenate(parts[4:], axis=0)
        depth_a[pair] = jnp.where(even, high, low).astype(BF16)
        depth_b[pair] = jnp.where(even, low, high).astype(BF16)
    part = cell_z // PART
    values = (cell_row.astype(F32), (cell_z - part * PART).astype(F32), part.astype(F32), up_high)
    list_ref[...] = jnp.concatenate(
        [x[:, i * nz : (i + 1) * nz] for x in values for i in range(agents // nz)], axis=0
    )


def network_kernel(
    me_ref, slab_ref, species_ref, sensed_ref, death_ref, move_ref, route_ref, net_ref, sensing_ref, *outs
):
    agents, width = species_ref.shape
    depths = len(outs) - 2
    capacity = outs[0].shape[0]
    species = species_ref[...]
    sensing = sensing_ref[...].reshape(1, width)
    first = sensing.astype(BF16)
    rest = sensing - first.astype(F32)
    second = rest.astype(BF16)
    third = (rest - second.astype(F32)).astype(BF16)
    line = iota((8, width), 0)
    terms = jnp.where(
        line == 0, first.astype(F32),
        jnp.where(line == 1, second.astype(F32), jnp.where(line == 2, third.astype(F32), 0.0)),
    ).astype(BF16)
    activation = dot(species, net_ref[...], 1, 0) + dot(sensed_ref[...].astype(BF16), terms, 0, 0)
    updated = (0.5 * species.astype(F32) + jnp.tanh(activation)).astype(BF16)
    lanes = 128
    lines = -(-(depths + 2) // 8) * 8
    line = iota((lines, lanes), 0)
    square = iota((lanes, 2 * lanes), 0)
    column = iota((lanes, 2 * lanes), 1)
    counter = jnp.where(jnp.logical_or(column >= lanes, square < column), 1.0, 0.0).astype(BF16)
    blocks = agents // lanes
    route = route_ref[...].reshape(1, agents)
    move = move_ref[...].reshape(1, agents)
    death = death_ref[...].reshape(1, agents)
    hits = []
    for block in range(blocks):
        cut = slice(block * lanes, (block + 1) * lanes)
        wanted = jnp.where(line < depths, route[:, cut], jnp.where(line < depths + 2, move[:, cut] + (depths - 1), -1))
        hits.append((wanted == line).astype(F32))
    counts = dot(jnp.concatenate(hits, axis=0).astype(BF16), counter, 1, 0)
    me = me_ref[0]
    to_a = jnp.where(is_even(slab_ref[0]), 1, 2)
    running = jnp.zeros((lines, lanes), F32)
    keys = []
    for block in range(blocks):
        cut = slice(block * lanes, (block + 1) * lanes)
        own = slice(block * lines, (block + 1) * lines)
        before = (counts[own, :lanes] + running) * hits[block]
        running = running + counts[own, lanes:]
        slot = jnp.sum(jnp.where(line < depths, before, 0.0), axis=0, keepdims=True).astype(jnp.int32)
        rank = jnp.sum(jnp.where(line < depths, 0.0, before), axis=0, keepdims=True).astype(jnp.int32)
        hop = route[:, cut] - me
        hop = jnp.where(hop < 0, hop + depths, hop)
        key = jnp.where(
            move[:, cut] == 0,
            hop * capacity + slot,
            depths * capacity + jnp.where(move[:, cut] == to_a, 0, MIG) + rank,
        )
        keys.append(jnp.where(death[:, cut] == 0, key, -1))
    key = jnp.concatenate(keys, axis=1)
    start = 0
    for index, out in enumerate(outs):
        size = capacity if index < depths else MIG
        chosen = (iota((size, agents), 0) == key - start).astype(F32).astype(BF16)
        placed = dot(chosen, updated, 1, 0).astype(BF16)
        start += size
        if index < depths:
            out[...] = placed
        else:
            tiles = out.shape[2] // width
            for i in range(MIG // 16):
                at = (i % tiles) * width
                out[i // tiles, :, at : at + width] = placed[i * 16 : (i + 1) * 16]


def tiles_of(x):
    return [x[:, i : i + LANES] for i in range(0, x.shape[1], LANES)]


def third_sum(x):
    parts = tiles_of(x)
    lane = iota((x.shape[0], LANES), 1)
    before = jnp.where(lane == 0, 0.0, pltpu.roll(parts[-1], 1, 1))
    after = jnp.where(lane == LANES - 1, 0.0, pltpu.roll(parts[0], LANES - 1, 1))
    padded = [before] + parts + [after]
    return jnp.concatenate([x + y for x, y in zip(padded[:-2], padded[2:])], axis=1)


def neighbour_total(before, plane, after):
    rows = plane.shape[0]
    second = pltpu.roll(plane, 1, 0) + pltpu.roll(plane, rows - 1, 0)
    return before + after + second + third_sum(plane)


def relaxed(before, plane, after, target, centre):
    return (1.0 - DAMPING) * plane + (DAMPING / centre) * (
        target + neighbour_total(before, plane, after)
    )


def edge_mask(me, depths, halo):
    row = iota((2 * halo, 1), 0)
    return jnp.where(
        row < halo, (me < depths - 1).astype(F32), (me > 0).astype(F32)
    )


def masked(plane, own, mask):
    return jnp.concatenate([plane[:own], plane[own:] * mask], axis=0)


def halo_rows(side_a, side_b, even, plane, mask):
    at = 2 * HALO * (plane % 2)
    side_a = side_a[at : at + 2 * HALO].astype(F32)
    side_b = side_b[at : at + 2 * HALO].astype(F32)
    high = jnp.where(even, side_a, side_b)
    low = jnp.where(even, side_b, side_a)
    return (
        jnp.concatenate([high[:HALO], low[:HALO]], axis=0) * mask,
        jnp.concatenate([high[HALO:], low[HALO:]], axis=0),
    )


def corner_kernel(me_ref, slab_ref, side_a, side_b, list_ref, slab_a, slab_b):
    layers = 2 * side_a.shape[0]
    nz = side_a.shape[2]
    even = is_even(me_ref[0])
    slab_even = is_even(slab_ref[0])

    def layer(side, plane):
        at = 2 * HALO * (plane % 2)
        return side[plane // 2].astype(F32)[at : at + 2 * HALO]

    for ref, front in ((slab_a, slab_even), (slab_b, jnp.logical_not(slab_even))):
        parts = []
        for side, high in ((side_a, even), (side_b, jnp.logical_not(even))):
            targets = []
            for i in range(1, HALO):
                x = jnp.where(front, layer(side, layers - i), layer(side, i - 1))
                parts.append(jnp.where(high, x[: HALO - i], x[i:HALO]))
                if i < HALO - 1:
                    targets.append(
                        jnp.where(high, x[HALO : 2 * HALO - 1 - i], x[HALO + 1 + i :])
                    )
            parts += targets
        parts.append(list_ref[...])
        used = sum(part.shape[0] for part in parts)
        total = ref.shape[0] * ref.shape[1]
        parts.append(jnp.zeros((total - used, nz), F32))
        ref[...] = jnp.concatenate(parts, axis=0).astype(BF16).reshape(ref.shape)


def corner_rows(block_a, block_b, even, mask):
    high = jnp.where(even, block_a, block_b)
    low = jnp.where(even, block_b, block_a)
    nz = high.shape[1]
    fields, targets = [], []
    at = 0
    for rows, out in ((HALO, fields), (HALO - 1, targets)):
        for i in range(1, rows):
            count = rows - i
            gap = jnp.zeros((2 * (HALO - count), nz), F32)
            cut = slice(at, at + count)
            out.append(jnp.concatenate([high[cut], gap, low[cut]], axis=0) * mask)
            at += count
    return fields, targets + [jnp.zeros_like(fields[0])]


KEEP, PULL = 1.0 - DAMPING, DAMPING / CENTRE


def inner_kernel(
    depths, me_ref, slab_ref, u_ref, t_ref, side_a, side_b, field_a, field_b, u0, text_ref, u1, u2_ref, inside
):
    nx, ny, nz = u_ref.shape
    even = is_even(me_ref[0])
    slab_even = is_even(slab_ref[0])
    half = ny // 16
    mask = edge_mask(me_ref[0], depths, HALO)
    for field, after in ((field_a, slab_even), (field_b, jnp.logical_not(slab_even))):
        u_at = jnp.where(after, HALO + nx, 0)
        for k in range(HALO):
            u0[u_at + k, :ny] = field[k * half : (k + 1) * half].astype(F32).reshape(ny, nz)
            u0[u_at + k, ny:] = jnp.zeros((2 * HALO, nz), F32)
    for plane in range(nx):
        u0[HALO + plane, :ny] = u_ref[plane]
        text_ref[HALO - 1 + plane, :ny] = t_ref[plane]
        uh, th = halo_rows(side_a[plane // 2], side_b[plane // 2], even, plane, mask)
        u0[HALO + plane, ny:] = uh
        text_ref[HALO - 1 + plane, ny:] = th

    def outer(i, carry):
        for p in (i, nx + HALO - 1 + i):
            u1[p] = KEEP * u0[p + 1] + PULL * neighbour_total(u0[p], u0[p + 1], u0[p + 2])
        return carry

    lax.fori_loop(0, HALO - 1, outer, 0)

    def first(p, carry):
        v = relaxed(u0[p], u0[p + 1], u0[p + 2], text_ref[p], CENTRE)
        u1[p] = masked(v, ny, mask)
        return carry

    lax.fori_loop(HALO - 1, nx + HALO - 1, first, 0, unroll=2)

    def second(p, carry):
        v = relaxed(u1[p], u1[p + 1], u1[p + 2], text_ref[p + 1], CENTRE)
        u2_ref[p] = masked(v, ny, mask)
        return carry

    lax.fori_loop(HALO - 1, nx + 1, second, 0, unroll=2)
    for p in range(2, nx - 2):
        inside[p - 2] = residual(u2_ref, text_ref, p, ny)


def residual(u2_ref, text_ref, p, ny):
    v = u2_ref[p + 2]
    total = neighbour_total(u2_ref[p + 1], v, u2_ref[p + 3])
    return (text_ref[p + 3] - CENTRE * v + total)[:ny]


def smooth_kernel(
    depths, agents, me_ref, slab_ref, u0, text_in, u1_in, u2_in, inside, slab_a, slab_b,
    text_ref, u1, u2_ref, coarse_ref, coarse_all_ref, coarse_a, coarse_b, paired, foreign,
):
    nx = u0.shape[0] - 2 * HALO
    ny, nz = u0.shape[1] - 2 * HALO, u0.shape[2]
    mask = edge_mask(me_ref[0], depths, HALO)
    even = is_even(me_ref[0])
    slab_even = is_even(slab_ref[0])
    near = HALO - 1
    corner = HALO * near // 2 + near * (near - 1) // 2
    row = iota((8, 1), 0)
    first, last = (row == 0).astype(F32), (row == 7).astype(F32)
    for ref, after in ((slab_a, slab_even), (slab_b, jnp.logical_not(slab_even))):
        message = ref[...].astype(F32).reshape(-1, nz)
        fields, targets = corner_rows(message[:corner], message[corner : 2 * corner], even, mask)
        sign = jnp.where(after, 1, -1)
        edge = jnp.where(after, nx - 1, 0)
        lines = agents // nz
        cell_row, place, part, uptake = (
            jnp.concatenate([message[at + i : at + i + 1] for i in range(lines)], axis=1)
            for at in range(2 * corner, 2 * corner + 4 * lines, lines)
        )
        cell_row = cell_row.astype(jnp.int32) - jnp.where(after, 0, (nx - near) * ny)
        wanted = jnp.logical_and(cell_row >= 0, cell_row < near * ny)
        key = jnp.where(wanted, part.astype(jnp.int32) * (near * ny) + cell_row, -1)
        one_z = (iota((PART, agents), 0) == place.astype(jnp.int32)).astype(F32).astype(BF16)
        key_rows = iota((near * ny * (nz // PART), agents), 0)
        taken = jnp.where(key_rows == key, uptake, 0.0).astype(BF16)
        source = dot(taken, one_z, 1, 1)
        for i in range(nz // PART):
            foreign[:, i * PART : (i + 1) * PART] = source[i * near * ny : (i + 1) * near * ny]
        for i in range(1, HALO):
            p = edge + sign * i
            index = jnp.where(after, i - 1, HALO - 1 - i)
            t = SCREENING * u0[p + 4, :ny] - foreign[pl.ds(index * ny, ny)]
            text_ref[p + 3, :ny] = t
            text_ref[p + 3, ny:] = targets[i - 1]
            x = fields[i - 1]
            nearer = u0[p + 4 - sign, ny:] if i == 1 else fields[i - 2]
            total = nearer + third_sum(x)
            if i < HALO - 1:
                total = total + fields[i]
            beyond = u0[p + 4]
            up = jnp.where(row == 0, beyond[ny - 1 : ny], pltpu.roll(x, 1, 0))
            down = jnp.where(row == 7, beyond[0:1], pltpu.roll(x, 7, 0))
            u1[p + 3, ny:] = (KEEP * x + PULL * (targets[i - 1] + total + up + down)) * mask
            v = u1[p + 3, :ny] + PULL * t
            u1[p + 3, :ny] = v
            u1[p + 3, 0:8] = v[0:8] + (PULL * first) * x[7:8]
            u1[p + 3, ny - 8 : ny] = v[ny - 8 :] + (PULL * last) * x[0:1]
        u1[edge + 3, ny:] = u1[edge + 3, ny:] + PULL * fields[0]
        u2_ref[edge - sign + 2, ny:] = u2_ref[edge - sign + 2, ny:] + (PULL * PULL) * fields[0]

    def second(i, carry):
        for p in (i, nx + 1 + i):
            v = relaxed(u1[p], u1[p + 1], u1[p + 2], text_ref[p + 1], CENTRE)
            u2_ref[p] = masked(v, ny, mask)
        return carry

    lax.fori_loop(0, HALO - 1, second, 0)
    for q in range(nx // 2):
        both = 0.0
        for p in (2 * q, 2 * q + 1):
            known = 2 <= p < nx - 2
            both = both + (inside[p - 2] if known else residual(u2_ref, text_ref, p, ny))
        parts = tiles_of(both)
        for i in range(len(parts) // 2):
            paired[q, i] = parts[2 * i] + parts[2 * i + 1]
    cx, cy, cz = coarse_ref.shape
    coarse = jnp.concatenate(
        [
            jnp.concatenate(
                [
                    paired[q, i, pl.ds(0, cy, 2), :] + paired[q, i, pl.ds(1, cy, 2), :]
                    for i in range(cz // LANES)
                ],
                axis=1,
            )
            for q in range(cx)
        ],
        axis=0,
    )
    coarse = 0.5 * coarse
    coarse_ref[...] = coarse.reshape(cx, cy, cz)
    coarse_all_ref[...] = coarse.astype(BF16).reshape(cx, cy, cz)
    low, high = (
        jnp.concatenate([coarse_ref[q, start : start + HALO] for q in range(cx)], axis=0)
        for start in (0, cy - HALO)
    )
    coarse_a[0] = jnp.where(even, high, low).astype(BF16)
    coarse_b[0] = jnp.where(even, low, high).astype(BF16)


def post_kernel(depths, me_ref, u2_ref, text_ref, out_ref, back_ref, v1):
    nx, ny, nz = out_ref.shape
    back_ref[...] = shuffle(nz, True)
    mask = edge_mask(me_ref[0], depths, HALO)

    def first(p, carry):
        v = relaxed(u2_ref[p], u2_ref[p + 1], u2_ref[p + 2], text_ref[p + 2], CENTRE)
        v1[p] = masked(v, ny, mask)
        return carry

    lax.fori_loop(0, nx + 2, first, 0, unroll=2)

    def second(p, carry):
        v = relaxed(v1[p], v1[p + 1], v1[p + 2], text_ref[p + 3], CENTRE)
        out_ref[p] = v[:ny]
        return carry

    lax.fori_loop(0, nx, second, 0, unroll=2)


def correct_kernel(
    depths, me_ref, slab_ref, ct_ref, side_a, side_b, slab_a, slab_b, base_ref, back_ref, *rest
):
    packed = rest[:depths]
    out_any, agents_ref, fine, out_ref, sem = rest[depths:]
    nx, ny, nz = out_ref.shape
    cx, cy, cz = ct_ref.shape
    me = me_ref[0]
    even = is_even(me)
    slab_even = is_even(slab_ref[0])
    capacity = packed[0].shape[0]
    width = agents_ref.shape[1]
    copies = []
    for k in range(depths):
        origin = me - k
        origin = jnp.where(origin < 0, origin + depths, origin)
        place = pl.ds(pl.multiple_of(origin * capacity, capacity), capacity)
        copies.append(pltpu.make_async_copy(packed[k], agents_ref.at[place], sem.at[len(copies)]))
    tiles = cz // width
    for ref, late in ((slab_a, slab_even), (slab_b, jnp.logical_not(slab_even))):
        start = depths * capacity + jnp.where(late, MIG, 0)
        for i in range(MIG // 16):
            place = pl.ds(pl.multiple_of(start + i * 16, 16), 16)
            source = ref.at[cx + 2 + i // tiles, :, pl.ds((i % tiles) * width, width)]
            copies.append(pltpu.make_async_copy(source, agents_ref.at[place], sem.at[len(copies)]))
    for copy in copies:
        copy.start()
    mask = edge_mask(me, depths, HALO)

    def chosen(condition, x, y):
        return jnp.where(condition, x.astype(F32), y.astype(F32))

    planes = []
    for p in range(cx + 2 * HALO):
        if HALO <= p < HALO + cx:
            k = p - HALO
            own, one, two = ct_ref[k], side_a[0].astype(F32), side_b[0].astype(F32)
        else:
            before = p < HALO
            k = p + cx - HALO if before else p - HALO - cx
            x, y = (slab_b, slab_a) if before else (slab_a, slab_b)
            own, one, two = (chosen(slab_even, x[i], y[i]) for i in (k, cx, cx + 1))
        rows = slice(HALO * k, HALO * (k + 1))
        one, two = one[rows], two[rows]
        sides = jnp.concatenate([jnp.where(even, one, two), jnp.where(even, two, one)], axis=0)
        planes.append(jnp.concatenate([own, sides * mask], axis=0))
    values = [(DAMPING / COARSE_CENTRE) * plane for plane in planes]
    for sweep in range(1, HALO):
        values = [
            masked(
                relaxed(values[i - 1], values[i], values[i + 1], planes[i + sweep - 1], COARSE_CENTRE),
                cy,
                mask,
            )
            for i in range(1, len(values) - 1)
        ]
    wide = cy + 4
    for q, value in enumerate(values):
        value = jnp.concatenate([value[: cy + 2], value[cy + 2 * HALO - 2 :]], axis=0)
        for i, part in enumerate(tiles_of(value)):
            fine[q, i, pl.ds(0, wide, 2), :] = part
            fine[q, i, pl.ds(1, wide, 2), :] = part
    def second_total(plane):
        rows = plane.shape[0]
        return pltpu.roll(plane, 1, 0) + pltpu.roll(plane, rows - 1, 0)

    spread = [jnp.concatenate([fine[q, i] for i in range(cz // LANES)], axis=1) for q in range(cx + 2)]
    still = [KEEP * plane + PULL * second_total(plane) for plane in spread]
    once = []
    for p in range(-1, nx + 1):
        q = (p + 2) // 2
        if p % 2 == 0:
            others = spread[q - 1] + spread[q]
        else:
            others = spread[q] + spread[q + 1]
        once.append(masked(still[q] + PULL * others, ny, mask))

    def twice(plane):
        return jnp.concatenate([part for part in tiles_of(plane) for _ in range(2)], axis=1)

    back = back_ref[...]
    step = 2
    for start in range(0, nx, step):
        planes = []
        for p in range(start, start + step):
            plane = once[p + 1]
            total = once[p] + once[p + 2] + second_total(plane)
            none = (KEEP * plane + PULL * total)[:ny]
            one = (2.0 * PULL) * plane[:ny]
            two = (PULL * PULL) * spread[(p + 2) // 2][:ny]
            planes.append(base_ref[p] + twice(none) + third_sum(twice(one) + third_sum(twice(two))))
        high, low = halves(jnp.concatenate(planes, axis=0))
        done = dot(high, back, 1, 0) + dot(low, back, 1, 0)
        out_ref[start : start + step] = done.reshape(step, ny, nz)
        cut = pl.ds(start, step)
        copies.append(pltpu.make_async_copy(out_ref.at[cut], out_any.at[cut], sem.at[len(copies)]))
        copies[-1].start()
    for copy in copies:
        copy.wait()


def local(
    nutrient, species, agent_cell, death_flag, divide_flag, slab_move, depth_route, net_weight, sensing, uptake_weight
):
    depths = lax.axis_size("depth")
    nx, ny, nz = nutrient.shape
    agents, width = species.shape
    capacity = 2 * agents // depths
    me = lax.axis_index("depth").astype(jnp.int32).reshape(1)
    slab = lax.axis_index("slab").astype(jnp.int32).reshape(1)
    shape = jax.ShapeDtypeStruct
    cells, death, divide = (x.reshape(1, agents) for x in (agent_cell, death_flag, divide_flag))
    move, route = slab_move.reshape(1, agents), depth_route.reshape(1, agents)
    half = ny // 16
    if agents % nz or nx * ny > PART or nz % PART:
        raise ValueError("list digits")
    arguments = (
        cells, nutrient, divide, uptake_weight.reshape(1, width), species, death,
        move, route, net_weight, sensing.reshape(1, width),
    )
    (
        nutrient, target, sensed, depth_a, depth_b, field_a, field_b, agent_list,
        species, death, move, route, net_weight, sensing,
    ) = pl.pallas_call(
        begin_kernel,
        out_shape=(
            shape((nx, ny, nz), F32),
            shape((nx, ny, nz), F32),
            shape((8, agents), F32),
            shape((nx // 2, 16, nz), BF16),
            shape((nx // 2, 16, nz), BF16),
            shape((HALO * half, 16, nz), BF16),
            shape((HALO * half, 16, nz), BF16),
            shape((4 * agents // nz, nz), F32),
        )
        + tuple(shape(x.shape, x.dtype) for x in arguments[4:]),
        in_specs=[SMEM_SPEC] * 2 + [HBM_SPEC] * len(arguments),
        out_specs=[VMEM_SPEC] * (8 + len(arguments) - 4),
        scratch_shapes=[
            pltpu.VMEM((nx, ny, nz), F32),
            pltpu.VMEM((1, width), BF16),
            pltpu.VMEM((1, agents), jnp.int32),
            pltpu.VMEM((1, agents), jnp.int32),
            pltpu.SemaphoreType.DMA((len(arguments),)),
        ],
        compiler_params=PARAMS,
        name="begin",
    )(me, slab, *(pltpu.with_memory_space_constraint(x, pltpu.HBM) for x in arguments))
    field_a, field_b, depth_a, depth_b = lax.optimization_barrier(
        (field_a, field_b, depth_a, depth_b)
    )
    side_a = swapped(depth_a, "depth", "a")
    side_b = swapped(depth_b, "depth", "b")
    field_a = swapped(field_a, "slab", "a")
    field_b = swapped(field_b, "slab", "b")
    rows = 2 * (HALO - 1) ** 2 + agent_list.shape[0]
    rows = -(-rows // 16) * 16
    slab_a, slab_b = pl.pallas_call(
        corner_kernel,
        out_shape=tuple(shape((rows // 16, 16, nz), BF16) for _ in range(2)),
        in_specs=[SMEM_SPEC] * 2 + [VMEM_SPEC] * 3,
        out_specs=[VMEM_SPEC] * 2,
        compiler_params=PARAMS,
        name="corner",
    )(me, slab, side_a, side_b, agent_list)
    slab_a = swapped(slab_a, "slab", "a")
    slab_b = swapped(slab_b, "slab", "b")
    cx, cy, cz = nx // 2, ny // 2, nz // 2
    ext = ny + 2 * HALO
    sent = pl.pallas_call(
        network_kernel,
        out_shape=tuple(shape((capacity, width), BF16) for _ in range(depths))
        + tuple(shape((MIG * width // (16 * cz), 16, cz), BF16) for _ in range(2)),
        in_specs=[SMEM_SPEC] * 2 + [VMEM_SPEC] * 7,
        out_specs=[VMEM_SPEC] * (depths + 2),
        compiler_params=PARAMS,
        cost_estimate=pl.CostEstimate(flops=1 << 31, bytes_accessed=1<<20, transcendentals=0),
        name="network",
    )(me, slab, species, sensed, death, move, route, net_weight, sensing)
    u0, text, u1, u2, inside = pl.pallas_call(
        functools.partial(inner_kernel, depths),
        out_shape=(
            shape((nx + 2 * HALO, ext, nz), F32),
            shape((nx + 2 * HALO - 2, ext, nz), F32),
            shape((nx + 2 * HALO - 2, ext, nz), F32),
            shape((nx + 4, ext, nz), F32),
            shape((nx - 4, ny, nz), F32),
        ),
        in_specs=[SMEM_SPEC] * 2 + [VMEM_SPEC] * 6,
        out_specs=[VMEM_SPEC] * 5,
        compiler_params=PARAMS,
        cost_estimate=pl.CostEstimate(flops=1 << 20, bytes_accessed=1<<20, transcendentals=0),
        name="inner",
    )(me, slab, nutrient, target, side_a, side_b, field_a, field_b)
    slab_a, slab_b, inside, *sent = lax.optimization_barrier((slab_a, slab_b, inside, *sent))
    text, _, u2, ct, ct_all, coarse_a, coarse_b = pl.pallas_call(
        functools.partial(smooth_kernel, depths, agents),
        out_shape=(
            shape(text.shape, F32),
            shape(u1.shape, F32),
            shape(u2.shape, F32),
            shape((cx, cy, cz), F32),
            shape((cx, cy, cz), BF16),
            shape((1, cx * HALO, cz), BF16),
            shape((1, cx * HALO, cz), BF16),
        ),
        in_specs=[SMEM_SPEC] * 2 + [VMEM_SPEC] * 7,
        out_specs=[VMEM_SPEC] * 7,
        scratch_shapes=[
            pltpu.VMEM((cx, cz // LANES, ny, LANES), F32),
            pltpu.VMEM(((HALO - 1) * ny, nz), F32),
        ],
        input_output_aliases={3: 0, 4: 1, 5: 2},
        compiler_params=PARAMS,
        name="smooth",
    )(me, slab, u0, text, u1, u2, inside, slab_a, slab_b)
    arrived = [sent[0]] + [cyclic(sent[k], "depth", k) for k in range(1, depths)]
    coarse_a = swapped(coarse_a, "depth", "a")
    coarse_b = swapped(coarse_b, "depth", "b")
    tail_a, tail_b = (
        swapped(jnp.concatenate([ct_all, coarse_a, coarse_b, movers], axis=0), "slab", which)
        for which, movers in (("a", sent[depths]), ("b", sent[depths + 1]))
    )
    base, back = pl.pallas_call(
        functools.partial(post_kernel, depths),
        out_shape=(shape((nx, ny, nz), F32), shape((nz, nz), BF16)),
        in_specs=[SMEM_SPEC] + [VMEM_SPEC] * 2,
        out_specs=[VMEM_SPEC] * 2,
        scratch_shapes=[pltpu.VMEM((nx + 2, ext, nz), F32)],
        compiler_params=PARAMS,
        cost_estimate=pl.CostEstimate(flops=1 << 30, bytes_accessed=1 << 22, transcendentals=0),
        name="post",
    )(me, u2, text)
    return pl.pallas_call(
        functools.partial(correct_kernel, depths),
        out_shape=(
            shape((nx, ny, nz), F32),
            shape((depths * capacity + 2 * MIG, width), BF16),
        ),
        in_specs=[SMEM_SPEC] * 2 + [VMEM_SPEC] * 7 + [ANY_SPEC] * depths,
        out_specs=[HBM_SPEC, ANY_SPEC],
        scratch_shapes=[
            pltpu.VMEM((cx + 2, cz // LANES, ext, LANES), F32),
            pltpu.VMEM((nx, ny, nz), F32),
            pltpu.SemaphoreType.DMA((depths + 2 * (MIG // 16) + nx // 2,)),
        ],
        compiler_params=PARAMS,
        name="correct",
    )(me, slab, ct, coarse_a, coarse_b, tail_a, tail_b, base, back, *arrived)


def solution(mesh):
    rows = P(("slab", "depth"))
    in_specs = (
        P("slab", "depth", None),
        P(("slab", "depth"), None),
        rows,
        rows,
        rows,
        rows,
        P(("slab", "depth"), None),
        P(),
        P(),
        P(),
    )
    out_specs = (P("slab", "depth", None), P(("slab", "depth"), None))
    return jax.shard_map(local, mesh=mesh, in_specs=in_specs, out_specs=out_specs, check_vma=False)
```

```python
import functools

import jax
import jax.numpy as jnp
from jax import lax
from jax.experimental import pallas as pl
from jax.experimental.pallas import tpu as pltpu
from jax.sharding import PartitionSpec as P

MIG = 128
PART = 256
SCREENING = 0.05
DAMPING = 2.0 / 3.0
CENTRE = 6.0 + SCREENING
COARSE_CENTRE = 6.0 + 4.0 * SCREENING
HALO = 4
F32, BF16 = jnp.float32, jnp.bfloat16
VMEM_SPEC = pl.BlockSpec(memory_space=pltpu.VMEM)
ANY_SPEC = pl.BlockSpec(memory_space=pl.ANY)
HBM_SPEC = pl.BlockSpec(memory_space=pltpu.HBM)
SMEM_SPEC = pl.BlockSpec(memory_space=pltpu.SMEM)
PARAMS = pltpu.CompilerParams(vmem_limit_bytes=40 * 1024 * 1024)


def dot(a, b, ca, cb):
    return lax.dot_general(a, b, (((ca,), (cb,)), ((), ())), preferred_element_type=F32)


def halves(x):
    high = x.astype(BF16)
    return high, (x - high.astype(F32)).astype(BF16)


def iota(shape, dim):
    return lax.broadcasted_iota(jnp.int32, shape, dim)


def cyclic(x, axis, by):
    count = lax.axis_size(axis)
    return lax.ppermute(x, axis, [(i, (i + by) % count) for i in range(count)])


def swapped(x, axis, which):
    count = lax.axis_size(axis)
    if count % 2:
        raise ValueError("odd axis")
    first = 0 if which == "a" else 1
    pairs = []
    for i in range(first, count, 2):
        j = (i + 1) % count
        pairs += [(i, j), (j, i)]
    return lax.ppermute(x, axis, sorted(pairs))


def is_even(x):
    return lax.rem(x, 2) == 0


LANES = 128


def shuffle(nz, back):
    one, two = iota((nz, nz), 0), iota((nz, nz), 1)
    if back:
        one, two = two, one
    return (one == (two % LANES) * (nz // LANES) + two // LANES).astype(F32).astype(BF16)


def load_kernel(slab_ref, *refs):
    count = 10
    sources, refs = refs[:count], refs[count:]
    u_ref, place_ref, field_a, field_b, *targets = refs[:-2]
    raw, sem = refs[-2:]
    cell_ref = targets[0]
    targets.insert(1, raw)
    copies = [
        pltpu.make_async_copy(source, target, sem.at[i])
        for i, (source, target) in enumerate(zip(sources, targets, strict=True))
    ]
    for copy in copies:
        copy.start()
    nx, ny, nz = u_ref.shape
    rows = nx * ny
    tiles = nz // LANES
    order = shuffle(nz, False)
    copies[0].wait()
    cell_z = cell_ref[...] % nz
    cell_z = (cell_z % tiles) * LANES + cell_z // tiles
    place_ref[...] = (iota(place_ref.shape, 0) == cell_z).astype(F32).astype(BF16)
    copies[1].wait()
    high, low = halves(raw[...].reshape(rows, nz))
    both = dot(jnp.concatenate([high, low], axis=0), order, 1, 0)
    u_ref[...] = (both[:rows] + both[rows:]).reshape(nx, ny, nz)
    half = ny // 16
    slab_even = is_even(slab_ref[0])
    for ref, front in ((field_a, slab_even), (field_b, jnp.logical_not(slab_even))):
        start = jnp.where(front, nx - HALO, 0)
        for k in range(HALO):
            ref[k * half : (k + 1) * half] = u_ref[start + k].astype(BF16).reshape(half, 16, nz)
    for copy in copies[2:]:
        copy.wait()


def uptake_kernel(
    me_ref, u_ref, place_ref, cell_ref, divide_ref, weight_ref, species_ref, death_ref,
    t_ref, sensed_ref, depth_a, depth_b, list_ref,
):
    nx, ny, nz = u_ref.shape
    agents = species_ref.shape[0]
    rows = nx * ny
    tiles = nz // LANES
    cell = cell_ref[...]
    cell_row = cell // nz
    cell_z = cell - cell_row * nz
    cell_z = (cell_z % tiles) * LANES + cell_z // tiles
    one_z = place_ref[...]
    in_row = iota((rows, agents), 0) == cell_row
    u = u_ref[...].reshape(rows, nz)
    picked = dot(u.astype(BF16), one_z, 1, 0)
    sample = jnp.sum(jnp.where(in_row, picked, 0.0), axis=0, keepdims=True)
    sensed_ref[...] = jnp.broadcast_to(sample, (8, agents))
    weight = jnp.broadcast_to(weight_ref[...].reshape(1, -1), (8, species_ref.shape[1]))
    score = dot(weight, species_ref[...], 1, 1)[0:1]
    softplus = jnp.maximum(score, 0.0) + jnp.log1p(jnp.exp(-jnp.abs(score)))
    alive = (1 - death_ref[...].reshape(1, agents)).astype(F32)
    divide = divide_ref[...].reshape(1, agents).astype(F32)
    uptake = alive * (1.0 + divide) * softplus * sample / (0.5 + sample)
    up_high = uptake.astype(BF16).astype(F32)
    source = dot(jnp.where(in_row, up_high, 0.0).astype(BF16), one_z, 1, 1)
    t_ref[...] = (SCREENING * u - source).reshape(nx, ny, nz)
    even = is_even(me_ref[0])
    for pair in range(nx // 2):
        parts = []
        for start in (0, ny - HALO):
            for plane in (2 * pair, 2 * pair + 1):
                parts.append(u_ref[plane, start : start + HALO])
                parts.append(t_ref[plane, start : start + HALO])
        low = jnp.concatenate(parts[:4], axis=0)
        high = jnp.concatenate(parts[4:], axis=0)
        depth_a[pair] = jnp.where(even, high, low).astype(BF16)
        depth_b[pair] = jnp.where(even, low, high).astype(BF16)
    part = cell_z // PART
    values = (cell_row.astype(F32), (cell_z - part * PART).astype(F32), part.astype(F32), up_high)
    list_ref[...] = jnp.concatenate(
        [x[:, i * nz : (i + 1) * nz] for x in values for i in range(agents // nz)], axis=0
    )


def network_kernel(
    me_ref, slab_ref, species_ref, sensed_ref, death_ref, move_ref, route_ref, net_ref, sensing_ref, *outs
):
    agents, width = species_ref.shape
    depths = len(outs) - 2
    capacity = outs[0].shape[0] * 16
    species = species_ref[...]
    sensing = sensing_ref[...].reshape(1, width)
    first = sensing.astype(BF16)
    rest = sensing - first.astype(F32)
    second = rest.astype(BF16)
    third = (rest - second.astype(F32)).astype(BF16)
    line = iota((8, width), 0)
    terms = jnp.where(
        line == 0, first.astype(F32),
        jnp.where(line == 1, second.astype(F32), jnp.where(line == 2, third.astype(F32), 0.0)),
    ).astype(BF16)
    activation = dot(species, net_ref[...], 1, 0) + dot(sensed_ref[...].astype(BF16), terms, 0, 0)
    updated = (0.5 * species.astype(F32) + jnp.tanh(activation)).astype(BF16)
    lanes = 128
    lines = -(-(depths + 2) // 8) * 8
    line = iota((lines, lanes), 0)
    square = iota((lanes, 2 * lanes), 0)
    column = iota((lanes, 2 * lanes), 1)
    counter = jnp.where(jnp.logical_or(column >= lanes, square < column), 1.0, 0.0).astype(BF16)
    blocks = agents // lanes
    route = route_ref[...].reshape(1, agents)
    move = move_ref[...].reshape(1, agents)
    death = death_ref[...].reshape(1, agents)
    hits = []
    for block in range(blocks):
        cut = slice(block * lanes, (block + 1) * lanes)
        wanted = jnp.where(line < depths, route[:, cut], jnp.where(line < depths + 2, move[:, cut] + (depths - 1), -1))
        hits.append((wanted == line).astype(F32))
    counts = dot(jnp.concatenate(hits, axis=0).astype(BF16), counter, 1, 0)
    me = me_ref[0]
    to_a = jnp.where(is_even(slab_ref[0]), 1, 2)
    hop_a = jnp.where(is_even(me), 1, depths - 1)
    running = jnp.zeros((lines, lanes), F32)
    keys = []
    for block in range(blocks):
        cut = slice(block * lanes, (block + 1) * lanes)
        own = slice(block * lines, (block + 1) * lines)
        before = (counts[own, :lanes] + running) * hits[block]
        running = running + counts[own, lanes:]
        slot = jnp.sum(jnp.where(line < depths, before, 0.0), axis=0, keepdims=True).astype(jnp.int32)
        rank = jnp.sum(jnp.where(line < depths, 0.0, before), axis=0, keepdims=True).astype(jnp.int32)
        hop = route[:, cut] - me
        hop = jnp.where(hop < 0, hop + depths, hop)
        hop = jnp.where(hop == hop_a, 1, jnp.where(hop == depths - hop_a, 2, jnp.where(hop == 0, 0, hop + 1)))
        key = jnp.where(
            move[:, cut] == 0,
            hop * capacity + slot,
            depths * capacity + jnp.where(move[:, cut] == to_a, 0, MIG) + rank,
        )
        keys.append(jnp.where(death[:, cut] == 0, key, -1))
    key = jnp.concatenate(keys, axis=1)
    start = 0
    for index, out in enumerate(outs):
        size = capacity if index < depths else MIG
        chosen = (iota((size, agents), 0) == key - start).astype(F32).astype(BF16)
        placed = dot(chosen, updated, 1, 0).astype(BF16)
        start += size
        blocks = out.shape[0]
        for i in range(0, out.shape[2], width):
            part = placed[i // width * blocks * 16 :][: blocks * 16]
            out[:, :, i : i + width] = part.reshape(blocks, 16, width)


def tiles_of(x):
    return [x[:, i : i + LANES] for i in range(0, x.shape[1], LANES)]


def third_sum(x):
    parts = tiles_of(x)
    lane = iota((x.shape[0], LANES), 1)
    before = jnp.where(lane == 0, 0.0, pltpu.roll(parts[-1], 1, 1))
    after = jnp.where(lane == LANES - 1, 0.0, pltpu.roll(parts[0], LANES - 1, 1))
    padded = [before] + parts + [after]
    return jnp.concatenate([x + y for x, y in zip(padded[:-2], padded[2:])], axis=1)


def neighbour_total(before, plane, after):
    rows = plane.shape[0]
    second = pltpu.roll(plane, 1, 0) + pltpu.roll(plane, rows - 1, 0)
    return before + after + second + third_sum(plane)


def relaxed(before, plane, after, target, centre):
    return (1.0 - DAMPING) * plane + (DAMPING / centre) * (
        target + neighbour_total(before, plane, after)
    )


def edge_mask(me, depths, halo):
    row = iota((2 * halo, 1), 0)
    return jnp.where(
        row < halo, (me < depths - 1).astype(F32), (me > 0).astype(F32)
    )


def masked(plane, own, mask):
    return jnp.concatenate([plane[:own], plane[own:] * mask], axis=0)


def halo_rows(side_a, side_b, even, plane, mask):
    at = 2 * HALO * (plane % 2)
    side_a = side_a[at : at + 2 * HALO].astype(F32)
    side_b = side_b[at : at + 2 * HALO].astype(F32)
    high = jnp.where(even, side_a, side_b)
    low = jnp.where(even, side_b, side_a)
    return (
        jnp.concatenate([high[:HALO], low[:HALO]], axis=0) * mask,
        jnp.concatenate([high[HALO:], low[HALO:]], axis=0),
    )


def corner_kernel(me_ref, slab_ref, side_a, side_b, list_ref, slab_a, slab_b):
    layers = 2 * side_a.shape[0]
    nz = side_a.shape[2]
    even = is_even(me_ref[0])
    slab_even = is_even(slab_ref[0])

    def layer(side, plane):
        at = 2 * HALO * (plane % 2)
        return side[plane // 2].astype(F32)[at : at + 2 * HALO]

    for ref, front in ((slab_a, slab_even), (slab_b, jnp.logical_not(slab_even))):
        parts = []
        for side, high in ((side_a, even), (side_b, jnp.logical_not(even))):
            targets = []
            for i in range(1, HALO):
                x = jnp.where(front, layer(side, layers - i), layer(side, i - 1))
                parts.append(jnp.where(high, x[: HALO - i], x[i:HALO]))
                if i < HALO - 1:
                    targets.append(
                        jnp.where(high, x[HALO : 2 * HALO - 1 - i], x[HALO + 1 + i :])
                    )
            parts += targets
        parts.append(list_ref[...])
        used = sum(part.shape[0] for part in parts)
        total = ref.shape[0] * ref.shape[1]
        parts.append(jnp.zeros((total - used, nz), F32))
        ref[...] = jnp.concatenate(parts, axis=0).astype(BF16).reshape(ref.shape)


def corner_rows(block_a, block_b, even, mask):
    high = jnp.where(even, block_a, block_b)
    low = jnp.where(even, block_b, block_a)
    nz = high.shape[1]
    fields, targets = [], []
    at = 0
    for rows, out in ((HALO, fields), (HALO - 1, targets)):
        for i in range(1, rows):
            count = rows - i
            gap = jnp.zeros((2 * (HALO - count), nz), F32)
            cut = slice(at, at + count)
            out.append(jnp.concatenate([high[cut], gap, low[cut]], axis=0) * mask)
            at += count
    return fields, targets + [jnp.zeros_like(fields[0])]


KEEP, PULL = 1.0 - DAMPING, DAMPING / CENTRE


def inner_kernel(
    depths, me_ref, slab_ref, u_ref, t_ref, side_a, side_b, field_a, field_b, u0, text_ref, u1, u2_ref, inside
):
    nx, ny, nz = u_ref.shape
    even = is_even(me_ref[0])
    slab_even = is_even(slab_ref[0])
    half = ny // 16
    mask = edge_mask(me_ref[0], depths, HALO)
    for field, after in ((field_a, slab_even), (field_b, jnp.logical_not(slab_even))):
        u_at = jnp.where(after, HALO + nx, 0)
        for k in range(HALO):
            u0[u_at + k, :ny] = field[k * half : (k + 1) * half].astype(F32).reshape(ny, nz)
            u0[u_at + k, ny:] = jnp.zeros((2 * HALO, nz), F32)
    for plane in range(nx):
        u0[HALO + plane, :ny] = u_ref[plane]
        text_ref[HALO - 1 + plane, :ny] = t_ref[plane]
        uh, th = halo_rows(side_a[plane // 2], side_b[plane // 2], even, plane, mask)
        u0[HALO + plane, ny:] = uh
        text_ref[HALO - 1 + plane, ny:] = th

    def outer(i, carry):
        for p in (i, nx + HALO - 1 + i):
            u1[p] = KEEP * u0[p + 1] + PULL * neighbour_total(u0[p], u0[p + 1], u0[p + 2])
        return carry

    lax.fori_loop(0, HALO - 1, outer, 0)

    def first(p, carry):
        v = relaxed(u0[p], u0[p + 1], u0[p + 2], text_ref[p], CENTRE)
        u1[p] = masked(v, ny, mask)
        return carry

    lax.fori_loop(HALO - 1, nx + HALO - 1, first, 0, unroll=2)

    def second(p, carry):
        v = relaxed(u1[p], u1[p + 1], u1[p + 2], text_ref[p + 1], CENTRE)
        u2_ref[p] = masked(v, ny, mask)
        return carry

    lax.fori_loop(HALO - 1, nx + 1, second, 0, unroll=2)
    for p in range(2, nx - 2):
        inside[p - 2] = residual(u2_ref, text_ref, p, ny)


def residual(u2_ref, text_ref, p, ny):
    v = u2_ref[p + 2]
    total = neighbour_total(u2_ref[p + 1], v, u2_ref[p + 3])
    return (text_ref[p + 3] - CENTRE * v + total)[:ny]


def smooth_kernel(
    depths, agents, me_ref, slab_ref, u0, text_in, u1_in, u2_in, inside, slab_a, slab_b,
    text_ref, u1, u2_ref, coarse_ref, coarse_all_ref, coarse_a, coarse_b, paired, foreign,
):
    nx = u0.shape[0] - 2 * HALO
    ny, nz = u0.shape[1] - 2 * HALO, u0.shape[2]
    mask = edge_mask(me_ref[0], depths, HALO)
    even = is_even(me_ref[0])
    slab_even = is_even(slab_ref[0])
    near = HALO - 1
    corner = HALO * near // 2 + near * (near - 1) // 2
    row = iota((8, 1), 0)
    first, last = (row == 0).astype(F32), (row == 7).astype(F32)
    for ref, after in ((slab_a, slab_even), (slab_b, jnp.logical_not(slab_even))):
        message = ref[...].astype(F32).reshape(-1, nz)
        fields, targets = corner_rows(message[:corner], message[corner : 2 * corner], even, mask)
        sign = jnp.where(after, 1, -1)
        edge = jnp.where(after, nx - 1, 0)
        lines = agents // nz
        cell_row, place, part, uptake = (
            jnp.concatenate([message[at + i : at + i + 1] for i in range(lines)], axis=1)
            for at in range(2 * corner, 2 * corner + 4 * lines, lines)
        )
        cell_row = cell_row.astype(jnp.int32) - jnp.where(after, 0, (nx - near) * ny)
        wanted = jnp.logical_and(cell_row >= 0, cell_row < near * ny)
        key = jnp.where(wanted, part.astype(jnp.int32) * (near * ny) + cell_row, -1)
        one_z = (iota((PART, agents), 0) == place.astype(jnp.int32)).astype(F32).astype(BF16)
        key_rows = iota((near * ny * (nz // PART), agents), 0)
        taken = jnp.where(key_rows == key, uptake, 0.0).astype(BF16)
        source = dot(taken, one_z, 1, 1)
        for i in range(nz // PART):
            foreign[:, i * PART : (i + 1) * PART] = source[i * near * ny : (i + 1) * near * ny]
        for i in range(1, HALO):
            p = edge + sign * i
            index = jnp.where(after, i - 1, HALO - 1 - i)
            t = SCREENING * u0[p + 4, :ny] - foreign[pl.ds(index * ny, ny)]
            text_ref[p + 3, :ny] = t
            text_ref[p + 3, ny:] = targets[i - 1]
            x = fields[i - 1]
            nearer = u0[p + 4 - sign, ny:] if i == 1 else fields[i - 2]
            total = nearer + third_sum(x)
            if i < HALO - 1:
                total = total + fields[i]
            beyond = u0[p + 4]
            up = jnp.where(row == 0, beyond[ny - 1 : ny], pltpu.roll(x, 1, 0))
            down = jnp.where(row == 7, beyond[0:1], pltpu.roll(x, 7, 0))
            u1[p + 3, ny:] = (KEEP * x + PULL * (targets[i - 1] + total + up + down)) * mask
            v = u1[p + 3, :ny] + PULL * t
            u1[p + 3, :ny] = v
            u1[p + 3, 0:8] = v[0:8] + (PULL * first) * x[7:8]
            u1[p + 3, ny - 8 : ny] = v[ny - 8 :] + (PULL * last) * x[0:1]
        u1[edge + 3, ny:] = u1[edge + 3, ny:] + PULL * fields[0]
        u2_ref[edge - sign + 2, ny:] = u2_ref[edge - sign + 2, ny:] + (PULL * PULL) * fields[0]

    def second(i, carry):
        for p in (i, nx + 1 + i):
            v = relaxed(u1[p], u1[p + 1], u1[p + 2], text_ref[p + 1], CENTRE)
            u2_ref[p] = masked(v, ny, mask)
        return carry

    lax.fori_loop(0, HALO - 1, second, 0)
    for q in range(nx // 2):
        both = 0.0
        for p in (2 * q, 2 * q + 1):
            known = 2 <= p < nx - 2
            both = both + (inside[p - 2] if known else residual(u2_ref, text_ref, p, ny))
        parts = tiles_of(both)
        for i in range(len(parts) // 2):
            paired[q, i] = parts[2 * i] + parts[2 * i + 1]
    cx, cy, cz = coarse_ref.shape
    coarse = jnp.concatenate(
        [
            jnp.concatenate(
                [
                    paired[q, i, pl.ds(0, cy, 2), :] + paired[q, i, pl.ds(1, cy, 2), :]
                    for i in range(cz // LANES)
                ],
                axis=1,
            )
            for q in range(cx)
        ],
        axis=0,
    )
    coarse = 0.5 * coarse
    coarse_ref[...] = coarse.reshape(cx, cy, cz)
    coarse_all_ref[...] = coarse.astype(BF16).reshape(cx, cy, cz)
    low, high = (
        jnp.concatenate([coarse_ref[q, start : start + HALO] for q in range(cx)], axis=0)
        for start in (0, cy - HALO)
    )
    coarse_a[0] = jnp.where(even, high, low).astype(BF16)
    coarse_b[0] = jnp.where(even, low, high).astype(BF16)


def post_kernel(depths, me_ref, u2_ref, text_ref, out_ref, back_ref, v1):
    nx, ny, nz = out_ref.shape
    back = shuffle(nz, True)
    back_ref[...] = back
    mask = edge_mask(me_ref[0], depths, HALO)

    def first(p, carry):
        v = relaxed(u2_ref[p], u2_ref[p + 1], u2_ref[p + 2], text_ref[p + 2], CENTRE)
        v1[p] = masked(v, ny, mask)
        return carry

    lax.fori_loop(0, nx + 2, first, 0, unroll=2)

    def second(p, carry):
        v = relaxed(v1[p], v1[p + 1], v1[p + 2], text_ref[p + 3], CENTRE)
        out_ref[p] = v[:ny]
        return carry

    lax.fori_loop(0, nx, second, 0, unroll=2)
    high, low = halves(out_ref[...].reshape(nx * ny, nz))
    both = dot(jnp.concatenate([high, low], axis=0), back, 1, 0)
    out_ref[...] = (both[: nx * ny] + both[nx * ny :]).reshape(nx, ny, nz)


def correct_kernel(
    depths, me_ref, slab_ref, ct_ref, side_a, side_b, slab_a, slab_b, base_ref, back_ref, *rest
):
    packed = rest[: depths - 1]
    out_any, agents_ref, fine, out_ref, sem = rest[depths - 1 :]
    nx, ny, nz = out_ref.shape
    cx, cy, cz = ct_ref.shape
    me = me_ref[0]
    even = is_even(me)
    slab_even = is_even(slab_ref[0])
    blocks = packed[0].shape[0]
    width = agents_ref.shape[2]
    copies = []

    def place(source, start):
        target = agents_ref.at[pl.ds(start, source.shape[0])]
        copies.append(pltpu.make_async_copy(source, target, sem.at[len(copies)]))
        copies[-1].start()

    def place_wide(source, start):
        for i in range(source.shape[2] // width):
            part = source.at[:, :, pl.ds(i * width, width)]
            place(part, start + i * source.shape[0])

    up = jnp.where(me == depths - 1, 0, me + 1)
    down = jnp.where(me == 0, depths - 1, me - 1)
    place(packed[0], me * blocks)
    place_wide(side_a.at[pl.ds(1, side_a.shape[0] - 1)], jnp.where(even, up, down) * blocks)
    place(packed[1], jnp.where(even, down, up) * blocks)
    for k in range(2, depths - 1):
        origin = me - k
        place(packed[k], jnp.where(origin < 0, origin + depths, origin) * blocks)
    for ref, late in ((slab_a, slab_even), (slab_b, jnp.logical_not(slab_even))):
        start = depths * blocks + jnp.where(late, MIG // 16, 0)
        place_wide(ref.at[pl.ds(cx + 2, ref.shape[0] - cx - 2)], start)
    mask = edge_mask(me, depths, HALO)

    def chosen(condition, x, y):
        return jnp.where(condition, x.astype(F32), y.astype(F32))

    planes = []
    for p in range(cx + 2 * HALO):
        if HALO <= p < HALO + cx:
            k = p - HALO
            own, one, two = ct_ref[k], side_a[0].astype(F32), side_b[0].astype(F32)
        else:
            before = p < HALO
            k = p + cx - HALO if before else p - HALO - cx
            x, y = (slab_b, slab_a) if before else (slab_a, slab_b)
            own, one, two = (chosen(slab_even, x[i], y[i]) for i in (k, cx, cx + 1))
        rows = slice(HALO * k, HALO * (k + 1))
        one, two = one[rows], two[rows]
        sides = jnp.concatenate([jnp.where(even, one, two), jnp.where(even, two, one)], axis=0)
        planes.append(jnp.concatenate([own, sides * mask], axis=0))
    values = [(DAMPING / COARSE_CENTRE) * plane for plane in planes]
    for sweep in range(1, HALO):
        values = [
            masked(
                relaxed(values[i - 1], values[i], values[i + 1], planes[i + sweep - 1], COARSE_CENTRE),
                cy,
                mask,
            )
            for i in range(1, len(values) - 1)
        ]
    wide = cy + 4
    for q, value in enumerate(values):
        value = jnp.concatenate([value[: cy + 2], value[cy + 2 * HALO - 2 :]], axis=0)
        for i, part in enumerate(tiles_of(value)):
            fine[q, i, pl.ds(0, wide, 2), :] = part
            fine[q, i, pl.ds(1, wide, 2), :] = part
    def second_total(plane):
        rows = plane.shape[0]
        return pltpu.roll(plane, 1, 0) + pltpu.roll(plane, rows - 1, 0)

    spread = [jnp.concatenate([fine[q, i] for i in range(cz // LANES)], axis=1) for q in range(cx + 2)]
    still = [KEEP * plane + PULL * second_total(plane) for plane in spread]
    once = []
    for p in range(-1, nx + 1):
        q = (p + 2) // 2
        if p % 2 == 0:
            others = spread[q - 1] + spread[q]
        else:
            others = spread[q] + spread[q + 1]
        once.append(masked(still[q] + PULL * others, ny, mask))

    def twice(plane):
        return jnp.concatenate([part for part in tiles_of(plane) for _ in range(2)], axis=1)

    back = back_ref[...]
    step = 4
    for start in range(0, nx, step):
        planes = []
        for p in range(start, start + step):
            plane = once[p + 1]
            total = once[p] + once[p + 2] + second_total(plane)
            none = (KEEP * plane + PULL * total)[:ny]
            one = (2.0 * PULL) * plane[:ny]
            two = (PULL * PULL) * spread[(p + 2) // 2][:ny]
            planes.append(twice(none) + third_sum(twice(one) + third_sum(twice(two))))
        done = dot(jnp.concatenate(planes, axis=0).astype(BF16), back, 1, 0)
        out_ref[start : start + step] = base_ref[start : start + step] + done.reshape(step, ny, nz)
        cut = pl.ds(start, step)
        copies.append(pltpu.make_async_copy(out_ref.at[cut], out_any.at[cut], sem.at[len(copies)]))
        copies[-1].start()
    for copy in copies:
        copy.wait()


def local(
    nutrient, species, agent_cell, death_flag, divide_flag, slab_move, depth_route, net_weight, sensing, uptake_weight
):
    depths = lax.axis_size("depth")
    nx, ny, nz = nutrient.shape
    agents, width = species.shape
    capacity = 2 * agents // depths
    me = lax.axis_index("depth").astype(jnp.int32).reshape(1)
    slab = lax.axis_index("slab").astype(jnp.int32).reshape(1)
    shape = jax.ShapeDtypeStruct
    cells, death, divide = (x.reshape(1, agents) for x in (agent_cell, death_flag, divide_flag))
    move, route = slab_move.reshape(1, agents), depth_route.reshape(1, agents)
    half = ny // 16
    if agents % nz or nx * ny > PART or nz % PART or depths < 4:
        raise ValueError("list digits")
    arguments = (
        cells, nutrient, divide, uptake_weight.reshape(1, width), species, death,
        move, route, net_weight, sensing.reshape(1, width),
    )
    (
        nutrient, places, field_a, field_b, cells, divide, weight, species, death, move, route, net_weight, sensing
    ) = pl.pallas_call(
        load_kernel,
        out_shape=(
            shape((nx, ny, nz), F32),
            shape((nz, agents), BF16),
            shape((HALO * half, 16, nz), BF16),
            shape((HALO * half, 16, nz), BF16),
        )
        + tuple(shape(x.shape, x.dtype) for i, x in enumerate(arguments) if i != 1),
        in_specs=[SMEM_SPEC] + [HBM_SPEC] * len(arguments),
        out_specs=[VMEM_SPEC] * (4 + len(arguments) - 1),
        scratch_shapes=[
            pltpu.VMEM((nx, ny, nz), F32),
            pltpu.SemaphoreType.DMA((len(arguments),)),
        ],
        compiler_params=PARAMS,
        name="load",
    )(slab, *(pltpu.with_memory_space_constraint(x, pltpu.HBM) for x in arguments))
    target, sensed, depth_a, depth_b, agent_list = pl.pallas_call(
        uptake_kernel,
        out_shape=(
            shape((nx, ny, nz), F32),
            shape((8, agents), F32),
            shape((nx // 2, 16, nz), BF16),
            shape((nx // 2, 16, nz), BF16),
            shape((4 * agents // nz, nz), F32),
        ),
        in_specs=[SMEM_SPEC] + [VMEM_SPEC] * 7,
        out_specs=[VMEM_SPEC] * 5,
        compiler_params=PARAMS,
        cost_estimate=pl.CostEstimate(flops=1 << 31, bytes_accessed=1 << 20, transcendentals=0),
        name="uptake",
    )(me, nutrient, places, cells, divide, weight, species, death)
    field_a, field_b, depth_a, depth_b = lax.optimization_barrier((field_a, field_b, depth_a, depth_b))
    side_a = swapped(depth_a, "depth", "a")
    side_b = swapped(depth_b, "depth", "b")
    field_a = swapped(field_a, "slab", "a")
    field_b = swapped(field_b, "slab", "b")
    rows = 2 * (HALO - 1) ** 2 + agent_list.shape[0]
    rows = -(-rows // 16) * 16
    slab_a, slab_b = pl.pallas_call(
        corner_kernel,
        out_shape=tuple(shape((rows // 16, 16, nz), BF16) for _ in range(2)),
        in_specs=[SMEM_SPEC] * 2 + [VMEM_SPEC] * 3,
        out_specs=[VMEM_SPEC] * 2,
        compiler_params=PARAMS,
        name="corner",
    )(me, slab, side_a, side_b, agent_list)
    slab_a = swapped(slab_a, "slab", "a")
    slab_b = swapped(slab_b, "slab", "b")
    cx, cy, cz = nx // 2, ny // 2, nz // 2
    ext = ny + 2 * HALO
    sent = pl.pallas_call(
        network_kernel,
        out_shape=tuple(
            shape((capacity // 32, 16, 2 * width) if k == 1 else (capacity // 16, 16, width), BF16)
            for k in range(depths)
        )
        + tuple(shape((MIG * width // (16 * cz), 16, cz), BF16) for _ in range(2)),
        in_specs=[SMEM_SPEC] * 2 + [VMEM_SPEC] * 7,
        out_specs=[VMEM_SPEC] * (depths + 2),
        compiler_params=PARAMS,
        cost_estimate=pl.CostEstimate(flops=1 << 31, bytes_accessed=1<<20, transcendentals=0),
        name="network",
    )(me, slab, species, sensed, death, move, route, net_weight, sensing)
    u0, text, u1, u2, inside = pl.pallas_call(
        functools.partial(inner_kernel, depths),
        out_shape=(
            shape((nx + 2 * HALO, ext, nz), F32),
            shape((nx + 2 * HALO - 2, ext, nz), F32),
            shape((nx + 2 * HALO - 2, ext, nz), F32),
            shape((nx + 4, ext, nz), F32),
            shape((nx - 4, ny, nz), F32),
        ),
        in_specs=[SMEM_SPEC] * 2 + [VMEM_SPEC] * 6,
        out_specs=[VMEM_SPEC] * 5,
        compiler_params=PARAMS,
        cost_estimate=pl.CostEstimate(flops=1 << 20, bytes_accessed=1<<20, transcendentals=0),
        name="inner",
    )(me, slab, nutrient, target, side_a, side_b, field_a, field_b)
    slab_a, slab_b, inside, *sent = lax.optimization_barrier((slab_a, slab_b, inside, *sent))
    text, _, u2, ct, ct_all, coarse_a, coarse_b = pl.pallas_call(
        functools.partial(smooth_kernel, depths, agents),
        out_shape=(
            shape(text.shape, F32),
            shape(u1.shape, F32),
            shape(u2.shape, F32),
            shape((cx, cy, cz), F32),
            shape((cx, cy, cz), BF16),
            shape((1, cx * HALO, cz), BF16),
            shape((1, cx * HALO, cz), BF16),
        ),
        in_specs=[SMEM_SPEC] * 2 + [VMEM_SPEC] * 7,
        out_specs=[VMEM_SPEC] * 7,
        scratch_shapes=[
            pltpu.VMEM((cx, cz // LANES, ny, LANES), F32),
            pltpu.VMEM(((HALO - 1) * ny, nz), F32),
        ],
        input_output_aliases={3: 0, 4: 1, 5: 2},
        compiler_params=PARAMS,
        name="smooth",
    )(me, slab, u0, text, u1, u2, inside, slab_a, slab_b)
    coarse_a = swapped(jnp.concatenate([coarse_a, sent[1]], axis=0), "depth", "a")
    coarse_b = swapped(coarse_b, "depth", "b")
    arrived = [sent[0], swapped(sent[2], "depth", "b")]
    arrived += [cyclic(sent[k + 1], "depth", k) for k in range(2, depths - 1)]
    tail_a, tail_b = (
        swapped(jnp.concatenate([ct_all, coarse_a[:1], coarse_b, movers], axis=0), "slab", which)
        for which, movers in (("a", sent[depths]), ("b", sent[depths + 1]))
    )
    base, back = pl.pallas_call(
        functools.partial(post_kernel, depths),
        out_shape=(shape((nx, ny, nz), F32), shape((nz, nz), BF16)),
        in_specs=[SMEM_SPEC] + [VMEM_SPEC] * 2,
        out_specs=[VMEM_SPEC] * 2,
        scratch_shapes=[pltpu.VMEM((nx + 2, ext, nz), F32)],
        compiler_params=PARAMS,
        cost_estimate=pl.CostEstimate(flops=1 << 30, bytes_accessed=1 << 22, transcendentals=0),
        name="post",
    )(me, u2, text)
    grid_field, agents_out = pl.pallas_call(
        functools.partial(correct_kernel, depths),
        out_shape=(
            shape((nx, ny, nz), F32),
            shape(((depths * capacity + 2 * MIG) // 16, 16, width), BF16),
        ),
        in_specs=[SMEM_SPEC] * 2 + [VMEM_SPEC] * 7 + [ANY_SPEC] * (depths - 1),
        out_specs=[HBM_SPEC, ANY_SPEC],
        scratch_shapes=[
            pltpu.VMEM((cx + 2, cz // LANES, ext, LANES), F32),
            pltpu.VMEM((nx, ny, nz), F32),
            pltpu.SemaphoreType.DMA((depths + 5 + nx,)),
        ],
        compiler_params=PARAMS,
        name="correct",
    )(me, slab, ct, coarse_a, coarse_b, tail_a, tail_b, base, back, *arrived)
    return grid_field, agents_out.reshape(-1, width)


def solution(mesh):
    rows = P(("slab", "depth"))
    in_specs = (
        P("slab", "depth", None),
        P(("slab", "depth"), None),
        rows,
        rows,
        rows,
        rows,
        P(("slab", "depth"), None),
        P(),
        P(),
        P(),
    )
    out_specs = (P("slab", "depth", None), P(("slab", "depth"), None))
    return jax.shard_map(local, mesh=mesh, in_specs=in_specs, out_specs=out_specs, check_vma=False)
```

```python
import functools

import jax
import jax.numpy as jnp
from jax import lax
from jax.experimental import pallas as pl
from jax.experimental.pallas import tpu as pltpu
from jax.sharding import PartitionSpec as P

MIG = 128
PART = 256
SCREENING = 0.05
DAMPING = 2.0 / 3.0
CENTRE = 6.0 + SCREENING
COARSE_CENTRE = 6.0 + 4.0 * SCREENING
HALO = 4
F32, BF16 = jnp.float32, jnp.bfloat16
VMEM_SPEC = pl.BlockSpec(memory_space=pltpu.VMEM)
ANY_SPEC = pl.BlockSpec(memory_space=pl.ANY)
HBM_SPEC = pl.BlockSpec(memory_space=pltpu.HBM)
SMEM_SPEC = pl.BlockSpec(memory_space=pltpu.SMEM)
PARAMS = pltpu.CompilerParams(vmem_limit_bytes=40 * 1024 * 1024)


def dot(a, b, ca, cb):
    return lax.dot_general(a, b, (((ca,), (cb,)), ((), ())), preferred_element_type=F32)


def halves(x):
    high = x.astype(BF16)
    return high, (x - high.astype(F32)).astype(BF16)


def iota(shape, dim):
    return lax.broadcasted_iota(jnp.int32, shape, dim)


def cyclic(x, axis, by):
    count = lax.axis_size(axis)
    return lax.ppermute(x, axis, [(i, (i + by) % count) for i in range(count)])


def swapped(x, axis, which):
    count = lax.axis_size(axis)
    if count % 2:
        raise ValueError("odd axis")
    first = 0 if which == "a" else 1
    pairs = []
    for i in range(first, count, 2):
        j = (i + 1) % count
        pairs += [(i, j), (j, i)]
    return lax.ppermute(x, axis, sorted(pairs))


def is_even(x):
    return lax.rem(x, 2) == 0


LANES = 128


def shuffle(nz, back):
    one, two = iota((nz, nz), 0), iota((nz, nz), 1)
    if back:
        one, two = two, one
    return (one == (two % LANES) * (nz // LANES) + two // LANES).astype(F32).astype(BF16)


def load_kernel(slab_ref, *refs):
    count = 10
    sources, refs = refs[:count], refs[count:]
    u_ref, place_ref, field_a, field_b, *targets = refs[:-2]
    raw, sem = refs[-2:]
    cell_ref = targets[0]
    targets.insert(1, raw)
    copies = [
        pltpu.make_async_copy(source, target, sem.at[i])
        for i, (source, target) in enumerate(zip(sources, targets, strict=True))
    ]
    for copy in copies:
        copy.start()
    nx, ny, nz = u_ref.shape
    rows = nx * ny
    tiles = nz // LANES
    order = shuffle(nz, False)
    copies[0].wait()
    cell_z = cell_ref[...] % nz
    cell_z = (cell_z % tiles) * LANES + cell_z // tiles
    place_ref[...] = (iota(place_ref.shape, 0) == cell_z).astype(F32).astype(BF16)
    copies[1].wait()
    high, low = halves(raw[...].reshape(rows, nz))
    both = dot(jnp.concatenate([high, low], axis=0), order, 1, 0)
    u_ref[...] = (both[:rows] + both[rows:]).reshape(nx, ny, nz)
    half = ny // 16
    slab_even = is_even(slab_ref[0])
    for ref, front in ((field_a, slab_even), (field_b, jnp.logical_not(slab_even))):
        start = jnp.where(front, nx - HALO, 0)
        for k in range(HALO):
            ref[k * half : (k + 1) * half] = u_ref[start + k].astype(BF16).reshape(half, 16, nz)
    for copy in copies[2:]:
        copy.wait()


def uptake_kernel(
    me_ref, u_ref, place_ref, cell_ref, divide_ref, weight_ref, species_ref, death_ref,
    t_ref, sensed_ref, depth_a, depth_b, list_ref,
):
    nx, ny, nz = u_ref.shape
    agents = species_ref.shape[0]
    rows = nx * ny
    tiles = nz // LANES
    cell = cell_ref[...]
    cell_row = cell // nz
    cell_z = cell - cell_row * nz
    cell_z = (cell_z % tiles) * LANES + cell_z // tiles
    one_z = place_ref[...]
    in_row = iota((rows, agents), 0) == cell_row
    u = u_ref[...].reshape(rows, nz)
    picked = dot(u.astype(BF16), one_z, 1, 0)
    sample = jnp.sum(jnp.where(in_row, picked, 0.0), axis=0, keepdims=True)
    sensed_ref[...] = jnp.broadcast_to(sample, (8, agents))
    weight = jnp.broadcast_to(weight_ref[...].reshape(1, -1), (8, species_ref.shape[1]))
    score = dot(weight, species_ref[...], 1, 1)[0:1]
    softplus = jnp.maximum(score, 0.0) + jnp.log1p(jnp.exp(-jnp.abs(score)))
    alive = (1 - death_ref[...].reshape(1, agents)).astype(F32)
    divide = divide_ref[...].reshape(1, agents).astype(F32)
    uptake = alive * (1.0 + divide) * softplus * sample / (0.5 + sample)
    up_high = uptake.astype(BF16).astype(F32)
    source = dot(jnp.where(in_row, up_high, 0.0).astype(BF16), one_z, 1, 1)
    t_ref[...] = (SCREENING * u - source).reshape(nx, ny, nz)
    even = is_even(me_ref[0])
    for pair in range(nx // 2):
        parts = []
        for start in (0, ny - HALO):
            for plane in (2 * pair, 2 * pair + 1):
                parts.append(u_ref[plane, start : start + HALO])
                parts.append(t_ref[plane, start : start + HALO])
        low = jnp.concatenate(parts[:4], axis=0)
        high = jnp.concatenate(parts[4:], axis=0)
        depth_a[pair] = jnp.where(even, high, low).astype(BF16)
        depth_b[pair] = jnp.where(even, low, high).astype(BF16)
    part = cell_z // PART
    values = (cell_row.astype(F32), (cell_z - part * PART).astype(F32), part.astype(F32), up_high)
    list_ref[...] = jnp.concatenate(
        [x[:, i * nz : (i + 1) * nz] for x in values for i in range(agents // nz)], axis=0
    )


def network_kernel(
    me_ref, slab_ref, species_ref, sensed_ref, death_ref, move_ref, route_ref, net_ref, sensing_ref, *outs
):
    agents, width = species_ref.shape
    depths = len(outs) - 2
    capacity = outs[0].shape[0] * 16
    species = species_ref[...]
    sensing = sensing_ref[...].reshape(1, width)
    first = sensing.astype(BF16)
    rest = sensing - first.astype(F32)
    second = rest.astype(BF16)
    third = (rest - second.astype(F32)).astype(BF16)
    line = iota((8, width), 0)
    terms = jnp.where(
        line == 0, first.astype(F32),
        jnp.where(line == 1, second.astype(F32), jnp.where(line == 2, third.astype(F32), 0.0)),
    ).astype(BF16)
    activation = dot(species, net_ref[...], 1, 0) + dot(sensed_ref[...].astype(BF16), terms, 0, 0)
    updated = (0.5 * species.astype(F32) + jnp.tanh(activation)).astype(BF16)
    lanes = 128
    lines = -(-(depths + 2) // 8) * 8
    line = iota((lines, lanes), 0)
    square = iota((lanes, 2 * lanes), 0)
    column = iota((lanes, 2 * lanes), 1)
    counter = jnp.where(jnp.logical_or(column >= lanes, square < column), 1.0, 0.0).astype(BF16)
    blocks = agents // lanes
    route = route_ref[...].reshape(1, agents)
    move = move_ref[...].reshape(1, agents)
    death = death_ref[...].reshape(1, agents)
    hits = []
    for block in range(blocks):
        cut = slice(block * lanes, (block + 1) * lanes)
        wanted = jnp.where(line < depths, route[:, cut], jnp.where(line < depths + 2, move[:, cut] + (depths - 1), -1))
        hits.append((wanted == line).astype(F32))
    counts = dot(jnp.concatenate(hits, axis=0).astype(BF16), counter, 1, 0)
    me = me_ref[0]
    to_a = jnp.where(is_even(slab_ref[0]), 1, 2)
    hop_a = jnp.where(is_even(me), 1, depths - 1)
    running = jnp.zeros((lines, lanes), F32)
    keys = []
    for block in range(blocks):
        cut = slice(block * lanes, (block + 1) * lanes)
        own = slice(block * lines, (block + 1) * lines)
        before = (counts[own, :lanes] + running) * hits[block]
        running = running + counts[own, lanes:]
        slot = jnp.sum(jnp.where(line < depths, before, 0.0), axis=0, keepdims=True).astype(jnp.int32)
        rank = jnp.sum(jnp.where(line < depths, 0.0, before), axis=0, keepdims=True).astype(jnp.int32)
        hop = route[:, cut] - me
        hop = jnp.where(hop < 0, hop + depths, hop)
        hop = jnp.where(hop == hop_a, 1, jnp.where(hop == depths - hop_a, 2, jnp.where(hop == 0, 0, hop + 1)))
        key = jnp.where(
            move[:, cut] == 0,
            hop * capacity + slot,
            depths * capacity + jnp.where(move[:, cut] == to_a, 0, MIG) + rank,
        )
        keys.append(jnp.where(death[:, cut] == 0, key, -1))
    key = jnp.concatenate(keys, axis=1)
    start = 0
    for index, out in enumerate(outs):
        size = capacity if index < depths else MIG
        chosen = (iota((size, agents), 0) == key - start).astype(F32).astype(BF16)
        placed = dot(chosen, updated, 1, 0).astype(BF16)
        start += size
        blocks = out.shape[0]
        for i in range(0, out.shape[2], width):
            part = placed[i // width * blocks * 16 :][: blocks * 16]
            out[:, :, i : i + width] = part.reshape(blocks, 16, width)


def tiles_of(x):
    return [x[:, i : i + LANES] for i in range(0, x.shape[1], LANES)]


def third_sum(x):
    parts = tiles_of(x)
    lane = iota((x.shape[0], LANES), 1)
    before = jnp.where(lane == 0, 0.0, pltpu.roll(parts[-1], 1, 1))
    after = jnp.where(lane == LANES - 1, 0.0, pltpu.roll(parts[0], LANES - 1, 1))
    padded = [before] + parts + [after]
    return jnp.concatenate([x + y for x, y in zip(padded[:-2], padded[2:])], axis=1)


def neighbour_total(before, plane, after):
    rows = plane.shape[0]
    second = pltpu.roll(plane, 1, 0) + pltpu.roll(plane, rows - 1, 0)
    return before + after + second + third_sum(plane)


def relaxed(before, plane, after, target, centre):
    return (1.0 - DAMPING) * plane + (DAMPING / centre) * (
        target + neighbour_total(before, plane, after)
    )


def edge_mask(me, depths, halo):
    row = iota((2 * halo, 1), 0)
    return jnp.where(
        row < halo, (me < depths - 1).astype(F32), (me > 0).astype(F32)
    )


def masked(plane, own, mask):
    return jnp.concatenate([plane[:own], plane[own:] * mask], axis=0)


def halo_rows(side_a, side_b, even, plane, mask):
    at = 2 * HALO * (plane % 2)
    side_a = side_a[at : at + 2 * HALO].astype(F32)
    side_b = side_b[at : at + 2 * HALO].astype(F32)
    high = jnp.where(even, side_a, side_b)
    low = jnp.where(even, side_b, side_a)
    return (
        jnp.concatenate([high[:HALO], low[:HALO]], axis=0) * mask,
        jnp.concatenate([high[HALO:], low[HALO:]], axis=0),
    )


def corner_kernel(me_ref, slab_ref, side_a, side_b, list_ref, slab_a, slab_b):
    layers = 2 * side_a.shape[0]
    nz = side_a.shape[2]
    even = is_even(me_ref[0])
    slab_even = is_even(slab_ref[0])

    def layer(side, plane):
        at = 2 * HALO * (plane % 2)
        return side[plane // 2].astype(F32)[at : at + 2 * HALO]

    for ref, front in ((slab_a, slab_even), (slab_b, jnp.logical_not(slab_even))):
        parts = []
        for side, high in ((side_a, even), (side_b, jnp.logical_not(even))):
            targets = []
            for i in range(1, HALO):
                x = jnp.where(front, layer(side, layers - i), layer(side, i - 1))
                parts.append(jnp.where(high, x[: HALO - i], x[i:HALO]))
                if i < HALO - 1:
                    targets.append(
                        jnp.where(high, x[HALO : 2 * HALO - 1 - i], x[HALO + 1 + i :])
                    )
            parts += targets
        parts.append(list_ref[...])
        used = sum(part.shape[0] for part in parts)
        total = ref.shape[0] * ref.shape[1]
        parts.append(jnp.zeros((total - used, nz), F32))
        ref[...] = jnp.concatenate(parts, axis=0).astype(BF16).reshape(ref.shape)


def corner_rows(block_a, block_b, even, mask):
    high = jnp.where(even, block_a, block_b)
    low = jnp.where(even, block_b, block_a)
    nz = high.shape[1]
    fields, targets = [], []
    at = 0
    for rows, out in ((HALO, fields), (HALO - 1, targets)):
        for i in range(1, rows):
            count = rows - i
            gap = jnp.zeros((2 * (HALO - count), nz), F32)
            cut = slice(at, at + count)
            out.append(jnp.concatenate([high[cut], gap, low[cut]], axis=0) * mask)
            at += count
    return fields, targets + [jnp.zeros_like(fields[0])]


KEEP, PULL = 1.0 - DAMPING, DAMPING / CENTRE


def inner_kernel(
    depths, me_ref, slab_ref, u_ref, t_ref, side_a, side_b, field_a, field_b, u0, text_ref, u1, u2_ref, inside
):
    nx, ny, nz = u_ref.shape
    even = is_even(me_ref[0])
    slab_even = is_even(slab_ref[0])
    half = ny // 16
    mask = edge_mask(me_ref[0], depths, HALO)
    for field, after in ((field_a, slab_even), (field_b, jnp.logical_not(slab_even))):
        u_at = jnp.where(after, HALO + nx, 0)
        for k in range(HALO):
            u0[u_at + k, :ny] = field[k * half : (k + 1) * half].astype(F32).reshape(ny, nz)
            u0[u_at + k, ny:] = jnp.zeros((2 * HALO, nz), F32)
    for plane in range(nx):
        u0[HALO + plane, :ny] = u_ref[plane]
        text_ref[HALO - 1 + plane, :ny] = t_ref[plane]
        uh, th = halo_rows(side_a[plane // 2], side_b[plane // 2], even, plane, mask)
        u0[HALO + plane, ny:] = uh
        text_ref[HALO - 1 + plane, ny:] = th

    def outer(i, carry):
        for p in (i, nx + HALO - 1 + i):
            u1[p] = KEEP * u0[p + 1] + PULL * neighbour_total(u0[p], u0[p + 1], u0[p + 2])
        return carry

    lax.fori_loop(0, HALO - 1, outer, 0)

    def first(p, carry):
        v = relaxed(u0[p], u0[p + 1], u0[p + 2], text_ref[p], CENTRE)
        u1[p] = masked(v, ny, mask)
        return carry

    lax.fori_loop(HALO - 1, nx + HALO - 1, first, 0, unroll=2)

    def second(p, carry):
        v = relaxed(u1[p], u1[p + 1], u1[p + 2], text_ref[p + 1], CENTRE)
        u2_ref[p] = masked(v, ny, mask)
        return carry

    lax.fori_loop(HALO - 1, nx + 1, second, 0, unroll=2)
    for p in range(2, nx - 2):
        inside[p - 2] = residual(u2_ref, text_ref, p, ny)


def residual(u2_ref, text_ref, p, ny):
    v = u2_ref[p + 2]
    total = neighbour_total(u2_ref[p + 1], v, u2_ref[p + 3])
    return (text_ref[p + 3] - CENTRE * v + total)[:ny]


def smooth_kernel(
    depths, agents, me_ref, slab_ref, u0, text_in, u1_in, u2_in, inside, slab_a, slab_b,
    text_ref, u1, u2_ref, coarse_ref, coarse_all_ref, coarse_a, coarse_b, paired, foreign,
):
    nx = u0.shape[0] - 2 * HALO
    ny, nz = u0.shape[1] - 2 * HALO, u0.shape[2]
    mask = edge_mask(me_ref[0], depths, HALO)
    even = is_even(me_ref[0])
    slab_even = is_even(slab_ref[0])
    near = HALO - 1
    corner = HALO * near // 2 + near * (near - 1) // 2
    row = iota((8, 1), 0)
    first, last = (row == 0).astype(F32), (row == 7).astype(F32)
    sides = ((slab_a, slab_even), (slab_b, jnp.logical_not(slab_even)))
    messages = []
    lines = agents // nz
    for side, (ref, after) in enumerate(sides):
        message = ref[...].astype(F32).reshape(-1, nz)
        messages.append(message)
        cell_row, place, part, uptake = (
            jnp.concatenate([message[at + i : at + i + 1] for i in range(lines)], axis=1)
            for at in range(2 * corner, 2 * corner + 4 * lines, lines)
        )
        cell_row = cell_row.astype(jnp.int32) - jnp.where(after, 0, (nx - near) * ny)
        wanted = jnp.logical_and(cell_row >= 0, cell_row < near * ny)
        key = jnp.where(wanted, part.astype(jnp.int32) * (near * ny) + cell_row, -1)
        one_z = (iota((PART, agents), 0) == place.astype(jnp.int32)).astype(F32).astype(BF16)
        key_rows = iota((near * ny * (nz // PART), agents), 0)
        taken = jnp.where(key_rows == key, uptake, 0.0).astype(BF16)
        source = dot(taken, one_z, 1, 1)
        for i in range(nz // PART):
            foreign[side, :, i * PART : (i + 1) * PART] = source[i * near * ny : (i + 1) * near * ny]
    for side, (_, after) in enumerate(sides):
        message = messages[side]
        fields, targets = corner_rows(message[:corner], message[corner : 2 * corner], even, mask)
        sign = jnp.where(after, 1, -1)
        edge = jnp.where(after, nx - 1, 0)
        for i in range(1, HALO):
            p = edge + sign * i
            index = jnp.where(after, i - 1, HALO - 1 - i)
            t = SCREENING * u0[p + 4, :ny] - foreign[side, pl.ds(index * ny, ny)]
            text_ref[p + 3, :ny] = t
            text_ref[p + 3, ny:] = targets[i - 1]
            x = fields[i - 1]
            nearer = u0[p + 4 - sign, ny:] if i == 1 else fields[i - 2]
            total = nearer + third_sum(x)
            if i < HALO - 1:
                total = total + fields[i]
            beyond = u0[p + 4]
            up = jnp.where(row == 0, beyond[ny - 1 : ny], pltpu.roll(x, 1, 0))
            down = jnp.where(row == 7, beyond[0:1], pltpu.roll(x, 7, 0))
            u1[p + 3, ny:] = (KEEP * x + PULL * (targets[i - 1] + total + up + down)) * mask
            v = u1[p + 3, :ny] + PULL * t
            u1[p + 3, :ny] = v
            u1[p + 3, 0:8] = v[0:8] + (PULL * first) * x[7:8]
            u1[p + 3, ny - 8 : ny] = v[ny - 8 :] + (PULL * last) * x[0:1]
        u1[edge + 3, ny:] = u1[edge + 3, ny:] + PULL * fields[0]
        u2_ref[edge - sign + 2, ny:] = u2_ref[edge - sign + 2, ny:] + (PULL * PULL) * fields[0]

    def second(i, carry):
        for p in (i, nx + 1 + i):
            v = relaxed(u1[p], u1[p + 1], u1[p + 2], text_ref[p + 1], CENTRE)
            u2_ref[p] = masked(v, ny, mask)
        return carry

    lax.fori_loop(0, HALO - 1, second, 0)
    for q in range(nx // 2):
        both = 0.0
        for p in (2 * q, 2 * q + 1):
            known = 2 <= p < nx - 2
            both = both + (inside[p - 2] if known else residual(u2_ref, text_ref, p, ny))
        parts = tiles_of(both)
        for i in range(len(parts) // 2):
            paired[q, i, :ny] = parts[2 * i] + parts[2 * i + 1]
    cx, cy, cz = coarse_ref.shape
    coarse = jnp.concatenate(
        [
            jnp.concatenate(
                [
                    paired[q, i, pl.ds(0, cy, 2), :] + paired[q, i, pl.ds(1, cy, 2), :]
                    for i in range(cz // LANES)
                ],
                axis=1,
            )
            for q in range(cx)
        ],
        axis=0,
    )
    coarse = 0.5 * coarse
    coarse_ref[...] = coarse.reshape(cx, cy, cz)
    coarse_all_ref[...] = coarse.astype(BF16).reshape(cx, cy, cz)
    low, high = (
        jnp.concatenate([coarse_ref[q, start : start + HALO] for q in range(cx)], axis=0)
        for start in (0, cy - HALO)
    )
    coarse_a[0] = jnp.where(even, high, low).astype(BF16)
    coarse_b[0] = jnp.where(even, low, high).astype(BF16)


def post_kernel(depths, me_ref, u2_ref, text_ref, out_ref, back_ref, v1):
    nx, ny, nz = out_ref.shape
    back = shuffle(nz, True)
    back_ref[...] = back
    mask = edge_mask(me_ref[0], depths, HALO)

    def first(p, carry):
        v = relaxed(u2_ref[p], u2_ref[p + 1], u2_ref[p + 2], text_ref[p + 2], CENTRE)
        v1[p] = masked(v, ny, mask)
        return carry

    lax.fori_loop(0, nx + 2, first, 0, unroll=2)

    def second(p, carry):
        v = relaxed(v1[p], v1[p + 1], v1[p + 2], text_ref[p + 3], CENTRE)
        out_ref[p] = v[:ny]
        return carry

    lax.fori_loop(0, nx, second, 0, unroll=2)
    high, low = halves(out_ref[...].reshape(nx * ny, nz))
    both = dot(jnp.concatenate([high, low], axis=0), back, 1, 0)
    out_ref[...] = (both[: nx * ny] + both[nx * ny :]).reshape(nx, ny, nz)


def correct_kernel(
    depths, me_ref, slab_ref, ct_ref, side_a, side_b, slab_a, slab_b, base_ref, back_ref, *rest
):
    packed = rest[: depths - 1]
    out_any, agents_ref, fine, out_ref, sem = rest[depths - 1 :]
    nx, ny, nz = out_ref.shape
    cx, cy, cz = ct_ref.shape
    me = me_ref[0]
    even = is_even(me)
    slab_even = is_even(slab_ref[0])
    blocks = packed[0].shape[0]
    width = agents_ref.shape[2]
    copies = []

    def place(source, start):
        target = agents_ref.at[pl.ds(start, source.shape[0])]
        copies.append(pltpu.make_async_copy(source, target, sem.at[len(copies)]))
        copies[-1].start()

    def place_wide(source, start):
        for i in range(source.shape[2] // width):
            part = source.at[:, :, pl.ds(i * width, width)]
            place(part, start + i * source.shape[0])

    up = jnp.where(me == depths - 1, 0, me + 1)
    down = jnp.where(me == 0, depths - 1, me - 1)
    place(packed[0], me * blocks)
    place_wide(side_a.at[pl.ds(1, side_a.shape[0] - 1)], jnp.where(even, up, down) * blocks)
    place(packed[1], jnp.where(even, down, up) * blocks)
    for k in range(2, depths - 1):
        origin = me - k
        place(packed[k], jnp.where(origin < 0, origin + depths, origin) * blocks)
    for ref, late in ((slab_a, slab_even), (slab_b, jnp.logical_not(slab_even))):
        start = depths * blocks + jnp.where(late, MIG // 16, 0)
        place_wide(ref.at[pl.ds(cx + 2, ref.shape[0] - cx - 2)], start)
    mask = edge_mask(me, depths, HALO)

    def chosen(condition, x, y):
        return jnp.where(condition, x.astype(F32), y.astype(F32))

    planes = []
    for p in range(cx + 2 * HALO):
        if HALO <= p < HALO + cx:
            k = p - HALO
            own, one, two = ct_ref[k], side_a[0].astype(F32), side_b[0].astype(F32)
        else:
            before = p < HALO
            k = p + cx - HALO if before else p - HALO - cx
            x, y = (slab_b, slab_a) if before else (slab_a, slab_b)
            own, one, two = (chosen(slab_even, x[i], y[i]) for i in (k, cx, cx + 1))
        rows = slice(HALO * k, HALO * (k + 1))
        one, two = one[rows], two[rows]
        sides = jnp.concatenate([jnp.where(even, one, two), jnp.where(even, two, one)], axis=0)
        planes.append(jnp.concatenate([own, sides * mask], axis=0))
    values = [(DAMPING / COARSE_CENTRE) * plane for plane in planes]
    for sweep in range(1, HALO):
        values = [
            masked(
                relaxed(values[i - 1], values[i], values[i + 1], planes[i + sweep - 1], COARSE_CENTRE),
                cy,
                mask,
            )
            for i in range(1, len(values) - 1)
        ]
    wide = cy + 4
    for q, value in enumerate(values):
        value = jnp.concatenate([value[: cy + 2], value[cy + 2 * HALO - 2 :]], axis=0)
        for i, part in enumerate(tiles_of(value)):
            fine[q, i, pl.ds(0, wide, 2), :] = part
            fine[q, i, pl.ds(1, wide, 2), :] = part
    def second_total(plane):
        rows = plane.shape[0]
        return pltpu.roll(plane, 1, 0) + pltpu.roll(plane, rows - 1, 0)

    spread = [jnp.concatenate([fine[q, i, : 2 * wide] for i in range(cz // LANES)], axis=1) for q in range(cx + 2)]
    still = [KEEP * plane + PULL * second_total(plane) for plane in spread]
    once = []
    for p in range(-1, nx + 1):
        q = (p + 2) // 2
        if p % 2 == 0:
            others = spread[q - 1] + spread[q]
        else:
            others = spread[q] + spread[q + 1]
        once.append(masked(still[q] + PULL * others, ny, mask))

    def twice(plane):
        return jnp.concatenate([part for part in tiles_of(plane) for _ in range(2)], axis=1)

    back = back_ref[...]
    bounds = (0, nx // 2, nx // 4 * 3, nx)
    for start, end in zip(bounds, bounds[1:]):
        planes = []
        for p in range(start, end):
            plane = once[p + 1]
            total = once[p] + once[p + 2] + second_total(plane)
            none = (KEEP * plane + PULL * total)[:ny]
            one = (2.0 * PULL) * plane[:ny]
            two = (PULL * PULL) * spread[(p + 2) // 2][:ny]
            planes.append(twice(none) + third_sum(twice(one) + third_sum(twice(two))))
        done = dot(jnp.concatenate(planes, axis=0).astype(BF16), back, 1, 0)
        out_ref[start:end] = base_ref[start:end] + done.reshape(end - start, ny, nz)
        for p in range(start, end):
            copies.append(pltpu.make_async_copy(out_ref.at[p], out_any.at[p], sem.at[len(copies)]))
            copies[-1].start()
    for copy in copies:
        copy.wait()


def local(
    nutrient, species, agent_cell, death_flag, divide_flag, slab_move, depth_route, net_weight, sensing, uptake_weight
):
    depths = lax.axis_size("depth")
    nx, ny, nz = nutrient.shape
    agents, width = species.shape
    capacity = 2 * agents // depths
    me = lax.axis_index("depth").astype(jnp.int32).reshape(1)
    slab = lax.axis_index("slab").astype(jnp.int32).reshape(1)
    shape = jax.ShapeDtypeStruct
    cells, death, divide = (x.reshape(1, agents) for x in (agent_cell, death_flag, divide_flag))
    move, route = slab_move.reshape(1, agents), depth_route.reshape(1, agents)
    half = ny // 16
    if agents % nz or nx * ny > PART or nz % PART or depths < 4:
        raise ValueError("list digits")
    arguments = (
        cells, nutrient, divide, uptake_weight.reshape(1, width), species, death,
        move, route, net_weight, sensing.reshape(1, width),
    )
    (
        nutrient, places, field_a, field_b, cells, divide, weight, species, death, move, route, net_weight, sensing
    ) = pl.pallas_call(
        load_kernel,
        out_shape=(
            shape((nx, ny, nz), F32),
            shape((nz, agents), BF16),
            shape((HALO * half, 16, nz), BF16),
            shape((HALO * half, 16, nz), BF16),
        )
        + tuple(shape(x.shape, x.dtype) for i, x in enumerate(arguments) if i != 1),
        in_specs=[SMEM_SPEC] + [HBM_SPEC] * len(arguments),
        out_specs=[VMEM_SPEC] * (4 + len(arguments) - 1),
        scratch_shapes=[
            pltpu.VMEM((nx, ny, nz), F32),
            pltpu.SemaphoreType.DMA((len(arguments),)),
        ],
        compiler_params=PARAMS,
        name="load",
    )(slab, *(pltpu.with_memory_space_constraint(x, pltpu.HBM) for x in arguments))
    target, sensed, depth_a, depth_b, agent_list = pl.pallas_call(
        uptake_kernel,
        out_shape=(
            shape((nx, ny, nz), F32),
            shape((8, agents), F32),
            shape((nx // 2, 16, nz), BF16),
            shape((nx // 2, 16, nz), BF16),
            shape((4 * agents // nz, nz), F32),
        ),
        in_specs=[SMEM_SPEC] + [VMEM_SPEC] * 7,
        out_specs=[VMEM_SPEC] * 5,
        compiler_params=PARAMS,
        cost_estimate=pl.CostEstimate(flops=1 << 31, bytes_accessed=1 << 20, transcendentals=0),
        name="uptake",
    )(me, nutrient, places, cells, divide, weight, species, death)
    field_a, field_b, depth_a, depth_b = lax.optimization_barrier((field_a, field_b, depth_a, depth_b))
    side_a = swapped(depth_a, "depth", "a")
    side_b = swapped(depth_b, "depth", "b")
    field_a = swapped(field_a, "slab", "a")
    field_b = swapped(field_b, "slab", "b")
    rows = 2 * (HALO - 1) ** 2 + agent_list.shape[0]
    rows = -(-rows // 16) * 16
    slab_a, slab_b = pl.pallas_call(
        corner_kernel,
        out_shape=tuple(shape((rows // 16, 16, nz), BF16) for _ in range(2)),
        in_specs=[SMEM_SPEC] * 2 + [VMEM_SPEC] * 3,
        out_specs=[VMEM_SPEC] * 2,
        compiler_params=PARAMS,
        name="corner",
    )(me, slab, side_a, side_b, agent_list)
    slab_a = swapped(slab_a, "slab", "a")
    slab_b = swapped(slab_b, "slab", "b")
    cx, cy, cz = nx // 2, ny // 2, nz // 2
    ext = ny + 2 * HALO
    sent = pl.pallas_call(
        network_kernel,
        out_shape=tuple(
            shape((capacity // 32, 16, 2 * width) if k == 1 else (capacity // 16, 16, width), BF16)
            for k in range(depths)
        )
        + tuple(shape((MIG * width // (16 * cz), 16, cz), BF16) for _ in range(2)),
        in_specs=[SMEM_SPEC] * 2 + [VMEM_SPEC] * 7,
        out_specs=[VMEM_SPEC] * (depths + 2),
        compiler_params=PARAMS,
        cost_estimate=pl.CostEstimate(flops=1 << 31, bytes_accessed=1<<20, transcendentals=0),
        name="network",
    )(me, slab, species, sensed, death, move, route, net_weight, sensing)
    u0, text, u1, u2, inside = pl.pallas_call(
        functools.partial(inner_kernel, depths),
        out_shape=(
            shape((nx + 2 * HALO, ext, nz), F32),
            shape((nx + 2 * HALO - 2, ext, nz), F32),
            shape((nx + 2 * HALO - 2, ext, nz), F32),
            shape((nx + 4, ext, nz), F32),
            shape((nx - 4, ny, nz), F32),
        ),
        in_specs=[SMEM_SPEC] * 2 + [VMEM_SPEC] * 6,
        out_specs=[VMEM_SPEC] * 5,
        compiler_params=PARAMS,
        cost_estimate=pl.CostEstimate(flops=1 << 20, bytes_accessed=1<<20, transcendentals=0),
        name="inner",
    )(me, slab, nutrient, target, side_a, side_b, field_a, field_b)
    slab_a, slab_b, inside, *sent = lax.optimization_barrier((slab_a, slab_b, inside, *sent))
    text, _, u2, ct, ct_all, coarse_a, coarse_b = pl.pallas_call(
        functools.partial(smooth_kernel, depths, agents),
        out_shape=(
            shape(text.shape, F32),
            shape(u1.shape, F32),
            shape(u2.shape, F32),
            shape((cx, cy, cz), F32),
            shape((cx, cy, cz), BF16),
            shape((1, cx * HALO, cz), BF16),
            shape((1, cx * HALO, cz), BF16),
        ),
        in_specs=[SMEM_SPEC] * 2 + [VMEM_SPEC] * 7,
        out_specs=[VMEM_SPEC] * 7,
        scratch_shapes=[
            pltpu.VMEM((cx, cz // LANES, ny + 8, LANES), F32),
            pltpu.VMEM((2, (HALO - 1) * ny, nz), F32),
        ],
        input_output_aliases={3: 0, 4: 1, 5: 2},
        compiler_params=PARAMS,
        name="smooth",
    )(me, slab, u0, text, u1, u2, inside, slab_a, slab_b)
    coarse_a = swapped(jnp.concatenate([coarse_a, sent[1]], axis=0), "depth", "a")
    coarse_b = swapped(coarse_b, "depth", "b")
    arrived = [sent[0], swapped(sent[2], "depth", "b")]
    arrived += [cyclic(sent[k + 1], "depth", k) for k in range(2, depths - 1)]
    tail_a, tail_b = (
        swapped(jnp.concatenate([ct_all, coarse_a[:1], coarse_b, movers], axis=0), "slab", which)
        for which, movers in (("a", sent[depths]), ("b", sent[depths + 1]))
    )
    base, back = pl.pallas_call(
        functools.partial(post_kernel, depths),
        out_shape=(shape((nx, ny, nz), F32), shape((nz, nz), BF16)),
        in_specs=[SMEM_SPEC] + [VMEM_SPEC] * 2,
        out_specs=[VMEM_SPEC] * 2,
        scratch_shapes=[pltpu.VMEM((nx + 2, ext, nz), F32)],
        compiler_params=PARAMS,
        cost_estimate=pl.CostEstimate(flops=1 << 30, bytes_accessed=1 << 22, transcendentals=0),
        name="post",
    )(me, u2, text)
    grid_field, agents_out = pl.pallas_call(
        functools.partial(correct_kernel, depths),
        out_shape=(
            shape((nx, ny, nz), F32),
            shape(((depths * capacity + 2 * MIG) // 16, 16, width), BF16),
        ),
        in_specs=[SMEM_SPEC] * 2 + [VMEM_SPEC] * 7 + [ANY_SPEC] * (depths - 1),
        out_specs=[HBM_SPEC, ANY_SPEC],
        scratch_shapes=[
            pltpu.VMEM((cx + 2, cz // LANES, ext + 8, LANES), F32),
            pltpu.VMEM((nx, ny, nz), F32),
            pltpu.SemaphoreType.DMA((depths + 5 + nx,)),
        ],
        compiler_params=PARAMS,
        name="correct",
    )(me, slab, ct, coarse_a, coarse_b, tail_a, tail_b, base, back, *arrived)
    return grid_field, agents_out.reshape(-1, width)


def solution(mesh):
    rows = P(("slab", "depth"))
    in_specs = (
        P("slab", "depth", None),
        P(("slab", "depth"), None),
        rows,
        rows,
        rows,
        rows,
        P(("slab", "depth"), None),
        P(),
        P(),
        P(),
    )
    out_specs = (P("slab", "depth", None), P(("slab", "depth"), None))
    return jax.shard_map(local, mesh=mesh, in_specs=in_specs, out_specs=out_specs, check_vma=False)
```

```python
import functools

import jax
import jax.numpy as jnp
from jax import lax
from jax.experimental import pallas as pl
from jax.experimental.pallas import tpu as pltpu
from jax.sharding import PartitionSpec as P

MIG = 128
PART = 256
SCREENING = 0.05
DAMPING = 2.0 / 3.0
CENTRE = 6.0 + SCREENING
COARSE_CENTRE = 6.0 + 4.0 * SCREENING
HALO = 4
F32, BF16 = jnp.float32, jnp.bfloat16
VMEM_SPEC = pl.BlockSpec(memory_space=pltpu.VMEM)
ANY_SPEC = pl.BlockSpec(memory_space=pl.ANY)
HBM_SPEC = pl.BlockSpec(memory_space=pltpu.HBM)
SMEM_SPEC = pl.BlockSpec(memory_space=pltpu.SMEM)
PARAMS = pltpu.CompilerParams(vmem_limit_bytes=40 * 1024 * 1024)


def dot(a, b, ca, cb):
    return lax.dot_general(a, b, (((ca,), (cb,)), ((), ())), preferred_element_type=F32)


def halves(x):
    high = x.astype(BF16)
    return high, (x - high.astype(F32)).astype(BF16)


def iota(shape, dim):
    return lax.broadcasted_iota(jnp.int32, shape, dim)


def cyclic(x, axis, by):
    count = lax.axis_size(axis)
    return lax.ppermute(x, axis, [(i, (i + by) % count) for i in range(count)])


def swapped(x, axis, which):
    count = lax.axis_size(axis)
    if count % 2:
        raise ValueError("odd axis")
    first = 0 if which == "a" else 1
    pairs = []
    for i in range(first, count, 2):
        j = (i + 1) % count
        pairs += [(i, j), (j, i)]
    return lax.ppermute(x, axis, sorted(pairs))


def is_even(x):
    return lax.rem(x, 2) == 0


LANES = 128


def shuffle(nz, back):
    one, two = iota((nz, nz), 0), iota((nz, nz), 1)
    if back:
        one, two = two, one
    return (one == (two % LANES) * (nz // LANES) + two // LANES).astype(F32).astype(BF16)


def load_kernel(slab_ref, *refs):
    count = 10
    sources, refs = refs[:count], refs[count:]
    u_ref, place_ref, field_a, field_b, *targets = refs[:-2]
    raw, sem = refs[-2:]
    cell_ref = targets[0]
    targets.insert(1, raw)
    copies = [
        pltpu.make_async_copy(source, target, sem.at[i])
        for i, (source, target) in enumerate(zip(sources, targets, strict=True))
    ]
    for copy in copies:
        copy.start()
    nx, ny, nz = u_ref.shape
    rows = nx * ny
    tiles = nz // LANES
    order = shuffle(nz, False)
    copies[0].wait()
    cell_z = cell_ref[...] % nz
    cell_z = (cell_z % tiles) * LANES + cell_z // tiles
    place_ref[...] = (iota(place_ref.shape, 0) == cell_z).astype(F32).astype(BF16)
    copies[1].wait()
    high, low = halves(raw[...].reshape(rows, nz))
    both = dot(jnp.concatenate([high, low], axis=0), order, 1, 0)
    u_ref[...] = (both[:rows] + both[rows:]).reshape(nx, ny, nz)
    half = ny // 16
    slab_even = is_even(slab_ref[0])
    for ref, front in ((field_a, slab_even), (field_b, jnp.logical_not(slab_even))):
        start = jnp.where(front, nx - HALO, 0)
        for k in range(HALO):
            ref[k * half : (k + 1) * half] = u_ref[start + k].astype(BF16).reshape(half, 16, nz)
    for copy in copies[2:]:
        copy.wait()


def uptake_kernel(
    me_ref, u_ref, place_ref, cell_ref, divide_ref, weight_ref, species_ref, death_ref,
    t_ref, sensed_ref, depth_a, depth_b, list_ref,
):
    nx, ny, nz = u_ref.shape
    agents = species_ref.shape[0]
    rows = nx * ny
    tiles = nz // LANES
    cell = cell_ref[...]
    cell_row = cell // nz
    cell_z = cell - cell_row * nz
    cell_z = (cell_z % tiles) * LANES + cell_z // tiles
    one_z = place_ref[...]
    in_row = iota((rows, agents), 0) == cell_row
    u = u_ref[...].reshape(rows, nz)
    picked = dot(u.astype(BF16), one_z, 1, 0)
    sample = jnp.sum(jnp.where(in_row, picked, 0.0), axis=0, keepdims=True)
    sensed_ref[...] = jnp.broadcast_to(sample, (8, agents))
    weight = jnp.broadcast_to(weight_ref[...].reshape(1, -1), (8, species_ref.shape[1]))
    score = dot(weight, species_ref[...], 1, 1)[0:1]
    softplus = jnp.maximum(score, 0.0) + jnp.log1p(jnp.exp(-jnp.abs(score)))
    alive = (1 - death_ref[...].reshape(1, agents)).astype(F32)
    divide = divide_ref[...].reshape(1, agents).astype(F32)
    uptake = alive * (1.0 + divide) * softplus * sample / (0.5 + sample)
    up_high = uptake.astype(BF16).astype(F32)
    source = dot(jnp.where(in_row, up_high, 0.0).astype(BF16), one_z, 1, 1)
    t_ref[...] = (SCREENING * u - source).reshape(nx, ny, nz)
    even = is_even(me_ref[0])
    for pair in range(nx // 2):
        parts = []
        for start in (0, ny - HALO):
            for plane in (2 * pair, 2 * pair + 1):
                parts.append(u_ref[plane, start : start + HALO])
                parts.append(t_ref[plane, start : start + HALO])
        low = jnp.concatenate(parts[:4], axis=0)
        high = jnp.concatenate(parts[4:], axis=0)
        depth_a[pair] = jnp.where(even, high, low).astype(BF16)
        depth_b[pair] = jnp.where(even, low, high).astype(BF16)
    part = cell_z // PART
    values = (cell_row.astype(F32), (cell_z - part * PART).astype(F32), part.astype(F32), up_high)
    list_ref[...] = jnp.concatenate(
        [x[:, i * nz : (i + 1) * nz] for x in values for i in range(agents // nz)], axis=0
    )


def network_kernel(
    me_ref, slab_ref, species_ref, sensed_ref, death_ref, move_ref, route_ref, net_ref, sensing_ref, *outs
):
    agents, width = species_ref.shape
    depths = len(outs) - 2
    capacity = outs[0].shape[0] * 16
    species = species_ref[...]
    sensing = sensing_ref[...].reshape(1, width)
    first = sensing.astype(BF16)
    rest = sensing - first.astype(F32)
    second = rest.astype(BF16)
    third = (rest - second.astype(F32)).astype(BF16)
    line = iota((8, width), 0)
    terms = jnp.where(
        line == 0, first.astype(F32),
        jnp.where(line == 1, second.astype(F32), jnp.where(line == 2, third.astype(F32), 0.0)),
    ).astype(BF16)
    activation = dot(species, net_ref[...], 1, 0) + dot(sensed_ref[...].astype(BF16), terms, 0, 0)
    updated = (0.5 * species.astype(F32) + jnp.tanh(activation)).astype(BF16)
    lanes = 128
    lines = -(-(depths + 2) // 8) * 8
    line = iota((lines, lanes), 0)
    square = iota((lanes, 2 * lanes), 0)
    column = iota((lanes, 2 * lanes), 1)
    counter = jnp.where(jnp.logical_or(column >= lanes, square < column), 1.0, 0.0).astype(BF16)
    blocks = agents // lanes
    route = route_ref[...].reshape(1, agents)
    move = move_ref[...].reshape(1, agents)
    death = death_ref[...].reshape(1, agents)
    hits = []
    for block in range(blocks):
        cut = slice(block * lanes, (block + 1) * lanes)
        wanted = jnp.where(line < depths, route[:, cut], jnp.where(line < depths + 2, move[:, cut] + (depths - 1), -1))
        hits.append((wanted == line).astype(F32))
    counts = dot(jnp.concatenate(hits, axis=0).astype(BF16), counter, 1, 0)
    me = me_ref[0]
    to_a = jnp.where(is_even(slab_ref[0]), 1, 2)
    hop_a = jnp.where(is_even(me), 1, depths - 1)
    running = jnp.zeros((lines, lanes), F32)
    keys = []
    for block in range(blocks):
        cut = slice(block * lanes, (block + 1) * lanes)
        own = slice(block * lines, (block + 1) * lines)
        before = (counts[own, :lanes] + running) * hits[block]
        running = running + counts[own, lanes:]
        slot = jnp.sum(jnp.where(line < depths, before, 0.0), axis=0, keepdims=True).astype(jnp.int32)
        rank = jnp.sum(jnp.where(line < depths, 0.0, before), axis=0, keepdims=True).astype(jnp.int32)
        hop = route[:, cut] - me
        hop = jnp.where(hop < 0, hop + depths, hop)
        hop = jnp.where(hop == hop_a, 1, jnp.where(hop == depths - hop_a, 2, jnp.where(hop == 0, 0, hop + 1)))
        key = jnp.where(
            move[:, cut] == 0,
            hop * capacity + slot,
            depths * capacity + jnp.where(move[:, cut] == to_a, 0, MIG) + rank,
        )
        keys.append(jnp.where(death[:, cut] == 0, key, -1))
    key = jnp.concatenate(keys, axis=1)
    start = 0
    for index, out in enumerate(outs):
        size = capacity if index < depths else MIG
        chosen = (iota((size, agents), 0) == key - start).astype(F32).astype(BF16)
        placed = dot(chosen, updated, 1, 0).astype(BF16)
        start += size
        blocks = out.shape[0]
        for i in range(0, out.shape[2], width):
            part = placed[i // width * blocks * 16 :][: blocks * 16]
            out[:, :, i : i + width] = part.reshape(blocks, 16, width)


def tiles_of(x):
    return [x[:, i : i + LANES] for i in range(0, x.shape[1], LANES)]


def third_sum(x):
    parts = tiles_of(x)
    lane = iota((x.shape[0], LANES), 1)
    before = jnp.where(lane == 0, 0.0, pltpu.roll(parts[-1], 1, 1))
    after = jnp.where(lane == LANES - 1, 0.0, pltpu.roll(parts[0], LANES - 1, 1))
    padded = [before] + parts + [after]
    return jnp.concatenate([x + y for x, y in zip(padded[:-2], padded[2:])], axis=1)


def neighbour_total(before, plane, after):
    rows = plane.shape[0]
    second = pltpu.roll(plane, 1, 0) + pltpu.roll(plane, rows - 1, 0)
    return before + after + second + third_sum(plane)


def relaxed(before, plane, after, target, centre):
    return (1.0 - DAMPING) * plane + (DAMPING / centre) * (
        target + neighbour_total(before, plane, after)
    )


def edge_mask(me, depths, halo):
    row = iota((2 * halo, 1), 0)
    return jnp.where(
        row < halo, (me < depths - 1).astype(F32), (me > 0).astype(F32)
    )


def masked(plane, own, mask):
    return jnp.concatenate([plane[:own], plane[own:] * mask], axis=0)


def halo_rows(side_a, side_b, even, plane, mask):
    at = 2 * HALO * (plane % 2)
    side_a = side_a[at : at + 2 * HALO].astype(F32)
    side_b = side_b[at : at + 2 * HALO].astype(F32)
    high = jnp.where(even, side_a, side_b)
    low = jnp.where(even, side_b, side_a)
    return (
        jnp.concatenate([high[:HALO], low[:HALO]], axis=0) * mask,
        jnp.concatenate([high[HALO:], low[HALO:]], axis=0),
    )


def corner_kernel(me_ref, slab_ref, side_a, side_b, list_ref, slab_a, slab_b):
    layers = 2 * side_a.shape[0]
    nz = side_a.shape[2]
    even = is_even(me_ref[0])
    slab_even = is_even(slab_ref[0])

    def layer(side, plane):
        at = 2 * HALO * (plane % 2)
        return side[plane // 2].astype(F32)[at : at + 2 * HALO]

    for ref, front in ((slab_a, slab_even), (slab_b, jnp.logical_not(slab_even))):
        parts = []
        for side, high in ((side_a, even), (side_b, jnp.logical_not(even))):
            targets = []
            for i in range(1, HALO):
                x = jnp.where(front, layer(side, layers - i), layer(side, i - 1))
                parts.append(jnp.where(high, x[: HALO - i], x[i:HALO]))
                if i < HALO - 1:
                    targets.append(
                        jnp.where(high, x[HALO : 2 * HALO - 1 - i], x[HALO + 1 + i :])
                    )
            parts += targets
        parts.append(list_ref[...])
        used = sum(part.shape[0] for part in parts)
        total = ref.shape[0] * ref.shape[1]
        parts.append(jnp.zeros((total - used, nz), F32))
        ref[...] = jnp.concatenate(parts, axis=0).astype(BF16).reshape(ref.shape)


def corner_rows(block_a, block_b, even, mask):
    high = jnp.where(even, block_a, block_b)
    low = jnp.where(even, block_b, block_a)
    nz = high.shape[1]
    fields, targets = [], []
    at = 0
    for rows, out in ((HALO, fields), (HALO - 1, targets)):
        for i in range(1, rows):
            count = rows - i
            gap = jnp.zeros((2 * (HALO - count), nz), F32)
            cut = slice(at, at + count)
            out.append(jnp.concatenate([high[cut], gap, low[cut]], axis=0) * mask)
            at += count
    return fields, targets + [jnp.zeros_like(fields[0])]


KEEP, PULL = 1.0 - DAMPING, DAMPING / CENTRE


def inner_kernel(
    depths, me_ref, slab_ref, u_ref, t_ref, side_a, side_b, field_a, field_b, u0, text_ref, u1, u2_ref, inside
):
    nx, ny, nz = u_ref.shape
    even = is_even(me_ref[0])
    slab_even = is_even(slab_ref[0])
    half = ny // 16
    mask = edge_mask(me_ref[0], depths, HALO)
    for field, after in ((field_a, slab_even), (field_b, jnp.logical_not(slab_even))):
        u_at = jnp.where(after, HALO + nx, 0)
        for k in range(HALO):
            u0[u_at + k, :ny] = field[k * half : (k + 1) * half].astype(F32).reshape(ny, nz)
            u0[u_at + k, ny:] = jnp.zeros((2 * HALO, nz), F32)
    for plane in range(nx):
        u0[HALO + plane, :ny] = u_ref[plane]
        text_ref[HALO - 1 + plane, :ny] = t_ref[plane]
        uh, th = halo_rows(side_a[plane // 2], side_b[plane // 2], even, plane, mask)
        u0[HALO + plane, ny:] = uh
        text_ref[HALO - 1 + plane, ny:] = th

    def outer(i, carry):
        for p in (i, nx + HALO - 1 + i):
            u1[p] = KEEP * u0[p + 1] + PULL * neighbour_total(u0[p], u0[p + 1], u0[p + 2])
        return carry

    lax.fori_loop(0, HALO - 1, outer, 0)

    def first(p, carry):
        v = relaxed(u0[p], u0[p + 1], u0[p + 2], text_ref[p], CENTRE)
        u1[p] = masked(v, ny, mask)
        return carry

    lax.fori_loop(HALO - 1, nx + HALO - 1, first, 0, unroll=2)

    def second(p, carry):
        v = relaxed(u1[p], u1[p + 1], u1[p + 2], text_ref[p + 1], CENTRE)
        u2_ref[p] = masked(v, ny, mask)
        return carry

    lax.fori_loop(HALO - 1, nx + 1, second, 0, unroll=2)
    for p in range(2, nx - 2):
        inside[p - 2] = residual(u2_ref, text_ref, p, ny)


def residual(u2_ref, text_ref, p, ny):
    v = u2_ref[p + 2]
    total = neighbour_total(u2_ref[p + 1], v, u2_ref[p + 3])
    return (text_ref[p + 3] - CENTRE * v + total)[:ny]


def smooth_kernel(
    depths, agents, me_ref, slab_ref, u0, text_in, u1_in, u2_in, inside, slab_a, slab_b,
    text_ref, u1, u2_ref, coarse_ref, coarse_all_ref, coarse_a, coarse_b, paired, foreign,
):
    nx = u0.shape[0] - 2 * HALO
    ny, nz = u0.shape[1] - 2 * HALO, u0.shape[2]
    mask = edge_mask(me_ref[0], depths, HALO)
    even = is_even(me_ref[0])
    slab_even = is_even(slab_ref[0])
    near = HALO - 1
    corner = HALO * near // 2 + near * (near - 1) // 2
    row = iota((8, 1), 0)
    first, last = (row == 0).astype(F32), (row == 7).astype(F32)
    sides = ((slab_a, slab_even), (slab_b, jnp.logical_not(slab_even)))
    messages = []
    lines = agents // nz
    for side, (ref, after) in enumerate(sides):
        message = ref[...].astype(F32).reshape(-1, nz)
        messages.append(message)
        cell_row, place, part, uptake = (
            jnp.concatenate([message[at + i : at + i + 1] for i in range(lines)], axis=1)
            for at in range(2 * corner, 2 * corner + 4 * lines, lines)
        )
        cell_row = cell_row.astype(jnp.int32) - jnp.where(after, 0, (nx - near) * ny)
        wanted = jnp.logical_and(cell_row >= 0, cell_row < near * ny)
        key = jnp.where(wanted, part.astype(jnp.int32) * (near * ny) + cell_row, -1)
        one_z = (iota((PART, agents), 0) == place.astype(jnp.int32)).astype(F32).astype(BF16)
        key_rows = iota((near * ny * (nz // PART), agents), 0)
        taken = jnp.where(key_rows == key, uptake, 0.0).astype(BF16)
        source = dot(taken, one_z, 1, 1)
        for i in range(nz // PART):
            foreign[side, :, i * PART : (i + 1) * PART] = source[i * near * ny : (i + 1) * near * ny]
    for side, (_, after) in enumerate(sides):
        message = messages[side]
        fields, targets = corner_rows(message[:corner], message[corner : 2 * corner], even, mask)
        sign = jnp.where(after, 1, -1)
        edge = jnp.where(after, nx - 1, 0)
        for i in range(1, HALO):
            p = edge + sign * i
            index = jnp.where(after, i - 1, HALO - 1 - i)
            t = SCREENING * u0[p + 4, :ny] - foreign[side, pl.ds(index * ny, ny)]
            text_ref[p + 3, :ny] = t
            text_ref[p + 3, ny:] = targets[i - 1]
            x = fields[i - 1]
            nearer = u0[p + 4 - sign, ny:] if i == 1 else fields[i - 2]
            total = nearer + third_sum(x)
            if i < HALO - 1:
                total = total + fields[i]
            beyond = u0[p + 4]
            up = jnp.where(row == 0, beyond[ny - 1 : ny], pltpu.roll(x, 1, 0))
            down = jnp.where(row == 7, beyond[0:1], pltpu.roll(x, 7, 0))
            u1[p + 3, ny:] = (KEEP * x + PULL * (targets[i - 1] + total + up + down)) * mask
            v = u1[p + 3, :ny] + PULL * t
            u1[p + 3, :ny] = v
            u1[p + 3, 0:8] = v[0:8] + (PULL * first) * x[7:8]
            u1[p + 3, ny - 8 : ny] = v[ny - 8 :] + (PULL * last) * x[0:1]
        u1[edge + 3, ny:] = u1[edge + 3, ny:] + PULL * fields[0]
        u2_ref[edge - sign + 2, ny:] = u2_ref[edge - sign + 2, ny:] + (PULL * PULL) * fields[0]

    for p in (1, 2, nx + 1, nx + 2):
        v = relaxed(u1[p], u1[p + 1], u1[p + 2], text_ref[p + 1], CENTRE)
        u2_ref[p] = masked(v, ny, mask)
    for q in range(nx // 2):
        both = 0.0
        for p in (2 * q, 2 * q + 1):
            known = 2 <= p < nx - 2
            both = both + (inside[p - 2] if known else residual(u2_ref, text_ref, p, ny))
        parts = tiles_of(both)
        for i in range(len(parts) // 2):
            paired[q, i, :ny] = parts[2 * i] + parts[2 * i + 1]
    cx, cy, cz = coarse_ref.shape
    coarse = jnp.concatenate(
        [
            jnp.concatenate(
                [
                    paired[q, i, pl.ds(0, cy, 2), :] + paired[q, i, pl.ds(1, cy, 2), :]
                    for i in range(cz // LANES)
                ],
                axis=1,
            )
            for q in range(cx)
        ],
        axis=0,
    )
    coarse = 0.5 * coarse
    coarse_ref[...] = coarse.reshape(cx, cy, cz)
    coarse_all_ref[...] = coarse.astype(BF16).reshape(cx, cy, cz)
    low, high = (
        jnp.concatenate([coarse_ref[q, start : start + HALO] for q in range(cx)], axis=0)
        for start in (0, cy - HALO)
    )
    coarse_a[0] = jnp.where(even, high, low).astype(BF16)
    coarse_b[0] = jnp.where(even, low, high).astype(BF16)


def post_kernel(depths, me_ref, u1, u2_in, text_ref, out_ref, back_ref, v1, u2_ref):
    nx, ny, nz = out_ref.shape
    back = shuffle(nz, True)
    back_ref[...] = back
    mask = edge_mask(me_ref[0], depths, HALO)
    last = nx + 3
    for p in range(1, last):
        u2_ref[p] = u2_in[p]
    for p in (0, last):
        v = relaxed(u1[p], u1[p + 1], u1[p + 2], text_ref[p + 1], CENTRE)
        u2_ref[p] = masked(v, ny, mask)

    def first(p, carry):
        v = relaxed(u2_ref[p], u2_ref[p + 1], u2_ref[p + 2], text_ref[p + 2], CENTRE)
        v1[p] = masked(v, ny, mask)
        return carry

    lax.fori_loop(0, nx + 2, first, 0, unroll=2)

    def second(p, carry):
        v = relaxed(v1[p], v1[p + 1], v1[p + 2], text_ref[p + 3], CENTRE)
        out_ref[p] = v[:ny]
        return carry

    lax.fori_loop(0, nx, second, 0, unroll=2)
    high, low = halves(out_ref[...].reshape(nx * ny, nz))
    both = dot(jnp.concatenate([high, low], axis=0), back, 1, 0)
    out_ref[...] = (both[: nx * ny] + both[nx * ny :]).reshape(nx, ny, nz)


def correct_kernel(
    depths, me_ref, slab_ref, ct_ref, side_a, side_b, slab_a, slab_b, base_ref, back_ref, *rest
):
    packed = rest[: depths - 1]
    out_any, agents_ref, fine, out_ref, sem = rest[depths - 1 :]
    nx, ny, nz = out_ref.shape
    cx, cy, cz = ct_ref.shape
    me = me_ref[0]
    even = is_even(me)
    slab_even = is_even(slab_ref[0])
    blocks = packed[0].shape[0]
    width = agents_ref.shape[2]
    copies = []

    def place(source, start):
        target = agents_ref.at[pl.ds(start, source.shape[0])]
        copies.append(pltpu.make_async_copy(source, target, sem.at[len(copies)]))
        copies[-1].start()

    def place_wide(source, start):
        for i in range(source.shape[2] // width):
            part = source.at[:, :, pl.ds(i * width, width)]
            place(part, start + i * source.shape[0])

    up = jnp.where(me == depths - 1, 0, me + 1)
    down = jnp.where(me == 0, depths - 1, me - 1)
    place(packed[0], me * blocks)
    place_wide(side_a.at[pl.ds(1, side_a.shape[0] - 1)], jnp.where(even, up, down) * blocks)
    place(packed[1], jnp.where(even, down, up) * blocks)
    for k in range(2, depths - 1):
        origin = me - k
        place(packed[k], jnp.where(origin < 0, origin + depths, origin) * blocks)
    for ref, late in ((slab_a, slab_even), (slab_b, jnp.logical_not(slab_even))):
        start = depths * blocks + jnp.where(late, MIG // 16, 0)
        place_wide(ref.at[pl.ds(cx + 2, ref.shape[0] - cx - 2)], start)
    mask = edge_mask(me, depths, HALO)

    def chosen(condition, x, y):
        return jnp.where(condition, x.astype(F32), y.astype(F32))

    planes = []
    for p in range(cx + 2 * HALO):
        if HALO <= p < HALO + cx:
            k = p - HALO
            own, one, two = ct_ref[k], side_a[0].astype(F32), side_b[0].astype(F32)
        else:
            before = p < HALO
            k = p + cx - HALO if before else p - HALO - cx
            x, y = (slab_b, slab_a) if before else (slab_a, slab_b)
            own, one, two = (chosen(slab_even, x[i], y[i]) for i in (k, cx, cx + 1))
        rows = slice(HALO * k, HALO * (k + 1))
        one, two = one[rows], two[rows]
        sides = jnp.concatenate([jnp.where(even, one, two), jnp.where(even, two, one)], axis=0)
        planes.append(jnp.concatenate([own, sides * mask], axis=0))
    values = [(DAMPING / COARSE_CENTRE) * plane for plane in planes]
    for sweep in range(1, HALO):
        values = [
            masked(
                relaxed(values[i - 1], values[i], values[i + 1], planes[i + sweep - 1], COARSE_CENTRE),
                cy,
                mask,
            )
            for i in range(1, len(values) - 1)
        ]
    wide = cy + 4
    for q, value in enumerate(values):
        value = jnp.concatenate([value[: cy + 2], value[cy + 2 * HALO - 2 :]], axis=0)
        for i, part in enumerate(tiles_of(value)):
            fine[q, i, pl.ds(0, wide, 2), :] = part
            fine[q, i, pl.ds(1, wide, 2), :] = part
    def second_total(plane):
        rows = plane.shape[0]
        return pltpu.roll(plane, 1, 0) + pltpu.roll(plane, rows - 1, 0)

    spread = [jnp.concatenate([fine[q, i, : 2 * wide] for i in range(cz // LANES)], axis=1) for q in range(cx + 2)]
    still = [KEEP * plane + PULL * second_total(plane) for plane in spread]
    once = []
    for p in range(-1, nx + 1):
        q = (p + 2) // 2
        if p % 2 == 0:
            others = spread[q - 1] + spread[q]
        else:
            others = spread[q] + spread[q + 1]
        once.append(masked(still[q] + PULL * others, ny, mask))

    def twice(plane):
        return jnp.concatenate([part for part in tiles_of(plane) for _ in range(2)], axis=1)

    back = back_ref[...]
    bounds = (0, nx // 2, nx // 4 * 3, nx)
    for start, end in zip(bounds, bounds[1:]):
        planes = []
        for p in range(start, end):
            plane = once[p + 1]
            total = once[p] + once[p + 2] + second_total(plane)
            none = (KEEP * plane + PULL * total)[:ny]
            one = (2.0 * PULL) * plane[:ny]
            two = (PULL * PULL) * spread[(p + 2) // 2][:ny]
            planes.append(twice(none) + third_sum(twice(one) + third_sum(twice(two))))
        done = dot(jnp.concatenate(planes, axis=0).astype(BF16), back, 1, 0)
        out_ref[start:end] = base_ref[start:end] + done.reshape(end - start, ny, nz)
        for p in range(start, end):
            copies.append(pltpu.make_async_copy(out_ref.at[p], out_any.at[p], sem.at[len(copies)]))
            copies[-1].start()
    for copy in copies:
        copy.wait()


def local(
    nutrient, species, agent_cell, death_flag, divide_flag, slab_move, depth_route, net_weight, sensing, uptake_weight
):
    depths = lax.axis_size("depth")
    nx, ny, nz = nutrient.shape
    agents, width = species.shape
    capacity = 2 * agents // depths
    me = lax.axis_index("depth").astype(jnp.int32).reshape(1)
    slab = lax.axis_index("slab").astype(jnp.int32).reshape(1)
    shape = jax.ShapeDtypeStruct
    cells, death, divide = (x.reshape(1, agents) for x in (agent_cell, death_flag, divide_flag))
    move, route = slab_move.reshape(1, agents), depth_route.reshape(1, agents)
    half = ny // 16
    if agents % nz or nx * ny > PART or nz % PART or depths < 4:
        raise ValueError("list digits")
    arguments = (
        cells, nutrient, divide, uptake_weight.reshape(1, width), species, death,
        move, route, net_weight, sensing.reshape(1, width),
    )
    (
        nutrient, places, field_a, field_b, cells, divide, weight, species, death, move, route, net_weight, sensing
    ) = pl.pallas_call(
        load_kernel,
        out_shape=(
            shape((nx, ny, nz), F32),
            shape((nz, agents), BF16),
            shape((HALO * half, 16, nz), BF16),
            shape((HALO * half, 16, nz), BF16),
        )
        + tuple(shape(x.shape, x.dtype) for i, x in enumerate(arguments) if i != 1),
        in_specs=[SMEM_SPEC] + [HBM_SPEC] * len(arguments),
        out_specs=[VMEM_SPEC] * (4 + len(arguments) - 1),
        scratch_shapes=[
            pltpu.VMEM((nx, ny, nz), F32),
            pltpu.SemaphoreType.DMA((len(arguments),)),
        ],
        compiler_params=PARAMS,
        name="load",
    )(slab, *(pltpu.with_memory_space_constraint(x, pltpu.HBM) for x in arguments))
    target, sensed, depth_a, depth_b, agent_list = pl.pallas_call(
        uptake_kernel,
        out_shape=(
            shape((nx, ny, nz), F32),
            shape((8, agents), F32),
            shape((nx // 2, 16, nz), BF16),
            shape((nx // 2, 16, nz), BF16),
            shape((4 * agents // nz, nz), F32),
        ),
        in_specs=[SMEM_SPEC] + [VMEM_SPEC] * 7,
        out_specs=[VMEM_SPEC] * 5,
        compiler_params=PARAMS,
        cost_estimate=pl.CostEstimate(flops=1 << 31, bytes_accessed=1 << 20, transcendentals=0),
        name="uptake",
    )(me, nutrient, places, cells, divide, weight, species, death)
    field_a, field_b, depth_a, depth_b = lax.optimization_barrier((field_a, field_b, depth_a, depth_b))
    side_a = swapped(depth_a, "depth", "a")
    side_b = swapped(depth_b, "depth", "b")
    field_a = swapped(field_a, "slab", "a")
    field_b = swapped(field_b, "slab", "b")
    rows = 2 * (HALO - 1) ** 2 + agent_list.shape[0]
    rows = -(-rows // 16) * 16
    slab_a, slab_b = pl.pallas_call(
        corner_kernel,
        out_shape=tuple(shape((rows // 16, 16, nz), BF16) for _ in range(2)),
        in_specs=[SMEM_SPEC] * 2 + [VMEM_SPEC] * 3,
        out_specs=[VMEM_SPEC] * 2,
        compiler_params=PARAMS,
        name="corner",
    )(me, slab, side_a, side_b, agent_list)
    slab_a = swapped(slab_a, "slab", "a")
    slab_b = swapped(slab_b, "slab", "b")
    cx, cy, cz = nx // 2, ny // 2, nz // 2
    ext = ny + 2 * HALO
    sent = pl.pallas_call(
        network_kernel,
        out_shape=tuple(
            shape((capacity // 32, 16, 2 * width) if k == 1 else (capacity // 16, 16, width), BF16)
            for k in range(depths)
        )
        + tuple(shape((MIG * width // (16 * cz), 16, cz), BF16) for _ in range(2)),
        in_specs=[SMEM_SPEC] * 2 + [VMEM_SPEC] * 7,
        out_specs=[VMEM_SPEC] * (depths + 2),
        compiler_params=PARAMS,
        cost_estimate=pl.CostEstimate(flops=1 << 31, bytes_accessed=1<<20, transcendentals=0),
        name="network",
    )(me, slab, species, sensed, death, move, route, net_weight, sensing)
    u0, text, u1, u2, inside = pl.pallas_call(
        functools.partial(inner_kernel, depths),
        out_shape=(
            shape((nx + 2 * HALO, ext, nz), F32),
            shape((nx + 2 * HALO - 2, ext, nz), F32),
            shape((nx + 2 * HALO - 2, ext, nz), F32),
            shape((nx + 4, ext, nz), F32),
            shape((nx - 4, ny, nz), F32),
        ),
        in_specs=[SMEM_SPEC] * 2 + [VMEM_SPEC] * 6,
        out_specs=[VMEM_SPEC] * 5,
        compiler_params=PARAMS,
        cost_estimate=pl.CostEstimate(flops=1 << 20, bytes_accessed=1<<20, transcendentals=0),
        name="inner",
    )(me, slab, nutrient, target, side_a, side_b, field_a, field_b)
    slab_a, slab_b, inside, *sent = lax.optimization_barrier((slab_a, slab_b, inside, *sent))
    text, u1, u2, ct, ct_all, coarse_a, coarse_b = pl.pallas_call(
        functools.partial(smooth_kernel, depths, agents),
        out_shape=(
            shape(text.shape, F32),
            shape(u1.shape, F32),
            shape(u2.shape, F32),
            shape((cx, cy, cz), F32),
            shape((cx, cy, cz), BF16),
            shape((1, cx * HALO, cz), BF16),
            shape((1, cx * HALO, cz), BF16),
        ),
        in_specs=[SMEM_SPEC] * 2 + [VMEM_SPEC] * 7,
        out_specs=[VMEM_SPEC] * 7,
        scratch_shapes=[
            pltpu.VMEM((cx, cz // LANES, ny + 8, LANES), F32),
            pltpu.VMEM((2, (HALO - 1) * ny, nz), F32),
        ],
        input_output_aliases={3: 0, 4: 1, 5: 2},
        compiler_params=PARAMS,
        name="smooth",
    )(me, slab, u0, text, u1, u2, inside, slab_a, slab_b)
    coarse_a = swapped(jnp.concatenate([coarse_a, sent[1]], axis=0), "depth", "a")
    coarse_b = swapped(coarse_b, "depth", "b")
    arrived = [sent[0], swapped(sent[2], "depth", "b")]
    arrived += [cyclic(sent[k + 1], "depth", k) for k in range(2, depths - 1)]
    tail_a, tail_b = (
        swapped(jnp.concatenate([ct_all, coarse_a[:1], coarse_b, movers], axis=0), "slab", which)
        for which, movers in (("a", sent[depths]), ("b", sent[depths + 1]))
    )
    base, back = pl.pallas_call(
        functools.partial(post_kernel, depths),
        out_shape=(shape((nx, ny, nz), F32), shape((nz, nz), BF16)),
        in_specs=[SMEM_SPEC] + [VMEM_SPEC] * 3,
        out_specs=[VMEM_SPEC] * 2,
        scratch_shapes=[pltpu.VMEM((nx + 2, ext, nz), F32), pltpu.VMEM((nx + 4, ext, nz), F32)],
        compiler_params=PARAMS,
        cost_estimate=pl.CostEstimate(flops=1 << 30, bytes_accessed=1 << 22, transcendentals=0),
        name="post",
    )(me, u1, u2, text)
    grid_field, agents_out = pl.pallas_call(
        functools.partial(correct_kernel, depths),
        out_shape=(
            shape((nx, ny, nz), F32),
            shape(((depths * capacity + 2 * MIG) // 16, 16, width), BF16),
        ),
        in_specs=[SMEM_SPEC] * 2 + [VMEM_SPEC] * 7 + [ANY_SPEC] * (depths - 1),
        out_specs=[HBM_SPEC, ANY_SPEC],
        scratch_shapes=[
            pltpu.VMEM((cx + 2, cz // LANES, ext + 8, LANES), F32),
            pltpu.VMEM((nx, ny, nz), F32),
            pltpu.SemaphoreType.DMA((depths + 5 + nx,)),
        ],
        compiler_params=PARAMS,
        name="correct",
    )(me, slab, ct, coarse_a, coarse_b, tail_a, tail_b, base, back, *arrived)
    return grid_field, agents_out.reshape(-1, width)


def solution(mesh):
    rows = P(("slab", "depth"))
    in_specs = (
        P("slab", "depth", None),
        P(("slab", "depth"), None),
        rows,
        rows,
        rows,
        rows,
        P(("slab", "depth"), None),
        P(),
        P(),
        P(),
    )
    out_specs = (P("slab", "depth", None), P(("slab", "depth"), None))
    return jax.shard_map(local, mesh=mesh, in_specs=in_specs, out_specs=out_specs, check_vma=False)
```

```python
import functools

import jax
import jax.numpy as jnp
from jax import lax
from jax.experimental import pallas as pl
from jax.experimental.pallas import tpu as pltpu
from jax.sharding import PartitionSpec as P

MIG = 128
PART = 256
SCREENING = 0.05
DAMPING = 2.0 / 3.0
CENTRE = 6.0 + SCREENING
COARSE_CENTRE = 6.0 + 4.0 * SCREENING
HALO = 4
F32, BF16 = jnp.float32, jnp.bfloat16
VMEM_SPEC = pl.BlockSpec(memory_space=pltpu.VMEM)
ANY_SPEC = pl.BlockSpec(memory_space=pl.ANY)
HBM_SPEC = pl.BlockSpec(memory_space=pltpu.HBM)
SMEM_SPEC = pl.BlockSpec(memory_space=pltpu.SMEM)
PARAMS = pltpu.CompilerParams(vmem_limit_bytes=40 * 1024 * 1024)


def dot(a, b, ca, cb):
    return lax.dot_general(a, b, (((ca,), (cb,)), ((), ())), preferred_element_type=F32)


def halves(x):
    high = x.astype(BF16)
    return high, (x - high.astype(F32)).astype(BF16)


def iota(shape, dim):
    return lax.broadcasted_iota(jnp.int32, shape, dim)


def cyclic(x, axis, by):
    count = lax.axis_size(axis)
    return lax.ppermute(x, axis, [(i, (i + by) % count) for i in range(count)])


def swapped(x, axis, which):
    count = lax.axis_size(axis)
    if count % 2:
        raise ValueError("odd axis")
    first = 0 if which == "a" else 1
    pairs = []
    for i in range(first, count, 2):
        j = (i + 1) % count
        pairs += [(i, j), (j, i)]
    return lax.ppermute(x, axis, sorted(pairs))


def is_even(x):
    return lax.rem(x, 2) == 0


LANES = 128


def shuffle(nz, back):
    one, two = iota((nz, nz), 0), iota((nz, nz), 1)
    if back:
        one, two = two, one
    return (one == (two % LANES) * (nz // LANES) + two // LANES).astype(F32).astype(BF16)


def load_kernel(slab_ref, *refs):
    count = 10
    sources, refs = refs[:count], refs[count:]
    u_ref, place_ref, field_a, field_b, *targets = refs[:-2]
    raw, sem = refs[-2:]
    cell_ref = targets[0]
    targets.insert(1, raw)
    copies = [
        pltpu.make_async_copy(source, target, sem.at[i])
        for i, (source, target) in enumerate(zip(sources, targets, strict=True))
    ]
    for copy in copies:
        copy.start()
    nx, ny, nz = u_ref.shape
    rows = nx * ny
    tiles = nz // LANES
    order = shuffle(nz, False)
    copies[0].wait()
    cell_z = cell_ref[...] % nz
    cell_z = (cell_z % tiles) * LANES + cell_z // tiles
    place_ref[...] = (iota(place_ref.shape, 0) == cell_z).astype(F32).astype(BF16)
    copies[1].wait()
    high, low = halves(raw[...].reshape(rows, nz))
    both = dot(jnp.concatenate([high, low], axis=0), order, 1, 0)
    u_ref[...] = (both[:rows] + both[rows:]).reshape(nx, ny, nz)
    half = ny // 16
    slab_even = is_even(slab_ref[0])
    for ref, front in ((field_a, slab_even), (field_b, jnp.logical_not(slab_even))):
        start = jnp.where(front, nx - HALO, 0)
        for k in range(HALO):
            ref[k * half : (k + 1) * half] = u_ref[start + k].astype(BF16).reshape(half, 16, nz)
    for copy in copies[2:]:
        copy.wait()


def uptake_kernel(
    me_ref, u_ref, place_ref, cell_ref, divide_ref, weight_ref, species_ref, death_ref,
    t_ref, sensed_ref, depth_a, depth_b, list_ref,
):
    nx, ny, nz = u_ref.shape
    agents = species_ref.shape[0]
    rows = nx * ny
    tiles = nz // LANES
    cell = cell_ref[...]
    cell_row = cell // nz
    cell_z = cell - cell_row * nz
    cell_z = (cell_z % tiles) * LANES + cell_z // tiles
    one_z = place_ref[...]
    in_row = iota((rows, agents), 0) == cell_row
    u = u_ref[...].reshape(rows, nz)
    picked = dot(u.astype(BF16), one_z, 1, 0)
    sample = jnp.sum(jnp.where(in_row, picked, 0.0), axis=0, keepdims=True)
    sensed_ref[...] = jnp.broadcast_to(sample, (8, agents))
    weight = jnp.broadcast_to(weight_ref[...].reshape(1, -1), (8, species_ref.shape[1]))
    score = dot(weight, species_ref[...], 1, 1)[0:1]
    softplus = jnp.maximum(score, 0.0) + jnp.log1p(jnp.exp(-jnp.abs(score)))
    alive = (1 - death_ref[...].reshape(1, agents)).astype(F32)
    divide = divide_ref[...].reshape(1, agents).astype(F32)
    uptake = alive * (1.0 + divide) * softplus * sample / (0.5 + sample)
    up_high = uptake.astype(BF16).astype(F32)
    source = dot(jnp.where(in_row, up_high, 0.0).astype(BF16), one_z, 1, 1)
    t_ref[...] = (SCREENING * u - source).reshape(nx, ny, nz)
    even = is_even(me_ref[0])
    for pair in range(nx // 2):
        parts = []
        for start in (0, ny - HALO):
            for plane in (2 * pair, 2 * pair + 1):
                parts.append(u_ref[plane, start : start + HALO])
                parts.append(t_ref[plane, start : start + HALO])
        low = jnp.concatenate(parts[:4], axis=0)
        high = jnp.concatenate(parts[4:], axis=0)
        depth_a[pair] = jnp.where(even, high, low).astype(BF16)
        depth_b[pair] = jnp.where(even, low, high).astype(BF16)
    part = cell_z // PART
    values = (cell_row.astype(F32), (cell_z - part * PART).astype(F32), part.astype(F32), up_high)
    list_ref[...] = jnp.concatenate(
        [x[:, i * nz : (i + 1) * nz] for x in values for i in range(agents // nz)], axis=0
    )


def network_kernel(
    me_ref, slab_ref, species_ref, sensed_ref, death_ref, move_ref, route_ref, net_ref, sensing_ref, *outs
):
    agents, width = species_ref.shape
    depths = len(outs) - 2
    capacity = outs[0].shape[0] * 16
    species = species_ref[...]
    sensing = sensing_ref[...].reshape(1, width)
    first = sensing.astype(BF16)
    rest = sensing - first.astype(F32)
    second = rest.astype(BF16)
    third = (rest - second.astype(F32)).astype(BF16)
    line = iota((8, width), 0)
    terms = jnp.where(
        line == 0, first.astype(F32),
        jnp.where(line == 1, second.astype(F32), jnp.where(line == 2, third.astype(F32), 0.0)),
    ).astype(BF16)
    activation = dot(species, net_ref[...], 1, 0) + dot(sensed_ref[...].astype(BF16), terms, 0, 0)
    updated = (0.5 * species.astype(F32) + jnp.tanh(activation)).astype(BF16)
    lanes = 128
    lines = -(-(depths + 2) // 8) * 8
    line = iota((lines, lanes), 0)
    square = iota((lanes, 2 * lanes), 0)
    column = iota((lanes, 2 * lanes), 1)
    counter = jnp.where(jnp.logical_or(column >= lanes, square < column), 1.0, 0.0).astype(BF16)
    blocks = agents // lanes
    route = route_ref[...].reshape(1, agents)
    move = move_ref[...].reshape(1, agents)
    death = death_ref[...].reshape(1, agents)
    hits = []
    for block in range(blocks):
        cut = slice(block * lanes, (block + 1) * lanes)
        wanted = jnp.where(line < depths, route[:, cut], jnp.where(line < depths + 2, move[:, cut] + (depths - 1), -1))
        hits.append((wanted == line).astype(F32))
    counts = dot(jnp.concatenate(hits, axis=0).astype(BF16), counter, 1, 0)
    me = me_ref[0]
    to_a = jnp.where(is_even(slab_ref[0]), 1, 2)
    hop_a = jnp.where(is_even(me), 1, depths - 1)
    running = jnp.zeros((lines, lanes), F32)
    keys = []
    for block in range(blocks):
        cut = slice(block * lanes, (block + 1) * lanes)
        own = slice(block * lines, (block + 1) * lines)
        before = (counts[own, :lanes] + running) * hits[block]
        running = running + counts[own, lanes:]
        slot = jnp.sum(jnp.where(line < depths, before, 0.0), axis=0, keepdims=True).astype(jnp.int32)
        rank = jnp.sum(jnp.where(line < depths, 0.0, before), axis=0, keepdims=True).astype(jnp.int32)
        hop = route[:, cut] - me
        hop = jnp.where(hop < 0, hop + depths, hop)
        hop = jnp.where(hop == hop_a, 1, jnp.where(hop == depths - hop_a, 2, jnp.where(hop == 0, 0, hop + 1)))
        key = jnp.where(
            move[:, cut] == 0,
            hop * capacity + slot,
            depths * capacity + jnp.where(move[:, cut] == to_a, 0, MIG) + rank,
        )
        keys.append(jnp.where(death[:, cut] == 0, key, -1))
    key = jnp.concatenate(keys, axis=1)
    start = 0
    for index, out in enumerate(outs):
        size = capacity if index < depths else MIG
        chosen = (iota((size, agents), 0) == key - start).astype(F32).astype(BF16)
        placed = dot(chosen, updated, 1, 0).astype(BF16)
        start += size
        blocks = out.shape[0]
        for i in range(0, out.shape[2], width):
            part = placed[i // width * blocks * 16 :][: blocks * 16]
            out[:, :, i : i + width] = part.reshape(blocks, 16, width)


def tiles_of(x):
    return [x[:, i : i + LANES] for i in range(0, x.shape[1], LANES)]


def third_sum(x):
    parts = tiles_of(x)
    lane = iota((x.shape[0], LANES), 1)
    before = jnp.where(lane == 0, 0.0, pltpu.roll(parts[-1], 1, 1))
    after = jnp.where(lane == LANES - 1, 0.0, pltpu.roll(parts[0], LANES - 1, 1))
    padded = [before] + parts + [after]
    return jnp.concatenate([x + y for x, y in zip(padded[:-2], padded[2:])], axis=1)


def neighbour_total(before, plane, after):
    rows = plane.shape[0]
    second = pltpu.roll(plane, 1, 0) + pltpu.roll(plane, rows - 1, 0)
    return before + after + second + third_sum(plane)


def relaxed(before, plane, after, target, centre):
    return (1.0 - DAMPING) * plane + (DAMPING / centre) * (
        target + neighbour_total(before, plane, after)
    )


def edge_mask(me, depths, halo):
    row = iota((2 * halo, 1), 0)
    return jnp.where(
        row < halo, (me < depths - 1).astype(F32), (me > 0).astype(F32)
    )


def masked(plane, own, mask):
    return jnp.concatenate([plane[:own], plane[own:] * mask], axis=0)


def halo_rows(side_a, side_b, even, plane, mask):
    at = 2 * HALO * (plane % 2)
    side_a = side_a[at : at + 2 * HALO].astype(F32)
    side_b = side_b[at : at + 2 * HALO].astype(F32)
    high = jnp.where(even, side_a, side_b)
    low = jnp.where(even, side_b, side_a)
    return (
        jnp.concatenate([high[:HALO], low[:HALO]], axis=0) * mask,
        jnp.concatenate([high[HALO:], low[HALO:]], axis=0),
    )


def corner_kernel(me_ref, slab_ref, side_a, side_b, list_ref, slab_a, slab_b):
    layers = 2 * side_a.shape[0]
    nz = side_a.shape[2]
    even = is_even(me_ref[0])
    slab_even = is_even(slab_ref[0])

    def layer(side, plane):
        at = 2 * HALO * (plane % 2)
        return side[plane // 2].astype(F32)[at : at + 2 * HALO]

    for ref, front in ((slab_a, slab_even), (slab_b, jnp.logical_not(slab_even))):
        parts = []
        for side, high in ((side_a, even), (side_b, jnp.logical_not(even))):
            targets = []
            for i in range(1, HALO):
                x = jnp.where(front, layer(side, layers - i), layer(side, i - 1))
                parts.append(jnp.where(high, x[: HALO - i], x[i:HALO]))
                if i < HALO - 1:
                    targets.append(
                        jnp.where(high, x[HALO : 2 * HALO - 1 - i], x[HALO + 1 + i :])
                    )
            parts += targets
        parts.append(list_ref[...])
        used = sum(part.shape[0] for part in parts)
        total = ref.shape[0] * ref.shape[1]
        parts.append(jnp.zeros((total - used, nz), F32))
        ref[...] = jnp.concatenate(parts, axis=0).astype(BF16).reshape(ref.shape)


def corner_rows(block_a, block_b, even, mask):
    high = jnp.where(even, block_a, block_b)
    low = jnp.where(even, block_b, block_a)
    nz = high.shape[1]
    fields, targets = [], []
    at = 0
    for rows, out in ((HALO, fields), (HALO - 1, targets)):
        for i in range(1, rows):
            count = rows - i
            gap = jnp.zeros((2 * (HALO - count), nz), F32)
            cut = slice(at, at + count)
            out.append(jnp.concatenate([high[cut], gap, low[cut]], axis=0) * mask)
            at += count
    return fields, targets + [jnp.zeros_like(fields[0])]


KEEP, PULL = 1.0 - DAMPING, DAMPING / CENTRE


def inner_kernel(
    depths, me_ref, slab_ref, u_ref, t_ref, side_a, side_b, field_a, field_b, u0, text_ref, u1, u2_ref, inside
):
    nx, ny, nz = u_ref.shape
    even = is_even(me_ref[0])
    slab_even = is_even(slab_ref[0])
    half = ny // 16
    mask = edge_mask(me_ref[0], depths, HALO)
    for field, after in ((field_a, slab_even), (field_b, jnp.logical_not(slab_even))):
        u_at = jnp.where(after, HALO + nx, 0)
        for k in range(HALO):
            u0[u_at + k, :ny] = field[k * half : (k + 1) * half].astype(F32).reshape(ny, nz)
            u0[u_at + k, ny:] = jnp.zeros((2 * HALO, nz), F32)
    for plane in range(nx):
        u0[HALO + plane, :ny] = u_ref[plane]
        text_ref[HALO - 1 + plane, :ny] = t_ref[plane]
        uh, th = halo_rows(side_a[plane // 2], side_b[plane // 2], even, plane, mask)
        u0[HALO + plane, ny:] = uh
        text_ref[HALO - 1 + plane, ny:] = th

    def outer(i, carry):
        for p in (i, nx + HALO - 1 + i):
            u1[p] = KEEP * u0[p + 1] + PULL * neighbour_total(u0[p], u0[p + 1], u0[p + 2])
        return carry

    lax.fori_loop(0, HALO - 1, outer, 0, unroll=True)

    def first(p, carry):
        v = relaxed(u0[p], u0[p + 1], u0[p + 2], text_ref[p], CENTRE)
        u1[p] = masked(v, ny, mask)
        return carry

    lax.fori_loop(HALO - 1, nx + HALO - 1, first, 0, unroll=4)

    def second(p, carry):
        v = relaxed(u1[p], u1[p + 1], u1[p + 2], text_ref[p + 1], CENTRE)
        u2_ref[p] = masked(v, ny, mask)
        return carry

    lax.fori_loop(HALO - 1, nx + 1, second, 0, unroll=3)
    for p in range(2, nx - 2):
        inside[p - 2] = residual(u2_ref, text_ref, p, ny)


def residual(u2_ref, text_ref, p, ny):
    v = u2_ref[p + 2]
    total = neighbour_total(u2_ref[p + 1], v, u2_ref[p + 3])
    return (text_ref[p + 3] - CENTRE * v + total)[:ny]


def smooth_kernel(
    depths, agents, me_ref, slab_ref, u0, text_in, u1_in, u2_in, inside, slab_a, slab_b,
    text_ref, u1, u2_ref, coarse_ref, coarse_all_ref, coarse_a, coarse_b, paired, foreign,
):
    nx = u0.shape[0] - 2 * HALO
    ny, nz = u0.shape[1] - 2 * HALO, u0.shape[2]
    mask = edge_mask(me_ref[0], depths, HALO)
    even = is_even(me_ref[0])
    slab_even = is_even(slab_ref[0])
    near = HALO - 1
    corner = HALO * near // 2 + near * (near - 1) // 2
    row = iota((8, 1), 0)
    first, last = (row == 0).astype(F32), (row == 7).astype(F32)
    sides = ((slab_a, slab_even), (slab_b, jnp.logical_not(slab_even)))
    messages = []
    lines = agents // nz
    for side, (ref, after) in enumerate(sides):
        message = ref[...].astype(F32).reshape(-1, nz)
        messages.append(message)
        cell_row, place, part, uptake = (
            jnp.concatenate([message[at + i : at + i + 1] for i in range(lines)], axis=1)
            for at in range(2 * corner, 2 * corner + 4 * lines, lines)
        )
        cell_row = cell_row.astype(jnp.int32) - jnp.where(after, 0, (nx - near) * ny)
        wanted = jnp.logical_and(cell_row >= 0, cell_row < near * ny)
        key = jnp.where(wanted, part.astype(jnp.int32) * (near * ny) + cell_row, -1)
        one_z = (iota((PART, agents), 0) == place.astype(jnp.int32)).astype(F32).astype(BF16)
        key_rows = iota((near * ny * (nz // PART), agents), 0)
        taken = jnp.where(key_rows == key, uptake, 0.0).astype(BF16)
        source = dot(taken, one_z, 1, 1)
        for i in range(nz // PART):
            foreign[side, :, i * PART : (i + 1) * PART] = source[i * near * ny : (i + 1) * near * ny]
    for side, (_, after) in enumerate(sides):
        message = messages[side]
        fields, targets = corner_rows(message[:corner], message[corner : 2 * corner], even, mask)
        sign = jnp.where(after, 1, -1)
        edge = jnp.where(after, nx - 1, 0)
        for i in range(1, HALO):
            p = edge + sign * i
            index = jnp.where(after, i - 1, HALO - 1 - i)
            t = SCREENING * u0[p + 4, :ny] - foreign[side, pl.ds(index * ny, ny)]
            text_ref[p + 3, :ny] = t
            text_ref[p + 3, ny:] = targets[i - 1]
            x = fields[i - 1]
            nearer = u0[p + 4 - sign, ny:] if i == 1 else fields[i - 2]
            total = nearer + third_sum(x)
            if i < HALO - 1:
                total = total + fields[i]
            beyond = u0[p + 4]
            up = jnp.where(row == 0, beyond[ny - 1 : ny], pltpu.roll(x, 1, 0))
            down = jnp.where(row == 7, beyond[0:1], pltpu.roll(x, 7, 0))
            u1[p + 3, ny:] = (KEEP * x + PULL * (targets[i - 1] + total + up + down)) * mask
            v = u1[p + 3, :ny] + PULL * t
            u1[p + 3, :ny] = v
            u1[p + 3, 0:8] = v[0:8] + (PULL * first) * x[7:8]
            u1[p + 3, ny - 8 : ny] = v[ny - 8 :] + (PULL * last) * x[0:1]
        u1[edge + 3, ny:] = u1[edge + 3, ny:] + PULL * fields[0]
        u2_ref[edge - sign + 2, ny:] = u2_ref[edge - sign + 2, ny:] + (PULL * PULL) * fields[0]

    for p in (1, 2, nx + 1, nx + 2):
        v = relaxed(u1[p], u1[p + 1], u1[p + 2], text_ref[p + 1], CENTRE)
        u2_ref[p] = masked(v, ny, mask)
    for q in range(nx // 2):
        both = 0.0
        for p in (2 * q, 2 * q + 1):
            known = 2 <= p < nx - 2
            both = both + (inside[p - 2] if known else residual(u2_ref, text_ref, p, ny))
        parts = tiles_of(both)
        for i in range(len(parts) // 2):
            paired[q, i, :ny] = parts[2 * i] + parts[2 * i + 1]
    cx, cy, cz = coarse_ref.shape
    coarse = jnp.concatenate(
        [
            jnp.concatenate(
                [
                    paired[q, i, pl.ds(0, cy, 2), :] + paired[q, i, pl.ds(1, cy, 2), :]
                    for i in range(cz // LANES)
                ],
                axis=1,
            )
            for q in range(cx)
        ],
        axis=0,
    )
    coarse = 0.5 * coarse
    coarse_ref[...] = coarse.reshape(cx, cy, cz)
    coarse_all_ref[...] = coarse.astype(BF16).reshape(cx, cy, cz)
    low, high = (
        jnp.concatenate([coarse_ref[q, start : start + HALO] for q in range(cx)], axis=0)
        for start in (0, cy - HALO)
    )
    coarse_a[0] = jnp.where(even, high, low).astype(BF16)
    coarse_b[0] = jnp.where(even, low, high).astype(BF16)


def post_kernel(depths, me_ref, u1, u2_in, text_ref, out_ref, back_ref, v1, u2_ref):
    nx, ny, nz = out_ref.shape
    back = shuffle(nz, True)
    back_ref[...] = back
    mask = edge_mask(me_ref[0], depths, HALO)
    last = nx + 3
    for p in range(1, last):
        u2_ref[p] = u2_in[p]
    for p in (0, last):
        v = relaxed(u1[p], u1[p + 1], u1[p + 2], text_ref[p + 1], CENTRE)
        u2_ref[p] = masked(v, ny, mask)

    def first(p, carry):
        v = relaxed(u2_ref[p], u2_ref[p + 1], u2_ref[p + 2], text_ref[p + 2], CENTRE)
        v1[p] = masked(v, ny, mask)
        return carry

    lax.fori_loop(0, nx + 2, first, 0, unroll=2)

    def second(p, carry):
        v = relaxed(v1[p], v1[p + 1], v1[p + 2], text_ref[p + 3], CENTRE)
        out_ref[p] = v[:ny]
        return carry

    lax.fori_loop(0, nx, second, 0, unroll=2)
    high, low = halves(out_ref[...].reshape(nx * ny, nz))
    both = dot(jnp.concatenate([high, low], axis=0), back, 1, 0)
    out_ref[...] = (both[: nx * ny] + both[nx * ny :]).reshape(nx, ny, nz)


def correct_kernel(
    depths, me_ref, slab_ref, ct_ref, side_a, side_b, slab_a, slab_b, base_ref, back_ref, *rest
):
    packed = rest[: depths - 1]
    out_any, agents_ref, fine, out_ref, sem = rest[depths - 1 :]
    nx, ny, nz = out_ref.shape
    cx, cy, cz = ct_ref.shape
    me = me_ref[0]
    even = is_even(me)
    slab_even = is_even(slab_ref[0])
    blocks = packed[0].shape[0]
    width = agents_ref.shape[2]
    copies = []

    def place(source, start):
        target = agents_ref.at[pl.ds(start, source.shape[0])]
        copies.append(pltpu.make_async_copy(source, target, sem.at[len(copies)]))
        copies[-1].start()

    def place_wide(source, start):
        for i in range(source.shape[2] // width):
            part = source.at[:, :, pl.ds(i * width, width)]
            place(part, start + i * source.shape[0])

    up = jnp.where(me == depths - 1, 0, me + 1)
    down = jnp.where(me == 0, depths - 1, me - 1)
    place(packed[0], me * blocks)
    place_wide(side_a.at[pl.ds(1, side_a.shape[0] - 1)], jnp.where(even, up, down) * blocks)
    place(packed[1], jnp.where(even, down, up) * blocks)
    for k in range(2, depths - 1):
        origin = me - k
        place(packed[k], jnp.where(origin < 0, origin + depths, origin) * blocks)
    for ref, late in ((slab_a, slab_even), (slab_b, jnp.logical_not(slab_even))):
        start = depths * blocks + jnp.where(late, MIG // 16, 0)
        place_wide(ref.at[pl.ds(cx + 2, ref.shape[0] - cx - 2)], start)
    mask = edge_mask(me, depths, HALO)

    def chosen(condition, x, y):
        return jnp.where(condition, x.astype(F32), y.astype(F32))

    planes = []
    for p in range(cx + 2 * HALO):
        if HALO <= p < HALO + cx:
            k = p - HALO
            own, one, two = ct_ref[k], side_a[0].astype(F32), side_b[0].astype(F32)
        else:
            before = p < HALO
            k = p + cx - HALO if before else p - HALO - cx
            x, y = (slab_b, slab_a) if before else (slab_a, slab_b)
            own, one, two = (chosen(slab_even, x[i], y[i]) for i in (k, cx, cx + 1))
        rows = slice(HALO * k, HALO * (k + 1))
        one, two = one[rows], two[rows]
        sides = jnp.concatenate([jnp.where(even, one, two), jnp.where(even, two, one)], axis=0)
        planes.append(jnp.concatenate([own, sides * mask], axis=0))
    values = [(DAMPING / COARSE_CENTRE) * plane for plane in planes]
    for sweep in range(1, HALO):
        values = [
            masked(
                relaxed(values[i - 1], values[i], values[i + 1], planes[i + sweep - 1], COARSE_CENTRE),
                cy,
                mask,
            )
            for i in range(1, len(values) - 1)
        ]
    wide = cy + 4
    for q, value in enumerate(values):
        value = jnp.concatenate([value[: cy + 2], value[cy + 2 * HALO - 2 :]], axis=0)
        for i, part in enumerate(tiles_of(value)):
            fine[q, i, pl.ds(0, wide, 2), :] = part
            fine[q, i, pl.ds(1, wide, 2), :] = part
    def second_total(plane):
        rows = plane.shape[0]
        return pltpu.roll(plane, 1, 0) + pltpu.roll(plane, rows - 1, 0)

    spread = [jnp.concatenate([fine[q, i, : 2 * wide] for i in range(cz // LANES)], axis=1) for q in range(cx + 2)]
    still = [KEEP * plane + PULL * second_total(plane) for plane in spread]
    once = []
    for p in range(-1, nx + 1):
        q = (p + 2) // 2
        if p % 2 == 0:
            others = spread[q - 1] + spread[q]
        else:
            others = spread[q] + spread[q + 1]
        once.append(masked(still[q] + PULL * others, ny, mask))

    def twice(plane):
        return jnp.concatenate([part for part in tiles_of(plane) for _ in range(2)], axis=1)

    back = back_ref[...]
    bounds = (0, nx // 2, nx // 4 * 3, nx)
    for start, end in zip(bounds, bounds[1:]):
        planes = []
        for p in range(start, end):
            plane = once[p + 1]
            total = once[p] + once[p + 2] + second_total(plane)
            none = (KEEP * plane + PULL * total)[:ny]
            one = (2.0 * PULL) * plane[:ny]
            two = (PULL * PULL) * spread[(p + 2) // 2][:ny]
            planes.append(twice(none) + third_sum(twice(one) + third_sum(twice(two))))
        done = dot(jnp.concatenate(planes, axis=0).astype(BF16), back, 1, 0)
        out_ref[start:end] = base_ref[start:end] + done.reshape(end - start, ny, nz)
        for p in range(start, end):
            copies.append(pltpu.make_async_copy(out_ref.at[p], out_any.at[p], sem.at[len(copies)]))
            copies[-1].start()
    for copy in copies:
        copy.wait()


def local(
    nutrient, species, agent_cell, death_flag, divide_flag, slab_move, depth_route, net_weight, sensing, uptake_weight
):
    depths = lax.axis_size("depth")
    nx, ny, nz = nutrient.shape
    agents, width = species.shape
    capacity = 2 * agents // depths
    me = lax.axis_index("depth").astype(jnp.int32).reshape(1)
    slab = lax.axis_index("slab").astype(jnp.int32).reshape(1)
    shape = jax.ShapeDtypeStruct
    cells, death, divide = (x.reshape(1, agents) for x in (agent_cell, death_flag, divide_flag))
    move, route = slab_move.reshape(1, agents), depth_route.reshape(1, agents)
    half = ny // 16
    if agents % nz or nx * ny > PART or nz % PART or depths < 4:
        raise ValueError("list digits")
    arguments = (
        cells, nutrient, divide, uptake_weight.reshape(1, width), species, death,
        move, route, net_weight, sensing.reshape(1, width),
    )
    (
        nutrient, places, field_a, field_b, cells, divide, weight, species, death, move, route, net_weight, sensing
    ) = pl.pallas_call(
        load_kernel,
        out_shape=(
            shape((nx, ny, nz), F32),
            shape((nz, agents), BF16),
            shape((HALO * half, 16, nz), BF16),
            shape((HALO * half, 16, nz), BF16),
        )
        + tuple(shape(x.shape, x.dtype) for i, x in enumerate(arguments) if i != 1),
        in_specs=[SMEM_SPEC] + [HBM_SPEC] * len(arguments),
        out_specs=[VMEM_SPEC] * (4 + len(arguments) - 1),
        scratch_shapes=[
            pltpu.VMEM((nx, ny, nz), F32),
            pltpu.SemaphoreType.DMA((len(arguments),)),
        ],
        compiler_params=PARAMS,
        name="load",
    )(slab, *(pltpu.with_memory_space_constraint(x, pltpu.HBM) for x in arguments))
    target, sensed, depth_a, depth_b, agent_list = pl.pallas_call(
        uptake_kernel,
        out_shape=(
            shape((nx, ny, nz), F32),
            shape((8, agents), F32),
            shape((nx // 2, 16, nz), BF16),
            shape((nx // 2, 16, nz), BF16),
            shape((4 * agents // nz, nz), F32),
        ),
        in_specs=[SMEM_SPEC] + [VMEM_SPEC] * 7,
        out_specs=[VMEM_SPEC] * 5,
        compiler_params=PARAMS,
        cost_estimate=pl.CostEstimate(flops=1 << 31, bytes_accessed=1 << 20, transcendentals=0),
        name="uptake",
    )(me, nutrient, places, cells, divide, weight, species, death)
    field_a, field_b, depth_a, depth_b = lax.optimization_barrier((field_a, field_b, depth_a, depth_b))
    side_a = swapped(depth_a, "depth", "a")
    side_b = swapped(depth_b, "depth", "b")
    field_a = swapped(field_a, "slab", "a")
    field_b = swapped(field_b, "slab", "b")
    rows = 2 * (HALO - 1) ** 2 + agent_list.shape[0]
    rows = -(-rows // 16) * 16
    slab_a, slab_b = pl.pallas_call(
        corner_kernel,
        out_shape=tuple(shape((rows // 16, 16, nz), BF16) for _ in range(2)),
        in_specs=[SMEM_SPEC] * 2 + [VMEM_SPEC] * 3,
        out_specs=[VMEM_SPEC] * 2,
        compiler_params=PARAMS,
        name="corner",
    )(me, slab, side_a, side_b, agent_list)
    slab_a = swapped(slab_a, "slab", "a")
    slab_b = swapped(slab_b, "slab", "b")
    cx, cy, cz = nx // 2, ny // 2, nz // 2
    ext = ny + 2 * HALO
    sent = pl.pallas_call(
        network_kernel,
        out_shape=tuple(
            shape((capacity // 32, 16, 2 * width) if k == 1 else (capacity // 16, 16, width), BF16)
            for k in range(depths)
        )
        + tuple(shape((MIG * width // (16 * cz), 16, cz), BF16) for _ in range(2)),
        in_specs=[SMEM_SPEC] * 2 + [VMEM_SPEC] * 7,
        out_specs=[VMEM_SPEC] * (depths + 2),
        compiler_params=PARAMS,
        cost_estimate=pl.CostEstimate(flops=1 << 31, bytes_accessed=1<<20, transcendentals=0),
        name="network",
    )(me, slab, species, sensed, death, move, route, net_weight, sensing)
    u0, text, u1, u2, inside = pl.pallas_call(
        functools.partial(inner_kernel, depths),
        out_shape=(
            shape((nx + 2 * HALO, ext, nz), F32),
            shape((nx + 2 * HALO - 2, ext, nz), F32),
            shape((nx + 2 * HALO - 2, ext, nz), F32),
            shape((nx + 4, ext, nz), F32),
            shape((nx - 4, ny, nz), F32),
        ),
        in_specs=[SMEM_SPEC] * 2 + [VMEM_SPEC] * 6,
        out_specs=[VMEM_SPEC] * 5,
        compiler_params=PARAMS,
        cost_estimate=pl.CostEstimate(flops=1 << 20, bytes_accessed=1<<20, transcendentals=0),
        name="inner",
    )(me, slab, nutrient, target, side_a, side_b, field_a, field_b)
    slab_a, slab_b, inside, *sent = lax.optimization_barrier((slab_a, slab_b, inside, *sent))
    text, u1, u2, ct, ct_all, coarse_a, coarse_b = pl.pallas_call(
        functools.partial(smooth_kernel, depths, agents),
        out_shape=(
            shape(text.shape, F32),
            shape(u1.shape, F32),
            shape(u2.shape, F32),
            shape((cx, cy, cz), F32),
            shape((cx, cy, cz), BF16),
            shape((1, cx * HALO, cz), BF16),
            shape((1, cx * HALO, cz), BF16),
        ),
        in_specs=[SMEM_SPEC] * 2 + [VMEM_SPEC] * 7,
        out_specs=[VMEM_SPEC] * 7,
        scratch_shapes=[
            pltpu.VMEM((cx, cz // LANES, ny + 8, LANES), F32),
            pltpu.VMEM((2, (HALO - 1) * ny, nz), F32),
        ],
        input_output_aliases={3: 0, 4: 1, 5: 2},
        compiler_params=PARAMS,
        name="smooth",
    )(me, slab, u0, text, u1, u2, inside, slab_a, slab_b)
    coarse_a = swapped(jnp.concatenate([coarse_a, sent[1]], axis=0), "depth", "a")
    coarse_b = swapped(coarse_b, "depth", "b")
    arrived = [sent[0], swapped(sent[2], "depth", "b")]
    arrived += [cyclic(sent[k + 1], "depth", k) for k in range(2, depths - 1)]
    tail_a, tail_b = (
        swapped(jnp.concatenate([ct_all, coarse_a[:1], coarse_b, movers], axis=0), "slab", which)
        for which, movers in (("a", sent[depths]), ("b", sent[depths + 1]))
    )
    base, back = pl.pallas_call(
        functools.partial(post_kernel, depths),
        out_shape=(shape((nx, ny, nz), F32), shape((nz, nz), BF16)),
        in_specs=[SMEM_SPEC] + [VMEM_SPEC] * 3,
        out_specs=[VMEM_SPEC] * 2,
        scratch_shapes=[pltpu.VMEM((nx + 2, ext, nz), F32), pltpu.VMEM((nx + 4, ext, nz), F32)],
        compiler_params=PARAMS,
        cost_estimate=pl.CostEstimate(flops=1 << 30, bytes_accessed=1 << 22, transcendentals=0),
        name="post",
    )(me, u1, u2, text)
    grid_field, agents_out = pl.pallas_call(
        functools.partial(correct_kernel, depths),
        out_shape=(
            shape((nx, ny, nz), F32),
            shape(((depths * capacity + 2 * MIG) // 16, 16, width), BF16),
        ),
        in_specs=[SMEM_SPEC] * 2 + [VMEM_SPEC] * 7 + [ANY_SPEC] * (depths - 1),
        out_specs=[HBM_SPEC, ANY_SPEC],
        scratch_shapes=[
            pltpu.VMEM((cx + 2, cz // LANES, ext + 8, LANES), F32),
            pltpu.VMEM((nx, ny, nz), F32),
            pltpu.SemaphoreType.DMA((depths + 5 + nx,)),
        ],
        compiler_params=PARAMS,
        name="correct",
    )(me, slab, ct, coarse_a, coarse_b, tail_a, tail_b, base, back, *arrived)
    return grid_field, agents_out.reshape(-1, width)


def solution(mesh):
    rows = P(("slab", "depth"))
    in_specs = (
        P("slab", "depth", None),
        P(("slab", "depth"), None),
        rows,
        rows,
        rows,
        rows,
        P(("slab", "depth"), None),
        P(),
        P(),
        P(),
    )
    out_specs = (P("slab", "depth", None), P(("slab", "depth"), None))
    return jax.shard_map(local, mesh=mesh, in_specs=in_specs, out_specs=out_specs, check_vma=False)
```

```python
import functools

import jax
import jax.numpy as jnp
from jax import lax
from jax.experimental import pallas as pl
from jax.experimental.pallas import tpu as pltpu
from jax.sharding import PartitionSpec as P

MIG = 128
PART = 256
SCREENING = 0.05
DAMPING = 2.0 / 3.0
CENTRE = 6.0 + SCREENING
COARSE_CENTRE = 6.0 + 4.0 * SCREENING
HALO = 4
F32, BF16 = jnp.float32, jnp.bfloat16
VMEM_SPEC = pl.BlockSpec(memory_space=pltpu.VMEM)
ANY_SPEC = pl.BlockSpec(memory_space=pl.ANY)
HBM_SPEC = pl.BlockSpec(memory_space=pltpu.HBM)
SMEM_SPEC = pl.BlockSpec(memory_space=pltpu.SMEM)
PARAMS = pltpu.CompilerParams(vmem_limit_bytes=40 * 1024 * 1024)


def dot(a, b, ca, cb):
    return lax.dot_general(a, b, (((ca,), (cb,)), ((), ())), preferred_element_type=F32)


def halves(x):
    high = x.astype(BF16)
    return high, (x - high.astype(F32)).astype(BF16)


def iota(shape, dim):
    return lax.broadcasted_iota(jnp.int32, shape, dim)


def cyclic(x, axis, by):
    count = lax.axis_size(axis)
    return lax.ppermute(x, axis, [(i, (i + by) % count) for i in range(count)])


def swapped(x, axis, which):
    count = lax.axis_size(axis)
    if count % 2:
        raise ValueError("odd axis")
    first = 0 if which == "a" else 1
    pairs = []
    for i in range(first, count, 2):
        j = (i + 1) % count
        pairs += [(i, j), (j, i)]
    return lax.ppermute(x, axis, sorted(pairs))


def is_even(x):
    return lax.rem(x, 2) == 0


LANES = 128


def shuffle(nz, back):
    one, two = iota((nz, nz), 0), iota((nz, nz), 1)
    if back:
        one, two = two, one
    return (one == (two % LANES) * (nz // LANES) + two // LANES).astype(F32).astype(BF16)


def load_kernel(slab_ref, *refs):
    count = 10
    sources, refs = refs[:count], refs[count:]
    u_ref, place_ref, field_a, field_b, *targets = refs[:-2]
    raw, sem = refs[-2:]
    cell_ref = targets[0]
    targets.insert(1, raw)
    copies = [
        pltpu.make_async_copy(source, target, sem.at[i])
        for i, (source, target) in enumerate(zip(sources, targets, strict=True))
    ]
    for copy in copies:
        copy.start()
    nx, ny, nz = u_ref.shape
    rows = nx * ny
    tiles = nz // LANES
    order = shuffle(nz, False)
    copies[0].wait()
    cell_z = cell_ref[...] % nz
    cell_z = (cell_z % tiles) * LANES + cell_z // tiles
    place_ref[...] = (iota(place_ref.shape, 0) == cell_z).astype(BF16)
    copies[1].wait()
    high, low = halves(raw[...].reshape(rows, nz))
    both = dot(jnp.concatenate([high, low], axis=0), order, 1, 0)
    u_ref[...] = (both[:rows] + both[rows:]).reshape(nx, ny, nz)
    half = ny // 16
    slab_even = is_even(slab_ref[0])
    for ref, front in ((field_a, slab_even), (field_b, jnp.logical_not(slab_even))):
        start = jnp.where(front, nx - HALO, 0)
        for k in range(HALO):
            ref[k * half : (k + 1) * half] = u_ref[start + k].astype(BF16).reshape(half, 16, nz)
    for copy in copies[2:]:
        copy.wait()


def uptake_kernel(
    me_ref, u_ref, place_ref, cell_ref, divide_ref, weight_ref, species_ref, death_ref,
    t_ref, sensed_ref, depth_a, depth_b, list_ref,
):
    nx, ny, nz = u_ref.shape
    agents = species_ref.shape[0]
    rows = nx * ny
    tiles = nz // LANES
    cell = cell_ref[...]
    cell_row = cell // nz
    cell_z = cell - cell_row * nz
    cell_z = (cell_z % tiles) * LANES + cell_z // tiles
    one_z = place_ref[...]
    in_row = iota((rows, agents), 0) == cell_row
    u = u_ref[...].reshape(rows, nz)
    picked = dot(u.astype(BF16), one_z, 1, 0)
    sample = jnp.sum(jnp.where(in_row, picked, 0.0), axis=0, keepdims=True)
    sensed_ref[...] = jnp.broadcast_to(sample, (8, agents))
    weight = jnp.broadcast_to(weight_ref[...].reshape(1, -1), (8, species_ref.shape[1]))
    score = dot(weight, species_ref[...], 1, 1)[0:1]
    softplus = jnp.maximum(score, 0.0) + jnp.log1p(jnp.exp(-jnp.abs(score)))
    alive = (1 - death_ref[...].reshape(1, agents)).astype(F32)
    divide = divide_ref[...].reshape(1, agents).astype(F32)
    uptake = alive * (1.0 + divide) * softplus * sample / (0.5 + sample)
    up_high = uptake.astype(BF16).astype(F32)
    source = dot(jnp.where(in_row, up_high, 0.0).astype(BF16), one_z, 1, 1)
    t_ref[...] = (SCREENING * u - source).reshape(nx, ny, nz)
    even = is_even(me_ref[0])
    for pair in range(nx // 2):
        parts = []
        for start in (0, ny - HALO):
            for plane in (2 * pair, 2 * pair + 1):
                parts.append(u_ref[plane, start : start + HALO])
                parts.append(t_ref[plane, start : start + HALO])
        low = jnp.concatenate(parts[:4], axis=0)
        high = jnp.concatenate(parts[4:], axis=0)
        depth_a[pair] = jnp.where(even, high, low).astype(BF16)
        depth_b[pair] = jnp.where(even, low, high).astype(BF16)
    part = cell_z // PART
    values = (cell_row.astype(F32), (cell_z - part * PART).astype(F32), part.astype(F32), up_high)
    list_ref[...] = jnp.concatenate(
        [x[:, i * nz : (i + 1) * nz] for x in values for i in range(agents // nz)], axis=0
    )


def network_kernel(
    me_ref, slab_ref, species_ref, sensed_ref, death_ref, move_ref, route_ref, net_ref, sensing_ref, *outs
):
    agents, width = species_ref.shape
    depths = len(outs) - 2
    capacity = outs[0].shape[0] * 16
    species = species_ref[...]
    sensing = sensing_ref[...].reshape(1, width)
    first = sensing.astype(BF16)
    rest = sensing - first.astype(F32)
    second = rest.astype(BF16)
    third = (rest - second.astype(F32)).astype(BF16)
    line = iota((8, width), 0)
    terms = jnp.where(
        line == 0, first.astype(F32),
        jnp.where(line == 1, second.astype(F32), jnp.where(line == 2, third.astype(F32), 0.0)),
    ).astype(BF16)
    activation = dot(species, net_ref[...], 1, 0) + dot(sensed_ref[...].astype(BF16), terms, 0, 0)
    updated = (0.5 * species.astype(F32) + jnp.tanh(activation)).astype(BF16)
    lanes = 128
    lines = -(-(depths + 2) // 8) * 8
    line = iota((lines, lanes), 0)
    square = iota((lanes, 2 * lanes), 0)
    column = iota((lanes, 2 * lanes), 1)
    counter = jnp.where(jnp.logical_or(column >= lanes, square < column), 1.0, 0.0).astype(BF16)
    blocks = agents // lanes
    route = route_ref[...].reshape(1, agents)
    move = move_ref[...].reshape(1, agents)
    death = death_ref[...].reshape(1, agents)
    hits = []
    for block in range(blocks):
        cut = slice(block * lanes, (block + 1) * lanes)
        wanted = jnp.where(line < depths, route[:, cut], jnp.where(line < depths + 2, move[:, cut] + (depths - 1), -1))
        hits.append((wanted == line).astype(F32))
    counts = dot(jnp.concatenate(hits, axis=0).astype(BF16), counter, 1, 0)
    me = me_ref[0]
    to_a = jnp.where(is_even(slab_ref[0]), 1, 2)
    hop_a = jnp.where(is_even(me), 1, depths - 1)
    running = jnp.zeros((lines, lanes), F32)
    keys = []
    for block in range(blocks):
        cut = slice(block * lanes, (block + 1) * lanes)
        own = slice(block * lines, (block + 1) * lines)
        before = (counts[own, :lanes] + running) * hits[block]
        running = running + counts[own, lanes:]
        slot = jnp.sum(jnp.where(line < depths, before, 0.0), axis=0, keepdims=True).astype(jnp.int32)
        rank = jnp.sum(jnp.where(line < depths, 0.0, before), axis=0, keepdims=True).astype(jnp.int32)
        hop = route[:, cut] - me
        hop = jnp.where(hop < 0, hop + depths, hop)
        hop = jnp.where(hop == hop_a, 1, jnp.where(hop == depths - hop_a, 2, jnp.where(hop == 0, 0, hop + 1)))
        key = jnp.where(
            move[:, cut] == 0,
            hop * capacity + slot,
            depths * capacity + jnp.where(move[:, cut] == to_a, 0, MIG) + rank,
        )
        keys.append(jnp.where(death[:, cut] == 0, key, -1))
    key = jnp.concatenate(keys, axis=1)
    start = 0
    for index, out in enumerate(outs):
        size = capacity if index < depths else MIG
        chosen = (iota((size, agents), 0) == key - start).astype(BF16)
        placed = dot(chosen, updated, 1, 0).astype(BF16)
        start += size
        blocks = out.shape[0]
        for i in range(0, out.shape[2], width):
            part = placed[i // width * blocks * 16 :][: blocks * 16]
            out[:, :, i : i + width] = part.reshape(blocks, 16, width)


def tiles_of(x):
    return [x[:, i : i + LANES] for i in range(0, x.shape[1], LANES)]


def third_sum(x):
    parts = tiles_of(x)
    lane = iota((x.shape[0], LANES), 1)
    before = jnp.where(lane == 0, 0.0, pltpu.roll(parts[-1], 1, 1))
    after = jnp.where(lane == LANES - 1, 0.0, pltpu.roll(parts[0], LANES - 1, 1))
    padded = [before] + parts + [after]
    return jnp.concatenate([x + y for x, y in zip(padded[:-2], padded[2:])], axis=1)


def neighbour_total(before, plane, after):
    rows = plane.shape[0]
    second = pltpu.roll(plane, 1, 0) + pltpu.roll(plane, rows - 1, 0)
    return before + after + second + third_sum(plane)


def relaxed(before, plane, after, target, centre):
    return (1.0 - DAMPING) * plane + (DAMPING / centre) * (
        target + neighbour_total(before, plane, after)
    )


def edge_mask(me, depths, halo):
    row = iota((2 * halo, 1), 0)
    return jnp.where(
        row < halo, (me < depths - 1).astype(F32), (me > 0).astype(F32)
    )


def masked(plane, own, mask):
    return jnp.concatenate([plane[:own], plane[own:] * mask], axis=0)


def halo_rows(side_a, side_b, even, plane, mask):
    at = 2 * HALO * (plane % 2)
    side_a = side_a[at : at + 2 * HALO].astype(F32)
    side_b = side_b[at : at + 2 * HALO].astype(F32)
    high = jnp.where(even, side_a, side_b)
    low = jnp.where(even, side_b, side_a)
    return (
        jnp.concatenate([high[:HALO], low[:HALO]], axis=0) * mask,
        jnp.concatenate([high[HALO:], low[HALO:]], axis=0),
    )


def corner_kernel(me_ref, slab_ref, side_a, side_b, list_ref, slab_a, slab_b):
    layers = 2 * side_a.shape[0]
    nz = side_a.shape[2]
    even = is_even(me_ref[0])
    slab_even = is_even(slab_ref[0])

    def layer(side, plane):
        at = 2 * HALO * (plane % 2)
        return side[plane // 2].astype(F32)[at : at + 2 * HALO]

    for ref, front in ((slab_a, slab_even), (slab_b, jnp.logical_not(slab_even))):
        parts = []
        for side, high in ((side_a, even), (side_b, jnp.logical_not(even))):
            targets = []
            for i in range(1, HALO):
                x = jnp.where(front, layer(side, layers - i), layer(side, i - 1))
                parts.append(jnp.where(high, x[: HALO - i], x[i:HALO]))
                if i < HALO - 1:
                    targets.append(
                        jnp.where(high, x[HALO : 2 * HALO - 1 - i], x[HALO + 1 + i :])
                    )
            parts += targets
        parts.append(list_ref[...])
        used = sum(part.shape[0] for part in parts)
        total = ref.shape[0] * ref.shape[1]
        parts.append(jnp.zeros((total - used, nz), F32))
        ref[...] = jnp.concatenate(parts, axis=0).astype(BF16).reshape(ref.shape)


def corner_rows(block_a, block_b, even, mask):
    high = jnp.where(even, block_a, block_b)
    low = jnp.where(even, block_b, block_a)
    nz = high.shape[1]
    fields, targets = [], []
    at = 0
    for rows, out in ((HALO, fields), (HALO - 1, targets)):
        for i in range(1, rows):
            count = rows - i
            gap = jnp.zeros((2 * (HALO - count), nz), F32)
            cut = slice(at, at + count)
            out.append(jnp.concatenate([high[cut], gap, low[cut]], axis=0) * mask)
            at += count
    return fields, targets + [jnp.zeros_like(fields[0])]


KEEP, PULL = 1.0 - DAMPING, DAMPING / CENTRE


def inner_kernel(
    depths, me_ref, slab_ref, u_ref, t_ref, side_a, side_b, field_a, field_b, u0, text_ref, u1, u2_ref, inside
):
    nx, ny, nz = u_ref.shape
    even = is_even(me_ref[0])
    slab_even = is_even(slab_ref[0])
    half = ny // 16
    mask = edge_mask(me_ref[0], depths, HALO)
    for field, after in ((field_a, slab_even), (field_b, jnp.logical_not(slab_even))):
        u_at = jnp.where(after, HALO + nx, 0)
        for k in range(HALO):
            u0[u_at + k, :ny] = field[k * half : (k + 1) * half].astype(F32).reshape(ny, nz)
            u0[u_at + k, ny:] = jnp.zeros((2 * HALO, nz), F32)
    for plane in range(nx):
        u0[HALO + plane, :ny] = u_ref[plane]
        text_ref[HALO - 1 + plane, :ny] = t_ref[plane]
        uh, th = halo_rows(side_a[plane // 2], side_b[plane // 2], even, plane, mask)
        u0[HALO + plane, ny:] = uh
        text_ref[HALO - 1 + plane, ny:] = th

    def outer(i, carry):
        for p in (i, nx + HALO - 1 + i):
            u1[p] = KEEP * u0[p + 1] + PULL * neighbour_total(u0[p], u0[p + 1], u0[p + 2])
        return carry

    lax.fori_loop(0, HALO - 1, outer, 0, unroll=True)

    def first(p, carry):
        v = relaxed(u0[p], u0[p + 1], u0[p + 2], text_ref[p], CENTRE)
        u1[p] = masked(v, ny, mask)
        return carry

    lax.fori_loop(HALO - 1, nx + HALO - 1, first, 0, unroll=4)

    def second(p, carry):
        v = relaxed(u1[p], u1[p + 1], u1[p + 2], text_ref[p + 1], CENTRE)
        u2_ref[p] = masked(v, ny, mask)
        return carry

    lax.fori_loop(HALO - 1, nx + 1, second, 0, unroll=3)
    for p in range(2, nx - 2):
        inside[p - 2] = residual(u2_ref, text_ref, p, ny)


def residual(u2_ref, text_ref, p, ny):
    v = u2_ref[p + 2]
    total = neighbour_total(u2_ref[p + 1], v, u2_ref[p + 3])
    return (text_ref[p + 3] - CENTRE * v + total)[:ny]


def smooth_kernel(
    depths, agents, me_ref, slab_ref, u0, text_in, u1_in, u2_in, inside, slab_a, slab_b,
    text_ref, u1, u2_ref, coarse_ref, coarse_all_ref, coarse_a, coarse_b, paired, foreign,
):
    nx = u0.shape[0] - 2 * HALO
    ny, nz = u0.shape[1] - 2 * HALO, u0.shape[2]
    mask = edge_mask(me_ref[0], depths, HALO)
    even = is_even(me_ref[0])
    slab_even = is_even(slab_ref[0])
    near = HALO - 1
    corner = HALO * near // 2 + near * (near - 1) // 2
    row = iota((8, 1), 0)
    first, last = (row == 0).astype(F32), (row == 7).astype(F32)
    sides = ((slab_a, slab_even), (slab_b, jnp.logical_not(slab_even)))
    messages = []
    lines = agents // nz
    for side, (ref, after) in enumerate(sides):
        message = ref[...].astype(F32).reshape(-1, nz)
        messages.append(message)
        cell_row, place, part, uptake = (
            jnp.concatenate([message[at + i : at + i + 1] for i in range(lines)], axis=1)
            for at in range(2 * corner, 2 * corner + 4 * lines, lines)
        )
        cell_row = cell_row.astype(jnp.int32) - jnp.where(after, 0, (nx - near) * ny)
        wanted = jnp.logical_and(cell_row >= 0, cell_row < near * ny)
        key = jnp.where(wanted, part.astype(jnp.int32) * (near * ny) + cell_row, -1)
        one_z = (iota((PART, agents), 0) == place.astype(jnp.int32)).astype(BF16)
        key_rows = iota((near * ny * (nz // PART), agents), 0)
        taken = jnp.where(key_rows == key, uptake, 0.0).astype(BF16)
        source = dot(taken, one_z, 1, 1)
        for i in range(nz // PART):
            foreign[side, :, i * PART : (i + 1) * PART] = source[i * near * ny : (i + 1) * near * ny]
    for side, (_, after) in enumerate(sides):
        message = messages[side]
        fields, targets = corner_rows(message[:corner], message[corner : 2 * corner], even, mask)
        sign = jnp.where(after, 1, -1)
        edge = jnp.where(after, nx - 1, 0)
        for i in range(1, HALO):
            p = edge + sign * i
            index = jnp.where(after, i - 1, HALO - 1 - i)
            t = SCREENING * u0[p + 4, :ny] - foreign[side, pl.ds(index * ny, ny)]
            text_ref[p + 3, :ny] = t
            text_ref[p + 3, ny:] = targets[i - 1]
            x = fields[i - 1]
            nearer = u0[p + 4 - sign, ny:] if i == 1 else fields[i - 2]
            total = nearer + third_sum(x)
            if i < HALO - 1:
                total = total + fields[i]
            beyond = u0[p + 4]
            up = jnp.where(row == 0, beyond[ny - 1 : ny], pltpu.roll(x, 1, 0))
            down = jnp.where(row == 7, beyond[0:1], pltpu.roll(x, 7, 0))
            u1[p + 3, ny:] = (KEEP * x + PULL * (targets[i - 1] + total + up + down)) * mask
            v = u1[p + 3, :ny] + PULL * t
            u1[p + 3, :ny] = v
            u1[p + 3, 0:8] = v[0:8] + (PULL * first) * x[7:8]
            u1[p + 3, ny - 8 : ny] = v[ny - 8 :] + (PULL * last) * x[0:1]
        u1[edge + 3, ny:] = u1[edge + 3, ny:] + PULL * fields[0]
        u2_ref[edge - sign + 2, ny:] = u2_ref[edge - sign + 2, ny:] + (PULL * PULL) * fields[0]

    for p in (1, 2, nx + 1, nx + 2):
        v = relaxed(u1[p], u1[p + 1], u1[p + 2], text_ref[p + 1], CENTRE)
        u2_ref[p] = masked(v, ny, mask)
    for q in range(nx // 2):
        both = 0.0
        for p in (2 * q, 2 * q + 1):
            known = 2 <= p < nx - 2
            both = both + (inside[p - 2] if known else residual(u2_ref, text_ref, p, ny))
        parts = tiles_of(both)
        for i in range(len(parts) // 2):
            paired[q, i, :ny] = parts[2 * i] + parts[2 * i + 1]
    cx, cy, cz = coarse_ref.shape
    coarse = jnp.concatenate(
        [
            jnp.concatenate(
                [
                    paired[q, i, pl.ds(0, cy, 2), :] + paired[q, i, pl.ds(1, cy, 2), :]
                    for i in range(cz // LANES)
                ],
                axis=1,
            )
            for q in range(cx)
        ],
        axis=0,
    )
    coarse = 0.5 * coarse
    coarse_ref[...] = coarse.reshape(cx, cy, cz)
    coarse_all_ref[...] = coarse.astype(BF16).reshape(cx, cy, cz)
    low, high = (
        jnp.concatenate([coarse_ref[q, start : start + HALO] for q in range(cx)], axis=0)
        for start in (0, cy - HALO)
    )
    coarse_a[0] = jnp.where(even, high, low).astype(BF16)
    coarse_b[0] = jnp.where(even, low, high).astype(BF16)


def post_kernel(depths, me_ref, u1, u2_in, text_ref, out_ref, back_ref, v1, u2_ref):
    nx, ny, nz = out_ref.shape
    back = shuffle(nz, True)
    back_ref[...] = back
    mask = edge_mask(me_ref[0], depths, HALO)
    last = nx + 3
    for p in range(1, last):
        u2_ref[p] = u2_in[p]
    for p in (0, last):
        v = relaxed(u1[p], u1[p + 1], u1[p + 2], text_ref[p + 1], CENTRE)
        u2_ref[p] = masked(v, ny, mask)

    def first(p, carry):
        v = relaxed(u2_ref[p], u2_ref[p + 1], u2_ref[p + 2], text_ref[p + 2], CENTRE)
        v1[p] = masked(v, ny, mask)
        return carry

    lax.fori_loop(0, nx + 2, first, 0, unroll=2)

    def second(p, carry):
        v = relaxed(v1[p], v1[p + 1], v1[p + 2], text_ref[p + 3], CENTRE)
        out_ref[p] = v[:ny]
        return carry

    lax.fori_loop(0, nx, second, 0, unroll=2)
    high, low = halves(out_ref[...].reshape(nx * ny, nz))
    both = dot(jnp.concatenate([high, low], axis=0), back, 1, 0)
    out_ref[...] = (both[: nx * ny] + both[nx * ny :]).reshape(nx, ny, nz)


def correct_kernel(
    depths, me_ref, slab_ref, ct_ref, side_a, side_b, slab_a, slab_b, base_ref, back_ref, *rest
):
    packed = rest[: depths - 1]
    out_any, agents_ref, fine, out_ref, sem = rest[depths - 1 :]
    nx, ny, nz = out_ref.shape
    cx, cy, cz = ct_ref.shape
    me = me_ref[0]
    even = is_even(me)
    slab_even = is_even(slab_ref[0])
    blocks = packed[0].shape[0]
    width = agents_ref.shape[2]
    copies = []

    def place(source, start):
        target = agents_ref.at[pl.ds(start, source.shape[0])]
        copies.append(pltpu.make_async_copy(source, target, sem.at[len(copies)]))
        copies[-1].start()

    def place_wide(source, start):
        for i in range(source.shape[2] // width):
            part = source.at[:, :, pl.ds(i * width, width)]
            place(part, start + i * source.shape[0])

    up = jnp.where(me == depths - 1, 0, me + 1)
    down = jnp.where(me == 0, depths - 1, me - 1)
    place(packed[0], me * blocks)
    place_wide(side_a.at[pl.ds(1, side_a.shape[0] - 1)], jnp.where(even, up, down) * blocks)
    place(packed[1], jnp.where(even, down, up) * blocks)
    for k in range(2, depths - 1):
        origin = me - k
        place(packed[k], jnp.where(origin < 0, origin + depths, origin) * blocks)
    for ref, late in ((slab_a, slab_even), (slab_b, jnp.logical_not(slab_even))):
        start = depths * blocks + jnp.where(late, MIG // 16, 0)
        place_wide(ref.at[pl.ds(cx + 2, ref.shape[0] - cx - 2)], start)
    mask = edge_mask(me, depths, HALO)

    def chosen(condition, x, y):
        return jnp.where(condition, x.astype(F32), y.astype(F32))

    planes = []
    for p in range(cx + 2 * HALO):
        if HALO <= p < HALO + cx:
            k = p - HALO
            own, one, two = ct_ref[k], side_a[0].astype(F32), side_b[0].astype(F32)
        else:
            before = p < HALO
            k = p + cx - HALO if before else p - HALO - cx
            x, y = (slab_b, slab_a) if before else (slab_a, slab_b)
            own, one, two = (chosen(slab_even, x[i], y[i]) for i in (k, cx, cx + 1))
        rows = slice(HALO * k, HALO * (k + 1))
        one, two = one[rows], two[rows]
        sides = jnp.concatenate([jnp.where(even, one, two), jnp.where(even, two, one)], axis=0)
        planes.append(jnp.concatenate([own, sides * mask], axis=0))
    values = [(DAMPING / COARSE_CENTRE) * plane for plane in planes]
    for sweep in range(1, HALO):
        values = [
            masked(
                relaxed(values[i - 1], values[i], values[i + 1], planes[i + sweep - 1], COARSE_CENTRE),
                cy,
                mask,
            )
            for i in range(1, len(values) - 1)
        ]
    wide = cy + 4
    for q, value in enumerate(values):
        value = jnp.concatenate([value[: cy + 2], value[cy + 2 * HALO - 2 :]], axis=0)
        for i, part in enumerate(tiles_of(value)):
            fine[q, i, pl.ds(0, wide, 2), :] = part
            fine[q, i, pl.ds(1, wide, 2), :] = part
    def second_total(plane):
        rows = plane.shape[0]
        return pltpu.roll(plane, 1, 0) + pltpu.roll(plane, rows - 1, 0)

    spread = [jnp.concatenate([fine[q, i, : 2 * wide] for i in range(cz // LANES)], axis=1) for q in range(cx + 2)]
    still = [KEEP * plane + PULL * second_total(plane) for plane in spread]
    once = []
    for p in range(-1, nx + 1):
        q = (p + 2) // 2
        if p % 2 == 0:
            others = spread[q - 1] + spread[q]
        else:
            others = spread[q] + spread[q + 1]
        once.append(masked(still[q] + PULL * others, ny, mask))

    def twice(plane):
        return jnp.concatenate([part for part in tiles_of(plane) for _ in range(2)], axis=1)

    back = back_ref[...]
    bounds = (0, nx // 2, nx // 4 * 3, nx)
    for start, end in zip(bounds, bounds[1:]):
        planes = []
        for p in range(start, end):
            plane = once[p + 1]
            total = once[p] + once[p + 2] + second_total(plane)
            none = (KEEP * plane + PULL * total)[:ny]
            one = (2.0 * PULL) * plane[:ny]
            two = (PULL * PULL) * spread[(p + 2) // 2][:ny]
            planes.append(twice(none) + third_sum(twice(one) + third_sum(twice(two))))
        done = dot(jnp.concatenate(planes, axis=0).astype(BF16), back, 1, 0)
        out_ref[start:end] = base_ref[start:end] + done.reshape(end - start, ny, nz)
        for p in range(start, end):
            copies.append(pltpu.make_async_copy(out_ref.at[p], out_any.at[p], sem.at[len(copies)]))
            copies[-1].start()
    for copy in copies:
        copy.wait()


def local(
    nutrient, species, agent_cell, death_flag, divide_flag, slab_move, depth_route, net_weight, sensing, uptake_weight
):
    depths = lax.axis_size("depth")
    nx, ny, nz = nutrient.shape
    agents, width = species.shape
    capacity = 2 * agents // depths
    me = lax.axis_index("depth").astype(jnp.int32).reshape(1)
    slab = lax.axis_index("slab").astype(jnp.int32).reshape(1)
    shape = jax.ShapeDtypeStruct
    cells, death, divide = (x.reshape(1, agents) for x in (agent_cell, death_flag, divide_flag))
    move, route = slab_move.reshape(1, agents), depth_route.reshape(1, agents)
    half = ny // 16
    if agents % nz or nx * ny > PART or nz % PART or depths < 4:
        raise ValueError("list digits")
    arguments = (
        cells, nutrient, divide, uptake_weight.reshape(1, width), species, death,
        move, route, net_weight, sensing.reshape(1, width),
    )
    (
        nutrient, places, field_a, field_b, cells, divide, weight, species, death, move, route, net_weight, sensing
    ) = pl.pallas_call(
        load_kernel,
        out_shape=(
            shape((nx, ny, nz), F32),
            shape((nz, agents), BF16),
            shape((HALO * half, 16, nz), BF16),
            shape((HALO * half, 16, nz), BF16),
        )
        + tuple(shape(x.shape, x.dtype) for i, x in enumerate(arguments) if i != 1),
        in_specs=[SMEM_SPEC] + [HBM_SPEC] * len(arguments),
        out_specs=[VMEM_SPEC] * (4 + len(arguments) - 1),
        scratch_shapes=[
            pltpu.VMEM((nx, ny, nz), F32),
            pltpu.SemaphoreType.DMA((len(arguments),)),
        ],
        compiler_params=PARAMS,
        name="load",
    )(slab, *(pltpu.with_memory_space_constraint(x, pltpu.HBM) for x in arguments))
    target, sensed, depth_a, depth_b, agent_list = pl.pallas_call(
        uptake_kernel,
        out_shape=(
            shape((nx, ny, nz), F32),
            shape((8, agents), F32),
            shape((nx // 2, 16, nz), BF16),
            shape((nx // 2, 16, nz), BF16),
            shape((4 * agents // nz, nz), F32),
        ),
        in_specs=[SMEM_SPEC] + [VMEM_SPEC] * 7,
        out_specs=[VMEM_SPEC] * 5,
        compiler_params=PARAMS,
        cost_estimate=pl.CostEstimate(flops=1 << 31, bytes_accessed=1 << 20, transcendentals=0),
        name="uptake",
    )(me, nutrient, places, cells, divide, weight, species, death)
    field_a, field_b, depth_a, depth_b = lax.optimization_barrier((field_a, field_b, depth_a, depth_b))
    side_a = swapped(depth_a, "depth", "a")
    side_b = swapped(depth_b, "depth", "b")
    field_a = swapped(field_a, "slab", "a")
    field_b = swapped(field_b, "slab", "b")
    rows = 2 * (HALO - 1) ** 2 + agent_list.shape[0]
    rows = -(-rows // 16) * 16
    slab_a, slab_b = pl.pallas_call(
        corner_kernel,
        out_shape=tuple(shape((rows // 16, 16, nz), BF16) for _ in range(2)),
        in_specs=[SMEM_SPEC] * 2 + [VMEM_SPEC] * 3,
        out_specs=[VMEM_SPEC] * 2,
        compiler_params=PARAMS,
        name="corner",
    )(me, slab, side_a, side_b, agent_list)
    slab_a = swapped(slab_a, "slab", "a")
    slab_b = swapped(slab_b, "slab", "b")
    cx, cy, cz = nx // 2, ny // 2, nz // 2
    ext = ny + 2 * HALO
    sent = pl.pallas_call(
        network_kernel,
        out_shape=tuple(
            shape((capacity // 32, 16, 2 * width) if k == 1 else (capacity // 16, 16, width), BF16)
            for k in range(depths)
        )
        + tuple(shape((MIG * width // (16 * cz), 16, cz), BF16) for _ in range(2)),
        in_specs=[SMEM_SPEC] * 2 + [VMEM_SPEC] * 7,
        out_specs=[VMEM_SPEC] * (depths + 2),
        compiler_params=PARAMS,
        cost_estimate=pl.CostEstimate(flops=1 << 31, bytes_accessed=1<<20, transcendentals=0),
        name="network",
    )(me, slab, species, sensed, death, move, route, net_weight, sensing)
    u0, text, u1, u2, inside = pl.pallas_call(
        functools.partial(inner_kernel, depths),
        out_shape=(
            shape((nx + 2 * HALO, ext, nz), F32),
            shape((nx + 2 * HALO - 2, ext, nz), F32),
            shape((nx + 2 * HALO - 2, ext, nz), F32),
            shape((nx + 4, ext, nz), F32),
            shape((nx - 4, ny, nz), F32),
        ),
        in_specs=[SMEM_SPEC] * 2 + [VMEM_SPEC] * 6,
        out_specs=[VMEM_SPEC] * 5,
        compiler_params=PARAMS,
        cost_estimate=pl.CostEstimate(flops=1 << 20, bytes_accessed=1<<20, transcendentals=0),
        name="inner",
    )(me, slab, nutrient, target, side_a, side_b, field_a, field_b)
    slab_a, slab_b, inside, *sent = lax.optimization_barrier((slab_a, slab_b, inside, *sent))
    text, u1, u2, ct, ct_all, coarse_a, coarse_b = pl.pallas_call(
        functools.partial(smooth_kernel, depths, agents),
        out_shape=(
            shape(text.shape, F32),
            shape(u1.shape, F32),
            shape(u2.shape, F32),
            shape((cx, cy, cz), F32),
            shape((cx, cy, cz), BF16),
            shape((1, cx * HALO, cz), BF16),
            shape((1, cx * HALO, cz), BF16),
        ),
        in_specs=[SMEM_SPEC] * 2 + [VMEM_SPEC] * 7,
        out_specs=[VMEM_SPEC] * 7,
        scratch_shapes=[
            pltpu.VMEM((cx, cz // LANES, ny + 8, LANES), F32),
            pltpu.VMEM((2, (HALO - 1) * ny, nz), F32),
        ],
        input_output_aliases={3: 0, 4: 1, 5: 2},
        compiler_params=PARAMS,
        name="smooth",
    )(me, slab, u0, text, u1, u2, inside, slab_a, slab_b)
    coarse_a = swapped(jnp.concatenate([coarse_a, sent[1]], axis=0), "depth", "a")
    coarse_b = swapped(coarse_b, "depth", "b")
    arrived = [sent[0], swapped(sent[2], "depth", "b")]
    arrived += [cyclic(sent[k + 1], "depth", k) for k in range(2, depths - 1)]
    tail_a, tail_b = (
        swapped(jnp.concatenate([ct_all, coarse_a[:1], coarse_b, movers], axis=0), "slab", which)
        for which, movers in (("a", sent[depths]), ("b", sent[depths + 1]))
    )
    base, back = pl.pallas_call(
        functools.partial(post_kernel, depths),
        out_shape=(shape((nx, ny, nz), F32), shape((nz, nz), BF16)),
        in_specs=[SMEM_SPEC] + [VMEM_SPEC] * 3,
        out_specs=[VMEM_SPEC] * 2,
        scratch_shapes=[pltpu.VMEM((nx + 2, ext, nz), F32), pltpu.VMEM((nx + 4, ext, nz), F32)],
        compiler_params=PARAMS,
        cost_estimate=pl.CostEstimate(flops=1 << 30, bytes_accessed=1 << 22, transcendentals=0),
        name="post",
    )(me, u1, u2, text)
    grid_field, agents_out = pl.pallas_call(
        functools.partial(correct_kernel, depths),
        out_shape=(
            shape((nx, ny, nz), F32),
            shape(((depths * capacity + 2 * MIG) // 16, 16, width), BF16),
        ),
        in_specs=[SMEM_SPEC] * 2 + [VMEM_SPEC] * 7 + [ANY_SPEC] * (depths - 1),
        out_specs=[HBM_SPEC, ANY_SPEC],
        scratch_shapes=[
            pltpu.VMEM((cx + 2, cz // LANES, ext + 8, LANES), F32),
            pltpu.VMEM((nx, ny, nz), F32),
            pltpu.SemaphoreType.DMA((depths + 5 + nx,)),
        ],
        compiler_params=PARAMS,
        name="correct",
    )(me, slab, ct, coarse_a, coarse_b, tail_a, tail_b, base, back, *arrived)
    return grid_field, agents_out.reshape(-1, width)


def solution(mesh):
    rows = P(("slab", "depth"))
    in_specs = (
        P("slab", "depth", None),
        P(("slab", "depth"), None),
        rows,
        rows,
        rows,
        rows,
        P(("slab", "depth"), None),
        P(),
        P(),
        P(),
    )
    out_specs = (P("slab", "depth", None), P(("slab", "depth"), None))
    return jax.shard_map(local, mesh=mesh, in_specs=in_specs, out_specs=out_specs, check_vma=False)
```
